512 devices in a mesh: span: 16 (over x, y), plane: 32 (over z, core).
Axes of the slice: x: 4, y: 4, z: 16, core: 2. Of those that a mesh axis runs over, the one named last changes fastest.
Arguments:
- forcing: float32 [5, 256, 65536], P(None, 'span', 'plane'), may hold values from -2 to 2
- inv_diag: bfloat16 [5, 5, 256, 65536], P(None, None, 'span', 'plane')
- upper_jac: bfloat16 [5, 5, 256, 65536], P(None, None, 'span', 'plane')
- face_cell: int32 [131072], P(('span', 'plane')), may hold values from 0 to 32767
- face_owner: int32 [131072, 1], P(('span', 'plane')), may hold values from 0 to 31; in each aligned block of 256 rows (0 to 255, 256 to 511, ...) at most 16 rows name the same one
- face_slot: int32 [131072], P(('span', 'plane')), may hold values from 0 to 127
- face_count: int32 [512], P(('span', 'plane')), may hold values from 1 to 256, 98304 in all
- aileron: int32 [131072], P(('span', 'plane')), may hold values 0 or 1
- face_map: float32 [3, 5, 131072], P(None, None, ('span', 'plane')), may hold values from -6 to 6
- hinge_arm: float32 [131072], P(('span', 'plane')), may hold values from 0.3 to 3
Outputs:
- adjoint: float32 [5, 256, 65536], P(None, 'span', 'plane')
- shell_load: float32 [3, 65536], P(None, ('span', 'plane'))
- hinge: float32 [5], replicated
The draws below stay inside these ranges and needn't reach their ends.
Inputs may be any that keep to these rules, and one draw needn't show every extreme that they name: `face_cell`: a local index into the device's own block of 16 planes of 2048 cells. `face_owner`: among the 256 face slots of one device at most 16 name one owner, a bound that some block reaches. The first face_count slots of a device are live; some device has all 256 live.
All inputs are finite; a program needn't handle non-finite values. No bound on the sum of `aileron` on one device may be relied on, other than what follows from the above.
Results may differ from the reference program's by a relative error of at most 0.0003.
Values sent between devices are 32-bit elements; how exact they have to be, the bound alone decides.
A program may use at most 64 MiB of HBM per device.

```python
import math
import jax
import jax.numpy as jnp
import numpy as np
from jax import lax

FIELDS = 5
LOADS = 3
SK = 16
PC = 2048
FACES_DEV = 256
SHELL_DEV = 128
WINGWISE_SLICES = 256
PCELLS = 65536
FACES = 131072
SHELLS = 65536
CAP = 16
N_SPAN = 16
N_PLANE = 32


def draw_inv_diag(key, part):
    key = jax.random.fold_in(key, 11)
    first, second = jax.random.split(key)
    spread = 0.05
    offdiag = jax.random.uniform(first, (FIELDS, FIELDS, WINGWISE_SLICES, PCELLS), jnp.float32, -spread, spread)
    diagonal = jax.random.uniform(second, (FIELDS, WINGWISE_SLICES, PCELLS), jnp.float32, 0.97, 1.0)
    unit = jnp.eye(FIELDS, dtype=jnp.float32)[:, :, None, None]
    sweep_result = offdiag * (1.0 - unit) + unit * diagonal[None, :, :, :]
    return sweep_result.astype(jnp.bfloat16)


def draw_upper_jac(key, part):
    key = jax.random.fold_in(key, 23)
    first, second, third, quartic_component, fifth = jax.random.split(key, 5)
    share = 0.5
    slow_flag = jax.random.bernoulli(first, share, (FIELDS, 1, PCELLS))
    slow_rate = jax.random.uniform(second, (FIELDS, WINGWISE_SLICES, PCELLS), jnp.float32, 0.99, 0.998)
    fast_rate = jax.random.uniform(third, (FIELDS, WINGWISE_SLICES, PCELLS), jnp.float32, 0.85, 0.93)
    falloff_speed = jnp.where(slow_flag, slow_rate, fast_rate)
    spike_location = jax.random.randint(quartic_component, (3,), 0, WINGWISE_SLICES)
    tier_indices = jnp.arange(WINGWISE_SLICES, dtype=jnp.int32)
    spike_indicator = jnp.any(tier_indices[:, None] == spike_location[None, :], axis=1)
    falloff_speed = falloff_speed * jnp.where(spike_indicator, 0.6, 1.0)[None, :, None]
    offdiag = jax.random.uniform(fifth, (FIELDS, FIELDS, WINGWISE_SLICES, PCELLS), jnp.float32, -0.03, 0.03) * falloff_speed[:, None, :, :]
    unit = jnp.eye(FIELDS, dtype=jnp.float32)[:, :, None, None]
    sweep_result = offdiag * (1.0 - unit) - unit * falloff_speed[:, None, :, :]
    return sweep_result.astype(jnp.bfloat16)


def place_ends(values, stream_key, least, largest):
    extent = values.shape
    index_at = [jax.random.randint(jax.random.fold_in(stream_key, axis), (), 0, extent[axis]) for axis in range(len(extent))]
    values = values.at[tuple(index_at)].set(least)
    longest = extent.index(max(extent))
    index_at[longest] = (index_at[longest] + 1) % extent[longest]
    return values.at[tuple(index_at)].set(largest)


def block_levels(own_key, shape, cuts, smallest, largest):
    gain, own = 1.0, jax.random.fold_in(own_key, 6)
    for axis_at, blocks in cuts:
        draws = jnp.exp(jax.random.uniform(jax.random.fold_in(own, axis_at), (blocks,), jnp.float32, smallest / len(cuts), largest / len(cuts)))
        gain = gain * jnp.repeat(draws, shape[axis_at] // blocks).reshape([-1 if axis == axis_at else 1 for axis in range(len(shape))])
    return gain


def profile(amount, total, reach, lean):
    portions = [(1 << 20) // math.isqrt(grade ** lean) + 1 for grade in range(2, amount + 1)]
    rest, given = total - reach - (amount - 1), [1] * (amount - 1)
    while rest > 0:
        movable = [i for i in range(amount - 1) if given[i] < reach]
        mass, left = sum([portions[i] for i in movable]), rest
        for i in movable:
            extra = min(reach - given[i], max(1, left * portions[i] // mass), rest)
            given[i] = given[i] + extra
            rest = rest - extra
    return np.array([reach] + given)


def ragged_sizes(own_key, amount, total, limit, skew):
    if amount == 2:
        one = jax.random.randint(own_key, (), max(1, total - limit), min(limit, total - 1) + 1)
        return jnp.stack([one, total - one])
    sizes = jnp.asarray(profile(amount, total, limit, skew), jnp.int32)
    twos = (amount - 1) // 2
    donor, sink = sizes[1:1 + 2 * twos:2], sizes[2:2 + 2 * twos:2]
    margin = jnp.minimum(donor - 1, limit - sink)
    shifted = jax.random.randint(jax.random.fold_in(own_key, 1), (twos,), 0, 1 << 20) % (margin + 1)
    sizes = sizes.at[1:1 + 2 * twos:2].set(donor - shifted).at[2:2 + 2 * twos:2].set(sink + shifted)
    return sizes[jax.random.permutation(jax.random.fold_in(own_key, 2), amount)]


def assign_block(stream_key, own, number, rows, number_of, top, reach, lean):
    sequence = jax.random.permutation(stream_key, number_of)
    crowded, ordinary = shares(number_of, rows * top, reach, lean, True), shares(number_of, rows * top, reach, lean, False)
    places = jnp.arange(number_of)

    def named(sizes, rotation):
        used = int((sizes > 0).sum())
        fixed = max(1, used // 4)
        moved = fixed + (places - fixed + rotation * (used - fixed)) % max(1, number_of - fixed)
        return jnp.zeros((number_of,), jnp.int32).at[sequence[jnp.where(places < fixed, places, moved)]].set(jnp.asarray(sizes, jnp.int32))

    sizes = jnp.where(number % 4 == 0, named(crowded, number // 4), named(ordinary, number - number // 4 - 1))
    mixed = jax.random.permutation(jax.random.fold_in(own, 3), number_of)
    giver, receiver = mixed[0:number_of // 2 * 2:2], mixed[1:number_of // 2 * 2:2]
    margin = jnp.minimum(sizes[giver] - 1, reach - sizes[receiver]) // 2
    margin = jnp.where((giver == sequence[0]) | (receiver == sequence[0]) | (sizes[receiver] == 0), 0, jnp.maximum(margin, 0))
    moved = jax.random.randint(jax.random.fold_in(own, 4), (number_of // 2,), 0, 1 << 20) % (margin + 1)
    sizes = sizes.at[giver].add(-moved).at[receiver].add(moved)
    items = jnp.searchsorted(jnp.cumsum(sizes), jnp.arange(rows * top), side="right").astype(jnp.int32)
    listing = items.reshape(top, rows).T
    listing = listing[jax.random.permutation(jax.random.fold_in(own, 1), rows)]
    rotation = jax.random.randint(jax.random.fold_in(own, 2), (rows, 1), 0, top)
    return jnp.take_along_axis(listing, (jnp.arange(top)[None, :] + rotation) % top, axis=1)


def shares(amount, total, most, skew, full):
    portions = [(1 << 20) // math.isqrt(standing ** skew) + 1 for standing in range(1, amount + 1)]
    largest = most if full else min(most, max(-(-total // amount), total * portions[0] // sum(portions)))
    least = 1 if total - largest >= amount - 1 else 0
    given, surplus = [largest] + [least] * (amount - 1), total - largest - least * (amount - 1)
    while surplus > 0:
        free = [i for i in range(1, amount) if given[i] < largest] or [i for i in range(1, amount) if given[i] < most]
        pool, left = sum([portions[i] for i in free]), surplus
        for i in free:
            extra = min(most - given[i], max(1, left * portions[i] // pool), surplus)
            given[i] = given[i] + extra
            surplus = surplus - extra
    return np.array(given)


def gaussian(rng, shape, scale, bound, shards=(), held_as=jnp.bfloat16):
    gain = block_levels(rng, shape, shards, -0.22, 0.18) if shards else 1.0
    values = jax.random.normal(rng, shape, jnp.float32) * scale * gain
    return jnp.minimum(jnp.maximum(values, -bound), bound).astype(held_as)


def setup_inputs(seed: int = 0) -> dict:
    arg_keys = jax.random.split(jax.random.key(seed), 11)
    forcing = gaussian(arg_keys[0], (FIELDS, WINGWISE_SLICES, PCELLS), 0.15, 2.0, ((1, 16), (2, 32)), jnp.float32)
    inv_diag = draw_inv_diag(jax.random.fold_in(arg_keys[10], 71), 0)
    upper_jac = draw_upper_jac(jax.random.fold_in(arg_keys[10], 71), 0)
    face_cell = place_ends(jax.random.randint(arg_keys[3], (FACES,), 0, SK * PC), jax.random.fold_in(arg_keys[3], 1), 0, (SK * PC) - 1).astype(jnp.int32)
    face_owner_keys = jax.random.split(jax.random.fold_in(arg_keys[4], 1), FACES // FACES_DEV)
    face_owner_turns = jax.random.permutation(jax.random.fold_in(arg_keys[4], 3), FACES // FACES_DEV)
    face_owner = jax.vmap(lambda own, number: assign_block(jax.random.fold_in(arg_keys[4], 2), own, number, FACES_DEV, N_PLANE, 1, CAP, 2))(face_owner_keys, face_owner_turns).reshape((FACES, 1))
    face_slot = place_ends(jax.random.randint(arg_keys[5], (FACES,), 0, SHELL_DEV), jax.random.fold_in(arg_keys[5], 1), 0, SHELL_DEV - 1).astype(jnp.int32)
    face_count = ragged_sizes(arg_keys[6], N_SPAN * N_PLANE, N_SPAN * N_PLANE * FACES_DEV * 3 // 4, FACES_DEV, 2).astype(jnp.int32)
    aileron = place_ends((jax.random.randint(arg_keys[7], (FACES,), 0, 4) < 1).astype(jnp.int32), jax.random.fold_in(arg_keys[7], 1), 0, 1)
    face_map = gaussian(arg_keys[8], (LOADS, FIELDS, FACES), 0.5, 6.0, ((2, 512),), jnp.float32)
    hinge_arm = jnp.clip(jnp.exp(math.log(3.0) - 2.3025851 * jax.random.uniform(arg_keys[9], (FACES,), jnp.float32) ** block_levels(arg_keys[9], (FACES,), ((0, 512),), -0.2, 0.2)), 0.3, 3.0)
    return dict(forcing=forcing, inv_diag=inv_diag, upper_jac=upper_jac, face_cell=face_cell, face_owner=face_owner, face_slot=face_slot, face_count=face_count, aileron=aileron, face_map=face_map, hinge_arm=hinge_arm)


def plane_terms(inv_block, upper_block, rhs_plane):
    inv_t = jnp.swapaxes(inv_block, 0, 1)
    upper_t = jnp.swapaxes(upper_block, 0, 1)
    coupling = -lax.optimization_barrier(jnp.sum(inv_t[:, :, None, :] * upper_t[None, :, :, :], axis=1))
    source = lax.optimization_barrier(jnp.sum(inv_t * rhs_plane[None, :, :], axis=1))
    return (coupling, source)

def apply_block(matrix, vector):
    return lax.optimization_barrier(jnp.sum(matrix * vector[None, :, :], axis=1))

def reference(forcing, inv_diag, upper_jac, face_cell, face_owner, face_slot, face_count, aileron, face_map, hinge_arm):

    def sweep_plane(above, level):
        inv_block = lax.dynamic_index_in_dim(inv_diag, level, 2, keepdims=False).astype(jnp.float32)
        upper_block = lax.dynamic_index_in_dim(upper_jac, level, 2, keepdims=False).astype(jnp.float32)
        rhs_plane = lax.dynamic_index_in_dim(forcing, level, 1, keepdims=False)
        coupling, source = plane_terms(inv_block, upper_block, rhs_plane)
        present_state = apply_block(coupling, above) + source
        return (present_state, present_state)
    start = jnp.zeros((FIELDS, PCELLS), jnp.float32)
    levels = jnp.arange(WINGWISE_SLICES, dtype=jnp.int32)
    _, stacked = lax.scan(sweep_plane, start, levels, reverse=True)
    adjoint = jnp.moveaxis(stacked, 0, 1)
    face_ids = jnp.arange(FACES, dtype=jnp.int32)
    device_id = face_ids // FACES_DEV
    span_idx = device_id // N_PLANE
    plane_idx = device_id % N_PLANE
    level_idx = span_idx * SK + face_cell // PC
    cell_idx = plane_idx * PC + face_cell % PC
    face_rows = adjoint[:, level_idx, cell_idx]
    is_live = (face_ids % FACES_DEV < face_count[device_id]).astype(jnp.float32)
    face_load = lax.optimization_barrier(jnp.sum(face_map * face_rows[None, :, :], axis=1)) * is_live[None, :]
    target = (span_idx * N_PLANE + face_owner[:, 0]) * SHELL_DEV + face_slot
    shell_load = jnp.zeros((LOADS, SHELLS), jnp.float32).at[:, target].add(face_load)
    weight = aileron.astype(jnp.float32) * is_live * hinge_arm
    hinge = lax.optimization_barrier(jnp.sum(face_rows * weight[None, :], axis=1)) / math.sqrt(FACES)
    return (adjoint, shell_load, hinge)
```

```python
import math

import jax
import jax.numpy as jnp
from jax import lax
from jax.experimental import pallas as pl
from jax.experimental.pallas import tpu as pltpu
from jax.sharding import PartitionSpec as P

MESH = pl.DeviceIdType.MESH

FIELDS = 5
LOADS = 3
NS = 16
NP = 32
PLANES = 16
CELLS = 2048
LANES = 128
CHUNKS = CELLS // LANES
HALF = CHUNKS // 2
FACES = 256
SHELL = 128
CAP = 16
COMPS = FIELDS * (FIELDS + 1)
MAP_ROWS = 32
ROWS = CHUNKS * PLANES
GROUPS = 4
GROUP_CELLS = CELLS // GROUPS
GROUP_CHUNKS = CHUNKS // GROUPS
HINGE_AT = 0
LOAD_AT = 16
SLOT_AT = 64


def chunk_of(dev):
    x, y = dev // 4, dev % 4
    return HALF * ((x + y) % 2) + 2 * x + y // 2


def device_of(half, j):
    x = j // 2
    return 4 * x + 2 * (j % 2) + (half + x) % 2


def split(value):
    high = value.astype(jnp.bfloat16)
    low = (value - high.astype(jnp.float32)).astype(jnp.bfloat16)
    return high, low


def kernel(
    forcing,
    inv_diag,
    upper,
    cell,
    owner,
    slot,
    count,
    aileron,
    fmap,
    arm,
    adj_out,
    shell_out,
    hinge_out,
    f_v,
    d_v,
    u_v,
    cell_v,
    owner_v,
    slot_v,
    ail_v,
    fmap_v,
    arm_v,
    terms,
    maps,
    maps_in,
    inc_out,
    inc_in,
    adj,
    hot,
    msg,
    msg_in,
    hmsg,
    hmsg_in,
    load_sem,
    small_sem,
    out_sem,
    map_ssem,
    map_rsem,
    inc_ssem,
    inc_rsem,
    face_ssem,
    face_rsem,
    hinge_ssem,
    hinge_rsem,
):
    me = lax.axis_index("span")
    q = lax.axis_index("plane")
    barrier = pltpu.get_barrier_semaphore()

    def load_copies(g):
        cells = pl.ds(g * GROUP_CELLS, GROUP_CELLS)
        return (
            pltpu.make_async_copy(
                inv_diag.at[:, :, :, cells], d_v.at[:, :, :, cells], load_sem.at[g, 0]
            ),
            pltpu.make_async_copy(
                upper.at[:, :, :, cells], u_v.at[:, :, :, cells], load_sem.at[g, 1]
            ),
            pltpu.make_async_copy(
                forcing.at[:, :, cells], f_v.at[:, :, cells], load_sem.at[g, 2]
            ),
        )

    for g in range(GROUPS):
        for copy in load_copies(g):
            copy.start()
    small = [
        pltpu.make_async_copy(src, dst, small_sem.at[n])
        for n, (src, dst) in enumerate(
            (
                (cell, cell_v),
                (owner, owner_v),
                (slot, slot_v),
                (aileron, ail_v),
                (fmap, fmap_v),
                (arm, arm_v),
            )
        )
    ]
    for copy in small:
        copy.start()

    def greet_span(r, carry):
        pl.semaphore_signal(
            barrier, inc=1, device_id=((me + r) % NS, q), device_id_type=MESH
        )
        return carry

    def greet_plane(r, carry):
        pl.semaphore_signal(
            barrier, inc=1, device_id=(me, (q + r) % NP), device_id_type=MESH
        )
        return carry

    lax.fori_loop(1, NS, greet_span, 0)
    lax.fori_loop(1, NP, greet_plane, 0)
    inc_out[...] = jnp.zeros_like(inc_out)

    def chunk_terms(c, carry):
        cells = pl.ds(pl.multiple_of(c * LANES, LANES), LANES)
        rows = pl.ds(pl.multiple_of(c * PLANES, PLANES), PLANES)
        up = [
            [u_v[j, m, :, cells].astype(jnp.float32) for m in range(FIELDS)]
            for j in range(FIELDS)
        ]
        rhs = [f_v[m, :, cells] for m in range(FIELDS)]
        for i in range(FIELDS):
            inv = [d_v[m, i, :, cells].astype(jnp.float32) for m in range(FIELDS)]
            for j in range(FIELDS):
                total = inv[0] * up[j][0]
                for m in range(1, FIELDS):
                    total = total + inv[m] * up[j][m]
                terms[i * FIELDS + j, rows, :] = -total
            total = inv[0] * rhs[0]
            for m in range(1, FIELDS):
                total = total + inv[m] * rhs[m]
            terms[FIELDS * FIELDS + i, rows, :] = total
        return carry

    def term(n, half, k):
        return terms[n, pl.ds(half * HALF * PLANES + k, HALF, stride=PLANES), :]

    def matvec(coupling, vec, start=None):
        out = []
        for i in range(FIELDS):
            total = coupling[i * FIELDS] * vec[0]
            for j in range(1, FIELDS):
                total = total + coupling[i * FIELDS + j] * vec[j]
            out.append(total if start is None else total + start[i])
        return out

    def section_map(half):
        state = tuple(term(n, half, PLANES - 1) for n in range(COMPS))

        def compose(step, state):
            k = PLANES - 2 - step
            coupling = [term(n, half, k) for n in range(FIELDS * FIELDS)]
            source = [term(FIELDS * FIELDS + i, half, k) for i in range(FIELDS)]
            new = [None] * COMPS
            for col in range(FIELDS):
                column = matvec(coupling, [state[j * FIELDS + col] for j in range(FIELDS)])
                for i in range(FIELDS):
                    new[i * FIELDS + col] = column[i]
            new[FIELDS * FIELDS :] = matvec(coupling, state[FIELDS * FIELDS :], source)
            return tuple(new)

        state = lax.fori_loop(0, PLANES - 1, compose, state)
        for n in range(COMPS):
            maps[pl.ds(half * HALF * MAP_ROWS + n, HALF, stride=MAP_ROWS), :] = state[n]

    def map_rows(c):
        return pl.ds(pl.multiple_of(c * MAP_ROWS, MAP_ROWS), MAP_ROWS)

    def map_copy(c, dest, source):
        return pltpu.make_async_remote_copy(
            src_ref=maps.at[map_rows(c), :],
            dst_ref=maps_in.at[map_rows(source), :],
            send_sem=map_ssem.at[dest],
            recv_sem=map_rsem.at[source],
            device_id=(dest, q),
            device_id_type=MESH,
        )

    for n in range(COMPS, MAP_ROWS):
        maps[pl.ds(n, CHUNKS, stride=MAP_ROWS), :] = jnp.zeros((CHUNKS, LANES), jnp.float32)

    my_chunk = chunk_of(me)
    my_j = my_chunk % HALF
    for half in range(2):
        for g in range(half * GROUPS // 2, (half + 1) * GROUPS // 2):
            for copy in load_copies(g):
                copy.wait()
            lax.fori_loop(g * GROUP_CHUNKS, (g + 1) * GROUP_CHUNKS, chunk_terms, 0)
        section_map(half)
        if half == 0:
            pl.semaphore_wait(barrier, NS - 1 + NP - 1)

        def send_map(t, carry):
            j = (my_j + t) % HALF
            dest = device_of(half, j)

            @pl.when(dest != me)
            def _():
                map_copy(half * HALF + j, dest, me).start()

            return carry

        lax.fori_loop(0, HALF, send_map, 0)

    for copy in small:
        copy.wait()
    face_cell = cell_v[...].reshape(1, FACES)
    face_plane = face_cell // CELLS
    face_at = face_cell % CELLS
    for c in range(CHUNKS):
        at = lax.broadcasted_iota(jnp.int32, (LANES, FACES), 0) + c * LANES
        hot[pl.ds(c * LANES, LANES), :] = jnp.where(at == face_at, 1.0, 0.0).astype(jnp.bfloat16)
    plane_hit = lax.broadcasted_iota(jnp.int32, (PLANES, FACES), 0) == face_plane
    face_id = lax.broadcasted_iota(jnp.int32, (1, FACES), 1)
    live = jnp.where(face_id < count[0], 1.0, 0.0)
    owner_hot = jnp.where(
        lax.broadcasted_iota(jnp.int32, (NP, FACES), 0) == owner_v[...], 1.0, 0.0
    )
    owner_hot16 = owner_hot.astype(jnp.bfloat16)
    earlier = jnp.where(
        lax.broadcasted_iota(jnp.int32, (FACES, FACES), 0)
        < lax.broadcasted_iota(jnp.int32, (FACES, FACES), 1),
        1.0,
        0.0,
    ).astype(jnp.bfloat16)
    before = jnp.dot(owner_hot16, earlier, preferred_element_type=jnp.float32)
    rank = jnp.sum(owner_hot * before, axis=0, keepdims=True).astype(jnp.int32)
    rank_hot = jnp.where(lax.broadcasted_iota(jnp.int32, (CAP, FACES), 0) == rank, 1.0, 0.0)
    slot_value = (slot_v[...].reshape(1, FACES) + 1).astype(jnp.float32) * live
    slot_rows = rank_hot * slot_value
    weight = ail_v[...].reshape(1, FACES).astype(jnp.float32) * live * arm_v[...].reshape(1, FACES)

    maps_in[map_rows(me), :] = maps[map_rows(my_chunk), :]
    vec = [jnp.zeros((1, LANES), jnp.float32) for _ in range(FIELDS)]
    for section in range(NS - 1, 0, -1):

        @pl.when(me != section)
        def _():
            map_copy(0, section, section).wait_recv()

        def entry(n):
            return maps_in[pl.ds(section * MAP_ROWS + n, 1), :]

        matrix = [entry(n) for n in range(FIELDS * FIELDS)]
        vec = matvec(matrix, vec, [entry(FIELDS * FIELDS + i) for i in range(FIELDS)])
        for i in range(FIELDS):
            inc_out[pl.ds((section - 1) * 8 + i, 1), :] = vec[i]

    @pl.when(me != 0)
    def _():
        map_copy(0, 0, 0).wait_recv()

    def inc_copy(dest, c, source):
        return pltpu.make_async_remote_copy(
            src_ref=inc_out.at[pl.ds(pl.multiple_of(dest * 8, 8), 8), :],
            dst_ref=inc_in.at[pl.ds(pl.multiple_of(c * 8, 8), 8), :],
            send_sem=inc_ssem.at[dest],
            recv_sem=inc_rsem.at[source],
            device_id=(dest, q),
            device_id_type=MESH,
        )

    def send_inc(r, carry):
        inc_copy((me + r) % NS, my_chunk, me).start()
        return carry

    lax.fori_loop(1, NS, send_inc, 0)
    inc_in[pl.ds(pl.multiple_of(my_chunk * 8, 8), 8), :] = inc_out[
        pl.ds(pl.multiple_of(me * 8, 8), 8), :
    ]

    gathered = jnp.zeros((2 * FIELDS * PLANES, FACES), jnp.float32)
    outputs = []
    for half in range(2):
        for j in range(HALF):
            dev = device_of(half, j)

            @pl.when(me != dev)
            def _():
                inc_copy(dev, half * HALF + j, dev).wait_recv()

        state = tuple(
            inc_in[pl.ds(half * HALF * 8 + i, HALF, stride=8), :] for i in range(FIELDS)
        )

        def sweep(step, state):
            k = PLANES - 1 - step
            coupling = [term(n, half, k) for n in range(FIELDS * FIELDS)]
            source = [term(FIELDS * FIELDS + i, half, k) for i in range(FIELDS)]
            state = matvec(coupling, state, source)
            for i in range(FIELDS):
                adj[i, pl.ds(half * HALF * PLANES + k, HALF, stride=PLANES), :] = state[i]
            return tuple(state)

        lax.fori_loop(0, PLANES, sweep, state)
        for c in range(half * HALF, (half + 1) * HALF):
            copy = pltpu.make_async_copy(
                adj.at[:, pl.ds(c * PLANES, PLANES), :],
                adj_out.at[:, :, pl.ds(c * LANES, LANES)],
                out_sem.at[c],
            )
            copy.start()
            outputs.append(copy)
        for c in range(half * HALF, (half + 1) * HALF, 2):
            pair = jnp.concatenate(
                [
                    adj[:, pl.ds(e * PLANES, PLANES), :].reshape(FIELDS * PLANES, LANES)
                    for e in (c, c + 1)
                ],
                axis=1,
            )
            gathered = gathered + jnp.dot(
                jnp.concatenate(split(pair), axis=0),
                hot[pl.ds(c * LANES, 2 * LANES), :],
                preferred_element_type=jnp.float32,
            )

    both = gathered[: FIELDS * PLANES] + gathered[FIELDS * PLANES :]
    rows = [
        jnp.sum(
            jnp.where(plane_hit, both[i * PLANES : (i + 1) * PLANES], 0.0), axis=0, keepdims=True
        )
        for i in range(FIELDS)
    ]
    load_rows = []
    for a in range(LOADS):
        total = fmap_v[0, pl.ds(a, 1), :] * rows[0]
        for i in range(1, FIELDS):
            total = total + fmap_v[i, pl.ds(a, 1), :] * rows[i]
        load_rows.append(rank_hot * (total * live))
    hinge_rows = jnp.concatenate(
        [rows[i] * weight for i in range(FIELDS)]
        + [jnp.zeros((LANES - FIELDS, FACES), jnp.float32)],
        axis=0,
    )
    face_rows = jnp.concatenate(
        [jnp.zeros((LOAD_AT, FACES), jnp.float32)]
        + load_rows
        + [slot_rows, jnp.zeros((LANES - SLOT_AT - CAP, FACES), jnp.float32)],
        axis=0,
    )

    def by_face(left, right):
        return lax.dot_general(
            left, right, (((1,), (1,)), ((), ())), preferred_element_type=jnp.float32
        )

    every = jnp.ones((NP, FACES), jnp.bfloat16)
    packed = jnp.zeros((NP, LANES), jnp.float32)
    for piece in split(face_rows):
        packed = packed + by_face(owner_hot16, piece)
    for piece in split(hinge_rows):
        packed = packed + by_face(every, piece)
    msg[:, 0, :] = packed

    def face_copy(dest, source):
        return pltpu.make_async_remote_copy(
            src_ref=msg.at[dest],
            dst_ref=msg_in.at[source],
            send_sem=face_ssem.at[dest],
            recv_sem=face_rsem.at[source],
            device_id=(me, dest),
            device_id_type=MESH,
        )

    def send_face(r, carry):
        face_copy((q + r) % NP, q).start()
        return carry

    lax.fori_loop(1, NP, send_face, 0)
    msg_in[q] = msg[q]

    def wait_face(r, carry):
        peer = (q + r) % NP
        face_copy(peer, peer).wait_recv()
        return carry

    lax.fori_loop(1, NP, wait_face, 0)
    arrived = msg_in[:, 0, :]

    hmsg[0] = jnp.sum(arrived, axis=0, keepdims=True)

    def hinge_copy(dest, source):
        return pltpu.make_async_remote_copy(
            src_ref=hmsg.at[0],
            dst_ref=hmsg_in.at[source],
            send_sem=hinge_ssem.at[dest],
            recv_sem=hinge_rsem.at[source],
            device_id=(dest, q),
            device_id_type=MESH,
        )

    def send_hinge(r, carry):
        hinge_copy((me + r) % NS, me).start()
        return carry

    lax.fori_loop(1, NS, send_hinge, 0)
    hmsg_in[me] = hmsg[0]

    lane = lax.broadcasted_iota(jnp.int32, (NP, LANES), 1) + 1
    loads = [jnp.zeros((NP, SHELL), jnp.float32) for _ in range(LOADS)]
    for pos in range(CAP):
        at = SLOT_AT + pos
        hit = arrived[:, at : at + 1].astype(jnp.int32) == lane
        for a in range(LOADS):
            at = LOAD_AT + a * CAP + pos
            loads[a] = loads[a] + jnp.where(hit, arrived[:, at : at + 1], 0.0)
    for a in range(LOADS):
        shell_out[pl.ds(a, 1), :] = jnp.sum(loads[a], axis=0, keepdims=True)

    for copy in outputs:
        copy.wait()

    def sent(r, carry):
        peer = (me + r) % NS
        map_copy(0, peer, peer).wait_send()
        inc_copy(peer, 0, peer).wait_send()
        return carry

    lax.fori_loop(1, NS, sent, 0)

    def sent_face(r, carry):
        peer = (q + r) % NP
        face_copy(peer, peer).wait_send()
        return carry

    lax.fori_loop(1, NP, sent_face, 0)

    def wait_hinge(r, carry):
        peer = (me + r) % NS
        hinge_copy(peer, peer).wait_send()
        hinge_copy(peer, peer).wait_recv()
        return carry

    lax.fori_loop(1, NS, wait_hinge, 0)
    total = jnp.sum(hmsg_in[:, 0, :], axis=0) * (1.0 / math.sqrt(NS * NP * FACES))
    hinge_out[...] = total[:FIELDS]


def on_device(
    forcing,
    inv_diag,
    upper_jac,
    face_cell,
    face_owner,
    face_slot,
    face_count,
    aileron,
    face_map,
    hinge_arm,
):
    anywhere = pl.BlockSpec(memory_space=pl.ANY)
    vmem = pl.BlockSpec(memory_space=pltpu.VMEM)
    f32, bf16, i32 = jnp.float32, jnp.bfloat16, jnp.int32
    dma = pltpu.SemaphoreType.DMA
    return pl.pallas_call(
        kernel,
        out_shape=(
            jax.ShapeDtypeStruct((FIELDS, PLANES, CELLS), f32),
            jax.ShapeDtypeStruct((LOADS, SHELL), f32),
            jax.ShapeDtypeStruct((FIELDS,), f32),
        ),
        in_specs=[anywhere] * 6
        + [pl.BlockSpec(memory_space=pltpu.SMEM)]
        + [anywhere] * 3,
        out_specs=(anywhere, vmem, vmem),
        scratch_shapes=[
            pltpu.VMEM((FIELDS, PLANES, CELLS), f32),
            pltpu.VMEM((FIELDS, FIELDS, PLANES, CELLS), bf16),
            pltpu.VMEM((FIELDS, FIELDS, PLANES, CELLS), bf16),
            pltpu.VMEM((FACES,), i32),
            pltpu.VMEM((1, FACES), i32),
            pltpu.VMEM((FACES,), i32),
            pltpu.VMEM((FACES,), i32),
            pltpu.VMEM((FIELDS, LOADS, FACES), f32),
            pltpu.VMEM((FACES,), f32),
            pltpu.VMEM((COMPS, ROWS, LANES), f32),
            pltpu.VMEM((CHUNKS * MAP_ROWS, LANES), f32),
            pltpu.VMEM((NS * MAP_ROWS, LANES), f32),
            pltpu.VMEM((NS * 8, LANES), f32),
            pltpu.VMEM((CHUNKS * 8, LANES), f32),
            pltpu.VMEM((FIELDS, ROWS, LANES), f32),
            pltpu.VMEM((CELLS, FACES), bf16),
            pltpu.VMEM((NP, 1, LANES), f32),
            pltpu.VMEM((NP, 1, LANES), f32),
            pltpu.VMEM((1, 1, LANES), f32),
            pltpu.VMEM((NS, 1, LANES), f32),
            dma((GROUPS, 3)),
            dma((6,)),
            dma((CHUNKS,)),
            dma((NS,)),
            dma((NS,)),
            dma((NS,)),
            dma((NS,)),
            dma((NP,)),
            dma((NP,)),
            dma((NS,)),
            dma((NS,)),
        ],
        compiler_params=pltpu.CompilerParams(
            collective_id=0, has_side_effects=True, vmem_limit_bytes=48 * 1024 * 1024
        ),
        cost_estimate=pl.CostEstimate(
            flops=22_000_000, bytes_accessed=4_700_000, transcendentals=0
        ),
        name="sweep",
    )(
        forcing,
        inv_diag,
        upper_jac,
        face_cell,
        face_owner.T,
        face_slot,
        face_count,
        aileron,
        jnp.swapaxes(face_map, 0, 1),
        hinge_arm,
    )


def solution(mesh):
    in_specs = (
        P(None, "span", "plane"),
        P(None, None, "span", "plane"),
        P(None, None, "span", "plane"),
        P(("span", "plane")),
        P(("span", "plane"), None),
        P(("span", "plane")),
        P(("span", "plane")),
        P(("span", "plane")),
        P(None, None, ("span", "plane")),
        P(("span", "plane")),
    )
    out_specs = (P(None, "span", "plane"), P(None, ("span", "plane")), P())
    return jax.shard_map(
        on_device, mesh=mesh, in_specs=in_specs, out_specs=out_specs, check_vma=False
    )
```

```python
import math

import jax
import jax.numpy as jnp
from jax import lax
from jax.experimental import pallas as pl
from jax.experimental.pallas import tpu as pltpu
from jax.sharding import PartitionSpec as P

MESH = pl.DeviceIdType.MESH

FIELDS = 5
LOADS = 3
NS = 16
NP = 32
PLANES = 16
CELLS = 2048
LANES = 128
CHUNKS = CELLS // LANES
HALF = CHUNKS // 2
FACES = 256
SHELL = 128
CAP = 16
COMPS = FIELDS * (FIELDS + 1)
MAP_ROWS = 32
MAP_PITCH = 40
TERM_PITCH = 17
ADJ_PITCH = 24
GROUPS = 4
GROUP_CELLS = CELLS // GROUPS
GROUP_CHUNKS = CHUNKS // GROUPS
HINGE_AT = 0
LOAD_AT = 16
SLOT_AT = 64


def chunk_of(dev):
    x, y = dev // 4, dev % 4
    return HALF * ((x + y) % 2) + 2 * x + y // 2


def device_of(half, j):
    x = j // 2
    return 4 * x + 2 * (j % 2) + (half + x) % 2


def split(value):
    high = value.astype(jnp.bfloat16)
    low = (value - high.astype(jnp.float32)).astype(jnp.bfloat16)
    return high, low


def kernel(
    forcing,
    inv_diag,
    upper,
    cell,
    owner,
    slot,
    count,
    aileron,
    fmap,
    arm,
    adj_out,
    shell_out,
    hinge_out,
    f_v,
    d_v,
    u_v,
    cell_v,
    owner_v,
    slot_v,
    count_s,
    ail_v,
    fmap_v,
    arm_v,
    terms,
    maps,
    maps_in,
    inc_out,
    inc_in,
    adj,
    hot,
    msg,
    msg_in,
    rows_in,
    hmsg,
    hmsg_in,
    load_sem,
    small_sem,
    out_sem,
    map_ssem,
    map_rsem,
    inc_ssem,
    inc_rsem,
    face_ssem,
    face_rsem,
    hinge_ssem,
    hinge_rsem,
):
    me = lax.axis_index("span")
    q = lax.axis_index("plane")
    barrier = pltpu.get_barrier_semaphore()

    def load_copies(g):
        cells = pl.ds(g * GROUP_CELLS, GROUP_CELLS)
        return (
            pltpu.make_async_copy(
                inv_diag.at[:, :, :, cells], d_v.at[:, :, :, cells], load_sem.at[g, 0]
            ),
            pltpu.make_async_copy(
                upper.at[:, :, :, cells], u_v.at[:, :, :, cells], load_sem.at[g, 1]
            ),
            pltpu.make_async_copy(
                forcing.at[:, :, cells], f_v.at[:, :, cells], load_sem.at[g, 2]
            ),
        )

    for g in range(GROUPS):
        for copy in load_copies(g):
            copy.start()
    small = [
        pltpu.make_async_copy(src, dst, small_sem.at[n])
        for n, (src, dst) in enumerate(
            (
                (cell, cell_v),
                (owner, owner_v),
                (slot, slot_v),
                (count, count_s),
                (aileron, ail_v),
                (fmap, fmap_v),
                (arm, arm_v),
            )
        )
    ]
    for copy in small:
        copy.start()

    def greet_span(r, carry):
        pl.semaphore_signal(
            barrier, inc=1, device_id=((me + r) % NS, q), device_id_type=MESH
        )
        return carry

    def greet_plane(r, carry):
        pl.semaphore_signal(
            barrier, inc=1, device_id=(me, (q + r) % NP), device_id_type=MESH
        )
        return carry

    lax.fori_loop(1, NS, greet_span, 0)
    lax.fori_loop(1, NP, greet_plane, 0)
    inc_out[...] = jnp.zeros_like(inc_out)

    def chunk_terms(c, carry):
        cells = pl.ds(pl.multiple_of(c * LANES, LANES), LANES)
        rows = pl.ds(c * TERM_PITCH, PLANES)
        up = [
            [u_v[j, m, :, cells].astype(jnp.float32) for m in range(FIELDS)]
            for j in range(FIELDS)
        ]
        rhs = [f_v[m, :, cells] for m in range(FIELDS)]
        for i in range(FIELDS):
            inv = [d_v[m, i, :, cells].astype(jnp.float32) for m in range(FIELDS)]
            for j in range(FIELDS):
                total = inv[0] * up[j][0]
                for m in range(1, FIELDS):
                    total = total + inv[m] * up[j][m]
                terms[i * FIELDS + j, rows, :] = -total
            total = inv[0] * rhs[0]
            for m in range(1, FIELDS):
                total = total + inv[m] * rhs[m]
            terms[FIELDS * FIELDS + i, rows, :] = total
        return carry

    def term(n, half, k):
        return terms[n, pl.ds(half * HALF * TERM_PITCH + k, HALF, stride=TERM_PITCH), :]

    def matvec(coupling, vec, start=None):
        out = []
        for i in range(FIELDS):
            total = coupling[i * FIELDS] * vec[0]
            for j in range(1, FIELDS):
                total = total + coupling[i * FIELDS + j] * vec[j]
            out.append(total if start is None else total + start[i])
        return out

    def section_map(half):
        state = tuple(term(n, half, PLANES - 1) for n in range(COMPS))

        def compose(step, state):
            k = PLANES - 2 - step
            coupling = [term(n, half, k) for n in range(FIELDS * FIELDS)]
            source = [term(FIELDS * FIELDS + i, half, k) for i in range(FIELDS)]
            new = [None] * COMPS
            for col in range(FIELDS):
                column = matvec(coupling, [state[j * FIELDS + col] for j in range(FIELDS)])
                for i in range(FIELDS):
                    new[i * FIELDS + col] = column[i]
            new[FIELDS * FIELDS :] = matvec(coupling, state[FIELDS * FIELDS :], source)
            return tuple(new)

        state = lax.fori_loop(0, PLANES - 1, compose, state)
        for n in range(COMPS):
            maps[pl.ds(half * HALF * MAP_PITCH + n, HALF, stride=MAP_PITCH), :] = state[n]

    def out_rows(c):
        return pl.ds(pl.multiple_of(c * MAP_PITCH, 8), MAP_ROWS)

    def map_rows(c):
        return pl.ds(pl.multiple_of(c * MAP_ROWS, MAP_ROWS), MAP_ROWS)

    def map_copy(c, dest, source):
        return pltpu.make_async_remote_copy(
            src_ref=maps.at[out_rows(c), :],
            dst_ref=maps_in.at[map_rows(source), :],
            send_sem=map_ssem.at[dest],
            recv_sem=map_rsem.at[source],
            device_id=(dest, q),
            device_id_type=MESH,
        )

    for n in range(COMPS, MAP_ROWS):
        maps[pl.ds(n, CHUNKS, stride=MAP_PITCH), :] = jnp.zeros((CHUNKS, LANES), jnp.float32)

    my_chunk = chunk_of(me)
    my_j = my_chunk % HALF
    for half in range(2):
        for g in range(half * GROUPS // 2, (half + 1) * GROUPS // 2):
            for copy in load_copies(g):
                copy.wait()
            lax.fori_loop(g * GROUP_CHUNKS, (g + 1) * GROUP_CHUNKS, chunk_terms, 0)
        section_map(half)
        if half == 0:
            pl.semaphore_wait(barrier, NS - 1 + NP - 1)

        def send_map(t, carry):
            j = (my_j + t) % HALF
            dest = device_of(half, j)

            @pl.when(dest != me)
            def _():
                map_copy(half * HALF + j, dest, me).start()

            return carry

        lax.fori_loop(0, HALF, send_map, 0)

    for copy in small:
        copy.wait()
    face_cell = cell_v[...].reshape(1, FACES)
    face_plane = face_cell // CELLS
    face_at = face_cell % CELLS
    for c in range(CHUNKS):
        at = lax.broadcasted_iota(jnp.int32, (LANES, FACES), 0) + c * LANES
        hot[pl.ds(c * LANES, LANES), :] = jnp.where(at == face_at, 1.0, 0.0).astype(jnp.bfloat16)
    plane_hit = lax.broadcasted_iota(jnp.int32, (PLANES, FACES), 0) == face_plane
    face_id = lax.broadcasted_iota(jnp.int32, (1, FACES), 1)
    live = jnp.where(face_id < count_s[0], 1.0, 0.0)
    owner_hot = jnp.where(
        lax.broadcasted_iota(jnp.int32, (NP, FACES), 0) == owner_v[...], 1.0, 0.0
    )
    owner_hot16 = owner_hot.astype(jnp.bfloat16)
    earlier = jnp.where(
        lax.broadcasted_iota(jnp.int32, (FACES, FACES), 0)
        < lax.broadcasted_iota(jnp.int32, (FACES, FACES), 1),
        1.0,
        0.0,
    ).astype(jnp.bfloat16)
    before = jnp.dot(owner_hot16, earlier, preferred_element_type=jnp.float32)
    rank = jnp.sum(owner_hot * before, axis=0, keepdims=True).astype(jnp.int32)
    rank_hot = jnp.where(lax.broadcasted_iota(jnp.int32, (CAP, FACES), 0) == rank, 1.0, 0.0)
    slot_value = (slot_v[...].reshape(1, FACES) + 1).astype(jnp.float32) * live
    slot_rows = rank_hot * slot_value
    weight = ail_v[...].reshape(1, FACES).astype(jnp.float32) * live * arm_v[...].reshape(1, FACES)

    maps_in[map_rows(me), :] = maps[out_rows(my_chunk), :]
    vec = [jnp.zeros((1, LANES), jnp.float32) for _ in range(FIELDS)]
    for section in range(NS - 1, 0, -1):

        @pl.when(me != section)
        def _():
            map_copy(0, section, section).wait_recv()

        def entry(n):
            return maps_in[pl.ds(section * MAP_ROWS + n, 1), :]

        matrix = [entry(n) for n in range(FIELDS * FIELDS)]
        vec = matvec(matrix, vec, [entry(FIELDS * FIELDS + i) for i in range(FIELDS)])
        for i in range(FIELDS):
            inc_out[pl.ds((section - 1) * 8 + i, 1), :] = vec[i]

    @pl.when(me != 0)
    def _():
        map_copy(0, 0, 0).wait_recv()

    def inc_copy(dest, c, source):
        return pltpu.make_async_remote_copy(
            src_ref=inc_out.at[pl.ds(pl.multiple_of(dest * 8, 8), 8), :],
            dst_ref=inc_in.at[pl.ds(pl.multiple_of(c * 8, 8), 8), :],
            send_sem=inc_ssem.at[dest],
            recv_sem=inc_rsem.at[source],
            device_id=(dest, q),
            device_id_type=MESH,
        )

    def send_inc(r, carry):
        inc_copy((me + r) % NS, my_chunk, me).start()
        return carry

    lax.fori_loop(1, NS, send_inc, 0)
    inc_in[pl.ds(pl.multiple_of(my_chunk * 8, 8), 8), :] = inc_out[
        pl.ds(pl.multiple_of(me * 8, 8), 8), :
    ]

    for half in range(2):
        for j in range(HALF):
            dev = device_of(half, j)

            @pl.when(me != dev)
            def _():
                inc_copy(dev, half * HALF + j, dev).wait_recv()

    start = tuple(
        tuple(inc_in[pl.ds(half * HALF * 8 + i, HALF, stride=8), :] for i in range(FIELDS))
        for half in range(2)
    )

    def sweep(step, states):
        k = PLANES - 1 - step
        new = []
        for half in range(2):
            coupling = [term(n, half, k) for n in range(FIELDS * FIELDS)]
            source = [term(FIELDS * FIELDS + i, half, k) for i in range(FIELDS)]
            state = matvec(coupling, states[half], source)
            for i in range(FIELDS):
                adj[i, pl.ds(half * HALF * ADJ_PITCH + k, HALF, stride=ADJ_PITCH), :] = state[i]
            new.append(tuple(state))
        return tuple(new)

    lax.fori_loop(0, PLANES, sweep, start)
    outputs = []
    for c in range(CHUNKS):
        copy = pltpu.make_async_copy(
            adj.at[:, pl.ds(c * ADJ_PITCH, PLANES), :],
            adj_out.at[:, :, pl.ds(c * LANES, LANES)],
            out_sem.at[c],
        )
        copy.start()
        outputs.append(copy)
    gathered = jnp.zeros((2 * FIELDS * PLANES, FACES), jnp.float32)
    for c in range(0, CHUNKS, 2):
        pair = jnp.concatenate(
            [
                adj[:, pl.ds(e * ADJ_PITCH, PLANES), :].reshape(FIELDS * PLANES, LANES)
                for e in (c, c + 1)
            ],
            axis=1,
        )
        gathered = gathered + jnp.dot(
            jnp.concatenate(split(pair), axis=0),
            hot[pl.ds(c * LANES, 2 * LANES), :],
            preferred_element_type=jnp.float32,
        )

    both = gathered[: FIELDS * PLANES] + gathered[FIELDS * PLANES :]
    rows = [
        jnp.sum(
            jnp.where(plane_hit, both[i * PLANES : (i + 1) * PLANES], 0.0), axis=0, keepdims=True
        )
        for i in range(FIELDS)
    ]
    load_rows = []
    for a in range(LOADS):
        total = fmap_v[0, pl.ds(a, 1), :] * rows[0]
        for i in range(1, FIELDS):
            total = total + fmap_v[i, pl.ds(a, 1), :] * rows[i]
        load_rows.append(rank_hot * (total * live))
    hinge_rows = jnp.concatenate(
        [rows[i] * weight for i in range(FIELDS)]
        + [jnp.zeros((LANES - FIELDS, FACES), jnp.float32)],
        axis=0,
    )
    face_rows = jnp.concatenate(
        [jnp.zeros((LOAD_AT, FACES), jnp.float32)]
        + load_rows
        + [slot_rows, jnp.zeros((LANES - SLOT_AT - CAP, FACES), jnp.float32)],
        axis=0,
    )

    def by_face(left, right):
        return lax.dot_general(
            left, right, (((1,), (1,)), ((), ())), preferred_element_type=jnp.float32
        )

    every = jnp.ones((NP, FACES), jnp.bfloat16)
    packed = jnp.zeros((NP, LANES), jnp.float32)
    for piece in split(face_rows):
        packed = packed + by_face(owner_hot16, piece)
    for piece in split(hinge_rows):
        packed = packed + by_face(every, piece)
    msg[:, 0, :] = packed

    def face_copy(dest, source):
        return pltpu.make_async_remote_copy(
            src_ref=msg.at[dest],
            dst_ref=msg_in.at[source],
            send_sem=face_ssem.at[dest],
            recv_sem=face_rsem.at[source],
            device_id=(me, dest),
            device_id_type=MESH,
        )

    def send_face(r, carry):
        face_copy((q + r) % NP, q).start()
        return carry

    lax.fori_loop(1, NP, send_face, 0)
    msg_in[q] = msg[q]

    def wait_face(r, carry):
        peer = (q + r) % NP
        face_copy(peer, peer).wait_recv()
        return carry

    lax.fori_loop(1, NP, wait_face, 0)
    for peer in range(NP):
        rows_in[pl.ds(peer, 1), :] = msg_in[peer]
    arrived = rows_in[...]

    hmsg[0] = jnp.sum(arrived, axis=0, keepdims=True)

    def hinge_copy(dest, source):
        return pltpu.make_async_remote_copy(
            src_ref=hmsg.at[0],
            dst_ref=hmsg_in.at[source],
            send_sem=hinge_ssem.at[dest],
            recv_sem=hinge_rsem.at[source],
            device_id=(dest, q),
            device_id_type=MESH,
        )

    def send_hinge(r, carry):
        hinge_copy((me + r) % NS, me).start()
        return carry

    lax.fori_loop(1, NS, send_hinge, 0)
    hmsg_in[me] = hmsg[0]

    lane = lax.broadcasted_iota(jnp.int32, (NP, LANES), 1) + 1
    loads = [jnp.zeros((NP, SHELL), jnp.float32) for _ in range(LOADS)]
    for pos in range(CAP):
        at = SLOT_AT + pos
        hit = arrived[:, at : at + 1].astype(jnp.int32) == lane
        for a in range(LOADS):
            at = LOAD_AT + a * CAP + pos
            loads[a] = loads[a] + jnp.where(hit, arrived[:, at : at + 1], 0.0)
    for a in range(LOADS):
        shell_out[pl.ds(a, 1), :] = jnp.sum(loads[a], axis=0, keepdims=True)

    for copy in outputs:
        copy.wait()

    def sent(r, carry):
        peer = (me + r) % NS
        map_copy(0, peer, peer).wait_send()
        inc_copy(peer, 0, peer).wait_send()
        return carry

    lax.fori_loop(1, NS, sent, 0)

    def sent_face(r, carry):
        peer = (q + r) % NP
        face_copy(peer, peer).wait_send()
        return carry

    lax.fori_loop(1, NP, sent_face, 0)

    def wait_hinge(r, carry):
        peer = (me + r) % NS
        hinge_copy(peer, peer).wait_send()
        hinge_copy(peer, peer).wait_recv()
        return carry

    lax.fori_loop(1, NS, wait_hinge, 0)
    total = jnp.sum(hmsg_in[:, 0, :], axis=0) * (1.0 / math.sqrt(NS * NP * FACES))
    hinge_out[...] = total[:FIELDS]


def on_device(
    forcing,
    inv_diag,
    upper_jac,
    face_cell,
    face_owner,
    face_slot,
    face_count,
    aileron,
    face_map,
    hinge_arm,
):
    anywhere = pl.BlockSpec(memory_space=pltpu.HBM)
    vmem = pl.BlockSpec(memory_space=pltpu.VMEM)
    f32, bf16, i32 = jnp.float32, jnp.bfloat16, jnp.int32
    dma = pltpu.SemaphoreType.DMA
    return pl.pallas_call(
        kernel,
        out_shape=(
            jax.ShapeDtypeStruct((FIELDS, PLANES, CELLS), f32),
            jax.ShapeDtypeStruct((LOADS, SHELL), f32),
            jax.ShapeDtypeStruct((FIELDS,), f32),
        ),
        in_specs=[anywhere] * 10,
        out_specs=(anywhere, vmem, vmem),
        scratch_shapes=[
            pltpu.VMEM((FIELDS, PLANES, CELLS), f32),
            pltpu.VMEM((FIELDS, FIELDS, PLANES, CELLS), bf16),
            pltpu.VMEM((FIELDS, FIELDS, PLANES, CELLS), bf16),
            pltpu.VMEM((FACES,), i32),
            pltpu.VMEM((1, FACES), i32),
            pltpu.VMEM((FACES,), i32),
            pltpu.SMEM((1,), i32),
            pltpu.VMEM((FACES,), i32),
            pltpu.VMEM((FIELDS, LOADS, FACES), f32),
            pltpu.VMEM((FACES,), f32),
            pltpu.VMEM((COMPS, CHUNKS * TERM_PITCH, LANES), f32),
            pltpu.VMEM((CHUNKS * MAP_PITCH, LANES), f32),
            pltpu.VMEM((NS * MAP_ROWS, LANES), f32),
            pltpu.VMEM((NS * 8, LANES), f32),
            pltpu.VMEM((CHUNKS * 8, LANES), f32),
            pltpu.VMEM((FIELDS, CHUNKS * ADJ_PITCH, LANES), f32),
            pltpu.VMEM((CELLS, FACES), bf16),
            pltpu.VMEM((NP, 1, LANES), f32),
            pltpu.VMEM((NP, 1, LANES), f32),
            pltpu.VMEM((NP, LANES), f32),
            pltpu.VMEM((1, 1, LANES), f32),
            pltpu.VMEM((NS, 1, LANES), f32),
            dma((GROUPS, 3)),
            dma((7,)),
            dma((CHUNKS,)),
            dma((NS,)),
            dma((NS,)),
            dma((NS,)),
            dma((NS,)),
            dma((NP,)),
            dma((NP,)),
            dma((NS,)),
            dma((NS,)),
        ],
        compiler_params=pltpu.CompilerParams(
            collective_id=0, has_side_effects=True, vmem_limit_bytes=63 * 1024 * 1024
        ),
        cost_estimate=pl.CostEstimate(
            flops=22_000_000, bytes_accessed=4_700_000, transcendentals=0
        ),
        name="sweep",
    )(
        forcing,
        inv_diag,
        upper_jac,
        face_cell,
        face_owner.T,
        face_slot,
        face_count,
        aileron,
        jnp.swapaxes(face_map, 0, 1),
        hinge_arm,
    )


def solution(mesh):
    in_specs = (
        P(None, "span", "plane"),
        P(None, None, "span", "plane"),
        P(None, None, "span", "plane"),
        P(("span", "plane")),
        P(("span", "plane"), None),
        P(("span", "plane")),
        P(("span", "plane")),
        P(("span", "plane")),
        P(None, None, ("span", "plane")),
        P(("span", "plane")),
    )
    out_specs = (P(None, "span", "plane"), P(None, ("span", "plane")), P())
    return jax.shard_map(
        on_device, mesh=mesh, in_specs=in_specs, out_specs=out_specs, check_vma=False
    )
```

```python
import math

import jax
import jax.numpy as jnp
from jax import lax
from jax.experimental import pallas as pl
from jax.experimental.pallas import tpu as pltpu
from jax.sharding import PartitionSpec as P

MESH = pl.DeviceIdType.MESH

FIELDS = 5
LOADS = 3
NS = 16
NP = 32
PLANES = 16
CELLS = 2048
LANES = 128
CHUNKS = CELLS // LANES
HALF = CHUNKS // 2
FACES = 256
SHELL = 128
CAP = 16
COMPS = FIELDS * (FIELDS + 1)
MAP_ROWS = 32
MAP_PITCH = 40
TERM_PITCH = 17
ADJ_PITCH = 24
GROUPS = 4
GROUP_CELLS = CELLS // GROUPS
GROUP_CHUNKS = CHUNKS // GROUPS
HINGE_AT = 0
LOAD_AT = 16
SLOT_AT = 64


def chunk_of(dev):
    x, y = dev // 4, dev % 4
    return HALF * ((x + y) % 2) + 2 * x + y // 2


def device_of(half, j):
    x = j // 2
    return 4 * x + 2 * (j % 2) + (half + x) % 2


def split(value):
    high = value.astype(jnp.bfloat16)
    low = (value - high.astype(jnp.float32)).astype(jnp.bfloat16)
    return high, low


def kernel(
    forcing,
    inv_diag,
    upper,
    cell,
    owner,
    slot,
    count,
    aileron,
    fmap,
    arm,
    adj,
    shell_out,
    hinge_out,
    f_v,
    d_v,
    u_v,
    cell_v,
    owner_v,
    slot_v,
    ail_v,
    fmap_v,
    arm_v,
    terms,
    maps,
    maps_in,
    inc_out,
    inc_in,
    hot,
    msg,
    msg_in,
    rows_in,
    hmsg,
    hmsg_in,
    load_sem,
    small_sem,
    map_ssem,
    map_rsem,
    inc_ssem,
    inc_rsem,
    face_ssem,
    face_rsem,
    hinge_ssem,
    hinge_rsem,
):
    me = lax.axis_index("span")
    q = lax.axis_index("plane")
    barrier = pltpu.get_barrier_semaphore()

    def load_copies(g):
        cells = pl.ds(g * GROUP_CELLS, GROUP_CELLS)
        return (
            pltpu.make_async_copy(
                inv_diag.at[:, :, :, cells], d_v.at[:, :, :, cells], load_sem.at[g, 0]
            ),
            pltpu.make_async_copy(
                upper.at[:, :, :, cells], u_v.at[:, :, :, cells], load_sem.at[g, 1]
            ),
            pltpu.make_async_copy(
                forcing.at[:, :, cells], f_v.at[:, :, cells], load_sem.at[g, 2]
            ),
        )

    for g in range(GROUPS):
        for copy in load_copies(g):
            copy.start()
    small = [
        pltpu.make_async_copy(src, dst, small_sem.at[n])
        for n, (src, dst) in enumerate(
            (
                (cell, cell_v),
                (owner, owner_v),
                (slot, slot_v),
                (aileron, ail_v),
                (fmap, fmap_v),
                (arm, arm_v),
            )
        )
    ]
    for copy in small:
        copy.start()

    def greet_span(r, carry):
        pl.semaphore_signal(
            barrier, inc=1, device_id=((me + r) % NS, q), device_id_type=MESH
        )
        return carry

    def greet_plane(r, carry):
        pl.semaphore_signal(
            barrier, inc=1, device_id=(me, (q + r) % NP), device_id_type=MESH
        )
        return carry

    lax.fori_loop(1, NS, greet_span, 0)
    lax.fori_loop(1, NP, greet_plane, 0)
    inc_out[...] = jnp.zeros_like(inc_out)

    def chunk_terms(c, carry):
        cells = pl.ds(pl.multiple_of(c * LANES, LANES), LANES)
        rows = pl.ds(c * TERM_PITCH, PLANES)
        up = [
            [u_v[j, m, :, cells].astype(jnp.float32) for m in range(FIELDS)]
            for j in range(FIELDS)
        ]
        rhs = [f_v[m, :, cells] for m in range(FIELDS)]
        for i in range(FIELDS):
            inv = [d_v[m, i, :, cells].astype(jnp.float32) for m in range(FIELDS)]
            for j in range(FIELDS):
                total = inv[0] * up[j][0]
                for m in range(1, FIELDS):
                    total = total + inv[m] * up[j][m]
                terms[i * FIELDS + j, rows, :] = -total
            total = inv[0] * rhs[0]
            for m in range(1, FIELDS):
                total = total + inv[m] * rhs[m]
            terms[FIELDS * FIELDS + i, rows, :] = total
        return carry

    def term(n, half, k):
        return terms[n, pl.ds(half * HALF * TERM_PITCH + k, HALF, stride=TERM_PITCH), :]

    def matvec(coupling, vec, start=None):
        out = []
        for i in range(FIELDS):
            total = coupling[i * FIELDS] * vec[0]
            for j in range(1, FIELDS):
                total = total + coupling[i * FIELDS + j] * vec[j]
            out.append(total if start is None else total + start[i])
        return out

    def section_map(half):
        state = tuple(term(n, half, PLANES - 1) for n in range(COMPS))

        def compose(step, state):
            k = PLANES - 2 - step
            coupling = [term(n, half, k) for n in range(FIELDS * FIELDS)]
            source = [term(FIELDS * FIELDS + i, half, k) for i in range(FIELDS)]
            new = [None] * COMPS
            for col in range(FIELDS):
                column = matvec(coupling, [state[j * FIELDS + col] for j in range(FIELDS)])
                for i in range(FIELDS):
                    new[i * FIELDS + col] = column[i]
            new[FIELDS * FIELDS :] = matvec(coupling, state[FIELDS * FIELDS :], source)
            return tuple(new)

        state = lax.fori_loop(0, PLANES - 1, compose, state)
        for n in range(COMPS):
            maps[pl.ds(half * HALF * MAP_PITCH + n, HALF, stride=MAP_PITCH), :] = state[n]

    def out_rows(c):
        return pl.ds(pl.multiple_of(c * MAP_PITCH, 8), MAP_ROWS)

    def map_rows(c):
        return pl.ds(pl.multiple_of(c * MAP_ROWS, MAP_ROWS), MAP_ROWS)

    def map_copy(c, dest, source):
        return pltpu.make_async_remote_copy(
            src_ref=maps.at[out_rows(c), :],
            dst_ref=maps_in.at[map_rows(source), :],
            send_sem=map_ssem.at[dest],
            recv_sem=map_rsem.at[source],
            device_id=(dest, q),
            device_id_type=MESH,
        )

    for n in range(COMPS, MAP_ROWS):
        maps[pl.ds(n, CHUNKS, stride=MAP_PITCH), :] = jnp.zeros((CHUNKS, LANES), jnp.float32)

    my_chunk = chunk_of(me)
    my_j = my_chunk % HALF
    for half in range(2):
        for g in range(half * GROUPS // 2, (half + 1) * GROUPS // 2):
            for copy in load_copies(g):
                copy.wait()
            lax.fori_loop(g * GROUP_CHUNKS, (g + 1) * GROUP_CHUNKS, chunk_terms, 0)
        section_map(half)
        if half == 0:
            pl.semaphore_wait(barrier, NS - 1 + NP - 1)

        def send_map(t, carry):
            j = (my_j + t) % HALF
            dest = device_of(half, j)

            @pl.when(dest != me)
            def _():
                map_copy(half * HALF + j, dest, me).start()

            return carry

        lax.fori_loop(0, HALF, send_map, 0)

    for copy in small:
        copy.wait()
    face_cell = cell_v[...].reshape(1, FACES)
    face_plane = face_cell // CELLS
    face_at = face_cell % CELLS
    for c in range(CHUNKS):
        at = lax.broadcasted_iota(jnp.int32, (LANES, FACES), 0) + c * LANES
        hot[pl.ds(c * LANES, LANES), :] = jnp.where(at == face_at, 1.0, 0.0).astype(jnp.bfloat16)
    plane_hit = lax.broadcasted_iota(jnp.int32, (PLANES, FACES), 0) == face_plane
    face_id = lax.broadcasted_iota(jnp.int32, (1, FACES), 1)
    live = jnp.where(face_id < count[0], 1.0, 0.0)
    owner_hot = jnp.where(
        lax.broadcasted_iota(jnp.int32, (NP, FACES), 0) == owner_v[...], 1.0, 0.0
    )
    owner_hot16 = owner_hot.astype(jnp.bfloat16)
    earlier = jnp.where(
        lax.broadcasted_iota(jnp.int32, (FACES, FACES), 0)
        < lax.broadcasted_iota(jnp.int32, (FACES, FACES), 1),
        1.0,
        0.0,
    ).astype(jnp.bfloat16)
    before = jnp.dot(owner_hot16, earlier, preferred_element_type=jnp.float32)
    rank = jnp.sum(owner_hot * before, axis=0, keepdims=True).astype(jnp.int32)
    rank_hot = jnp.where(lax.broadcasted_iota(jnp.int32, (CAP, FACES), 0) == rank, 1.0, 0.0)
    slot_value = (slot_v[...].reshape(1, FACES) + 1).astype(jnp.float32) * live
    slot_rows = rank_hot * slot_value
    weight = ail_v[...].reshape(1, FACES).astype(jnp.float32) * live * arm_v[...].reshape(1, FACES)

    maps_in[map_rows(me), :] = maps[out_rows(my_chunk), :]
    vec = [jnp.zeros((1, LANES), jnp.float32) for _ in range(FIELDS)]
    for section in range(NS - 1, 0, -1):

        @pl.when(me != section)
        def _():
            map_copy(0, section, section).wait_recv()

        def entry(n):
            return maps_in[pl.ds(section * MAP_ROWS + n, 1), :]

        matrix = [entry(n) for n in range(FIELDS * FIELDS)]
        vec = matvec(matrix, vec, [entry(FIELDS * FIELDS + i) for i in range(FIELDS)])
        for i in range(FIELDS):
            inc_out[pl.ds((section - 1) * 8 + i, 1), :] = vec[i]

    @pl.when(me != 0)
    def _():
        map_copy(0, 0, 0).wait_recv()

    def inc_copy(dest, c, source):
        return pltpu.make_async_remote_copy(
            src_ref=inc_out.at[pl.ds(pl.multiple_of(dest * 8, 8), 8), :],
            dst_ref=inc_in.at[pl.ds(pl.multiple_of(c * 8, 8), 8), :],
            send_sem=inc_ssem.at[dest],
            recv_sem=inc_rsem.at[source],
            device_id=(dest, q),
            device_id_type=MESH,
        )

    def send_inc(r, carry):
        inc_copy((me + r) % NS, my_chunk, me).start()
        return carry

    lax.fori_loop(1, NS, send_inc, 0)
    inc_in[pl.ds(pl.multiple_of(my_chunk * 8, 8), 8), :] = inc_out[
        pl.ds(pl.multiple_of(me * 8, 8), 8), :
    ]

    for half in range(2):
        for j in range(HALF):
            dev = device_of(half, j)

            @pl.when(me != dev)
            def _():
                inc_copy(dev, half * HALF + j, dev).wait_recv()

    start = tuple(
        tuple(inc_in[pl.ds(half * HALF * 8 + i, HALF, stride=8), :] for i in range(FIELDS))
        for half in range(2)
    )

    def sweep(step, states):
        k = PLANES - 1 - step
        new = []
        for half in range(2):
            coupling = [term(n, half, k) for n in range(FIELDS * FIELDS)]
            source = [term(FIELDS * FIELDS + i, half, k) for i in range(FIELDS)]
            state = matvec(coupling, states[half], source)
            for i in range(FIELDS):
                adj[i, pl.ds(half * HALF * ADJ_PITCH + k, HALF, stride=ADJ_PITCH), :] = state[i]
            new.append(tuple(state))
        return tuple(new)

    lax.fori_loop(0, PLANES, sweep, start)
    gathered = jnp.zeros((2 * FIELDS * PLANES, FACES), jnp.float32)
    for c in range(0, CHUNKS, 2):
        pair = jnp.concatenate(
            [
                adj[:, pl.ds(e * ADJ_PITCH, PLANES), :].reshape(FIELDS * PLANES, LANES)
                for e in (c, c + 1)
            ],
            axis=1,
        )
        gathered = gathered + jnp.dot(
            jnp.concatenate(split(pair), axis=0),
            hot[pl.ds(c * LANES, 2 * LANES), :],
            preferred_element_type=jnp.float32,
        )

    both = gathered[: FIELDS * PLANES] + gathered[FIELDS * PLANES :]
    rows = [
        jnp.sum(
            jnp.where(plane_hit, both[i * PLANES : (i + 1) * PLANES], 0.0), axis=0, keepdims=True
        )
        for i in range(FIELDS)
    ]
    load_rows = []
    for a in range(LOADS):
        total = fmap_v[0, pl.ds(a, 1), :] * rows[0]
        for i in range(1, FIELDS):
            total = total + fmap_v[i, pl.ds(a, 1), :] * rows[i]
        load_rows.append(rank_hot * (total * live))
    hinge_rows = jnp.concatenate(
        [rows[i] * weight for i in range(FIELDS)]
        + [jnp.zeros((LANES - FIELDS, FACES), jnp.float32)],
        axis=0,
    )
    face_rows = jnp.concatenate(
        [jnp.zeros((LOAD_AT, FACES), jnp.float32)]
        + load_rows
        + [slot_rows, jnp.zeros((LANES - SLOT_AT - CAP, FACES), jnp.float32)],
        axis=0,
    )

    def by_face(left, right):
        return lax.dot_general(
            left, right, (((1,), (1,)), ((), ())), preferred_element_type=jnp.float32
        )

    every = jnp.ones((NP, FACES), jnp.bfloat16)
    packed = jnp.zeros((NP, LANES), jnp.float32)
    for piece in split(face_rows):
        packed = packed + by_face(owner_hot16, piece)
    for piece in split(hinge_rows):
        packed = packed + by_face(every, piece)
    msg[:, 0, :] = packed

    def face_copy(dest, source):
        return pltpu.make_async_remote_copy(
            src_ref=msg.at[dest],
            dst_ref=msg_in.at[source],
            send_sem=face_ssem.at[dest],
            recv_sem=face_rsem.at[source],
            device_id=(me, dest),
            device_id_type=MESH,
        )

    def send_face(r, carry):
        face_copy((q + r) % NP, q).start()
        return carry

    lax.fori_loop(1, NP, send_face, 0)
    msg_in[q] = msg[q]

    def wait_face(r, carry):
        peer = (q + r) % NP
        face_copy(peer, peer).wait_recv()
        return carry

    lax.fori_loop(1, NP, wait_face, 0)
    for peer in range(NP):
        rows_in[pl.ds(peer, 1), :] = msg_in[peer]
    arrived = rows_in[...]

    hmsg[0] = jnp.sum(arrived, axis=0, keepdims=True)

    def hinge_copy(dest, source):
        return pltpu.make_async_remote_copy(
            src_ref=hmsg.at[0],
            dst_ref=hmsg_in.at[source],
            send_sem=hinge_ssem.at[dest],
            recv_sem=hinge_rsem.at[source],
            device_id=(dest, q),
            device_id_type=MESH,
        )

    def send_hinge(r, carry):
        hinge_copy((me + r) % NS, me).start()
        return carry

    lax.fori_loop(1, NS, send_hinge, 0)
    hmsg_in[me] = hmsg[0]

    lane = lax.broadcasted_iota(jnp.int32, (NP, LANES), 1) + 1
    loads = [jnp.zeros((NP, SHELL), jnp.float32) for _ in range(LOADS)]
    for pos in range(CAP):
        at = SLOT_AT + pos
        hit = arrived[:, at : at + 1].astype(jnp.int32) == lane
        for a in range(LOADS):
            at = LOAD_AT + a * CAP + pos
            loads[a] = loads[a] + jnp.where(hit, arrived[:, at : at + 1], 0.0)
    for a in range(LOADS):
        shell_out[pl.ds(a, 1), :] = jnp.sum(loads[a], axis=0, keepdims=True)

    def sent(r, carry):
        peer = (me + r) % NS
        map_copy(0, peer, peer).wait_send()
        inc_copy(peer, 0, peer).wait_send()
        return carry

    lax.fori_loop(1, NS, sent, 0)

    def sent_face(r, carry):
        peer = (q + r) % NP
        face_copy(peer, peer).wait_send()
        return carry

    lax.fori_loop(1, NP, sent_face, 0)

    def wait_hinge(r, carry):
        peer = (me + r) % NS
        hinge_copy(peer, peer).wait_send()
        hinge_copy(peer, peer).wait_recv()
        return carry

    lax.fori_loop(1, NS, wait_hinge, 0)
    total = jnp.sum(hmsg_in[:, 0, :], axis=0, keepdims=True)
    hinge_out[...] = total * (1.0 / math.sqrt(NS * NP * FACES))


def store(adj, shell, hinge, adj_out, shell_out, hinge_out, sem):
    copies = [
        pltpu.make_async_copy(
            adj.at[:, pl.ds(c * ADJ_PITCH, PLANES), :],
            adj_out.at[:, :, pl.ds(c * LANES, LANES)],
            sem.at[c],
        )
        for c in range(CHUNKS)
    ]
    for copy in copies:
        copy.start()
    shell_out[...] = shell[...]
    hinge_out[...] = hinge[0, :FIELDS]
    for copy in copies:
        copy.wait()


def on_device(
    forcing,
    inv_diag,
    upper_jac,
    face_cell,
    face_owner,
    face_slot,
    face_count,
    aileron,
    face_map,
    hinge_arm,
):
    anywhere = pl.BlockSpec(memory_space=pltpu.HBM)
    vmem = pl.BlockSpec(memory_space=pltpu.VMEM)
    f32, bf16, i32 = jnp.float32, jnp.bfloat16, jnp.int32
    dma = pltpu.SemaphoreType.DMA
    operands = (
        forcing,
        inv_diag,
        upper_jac,
        face_cell,
        face_owner.T,
        face_slot,
        face_count,
        aileron,
        jnp.swapaxes(face_map, 0, 1),
        hinge_arm,
    )
    operands = [
        x if x is face_count else pltpu.with_memory_space_constraint(x, pltpu.HBM)
        for x in operands
    ]
    results = pl.pallas_call(
        kernel,
        out_shape=(
            pltpu.VMEM((FIELDS, CHUNKS * ADJ_PITCH, LANES), f32),
            pltpu.VMEM((LOADS, SHELL), f32),
            pltpu.VMEM((1, LANES), f32),
        ),
        in_specs=[anywhere] * 6
        + [pl.BlockSpec(memory_space=pltpu.SMEM)]
        + [anywhere] * 3,
        out_specs=(vmem, vmem, vmem),
        scratch_shapes=[
            pltpu.VMEM((FIELDS, PLANES, CELLS), f32),
            pltpu.VMEM((FIELDS, FIELDS, PLANES, CELLS), bf16),
            pltpu.VMEM((FIELDS, FIELDS, PLANES, CELLS), bf16),
            pltpu.VMEM((FACES,), i32),
            pltpu.VMEM((1, FACES), i32),
            pltpu.VMEM((FACES,), i32),
            pltpu.VMEM((FACES,), i32),
            pltpu.VMEM((FIELDS, LOADS, FACES), f32),
            pltpu.VMEM((FACES,), f32),
            pltpu.VMEM((COMPS, CHUNKS * TERM_PITCH, LANES), f32),
            pltpu.VMEM((CHUNKS * MAP_PITCH, LANES), f32),
            pltpu.VMEM((NS * MAP_ROWS, LANES), f32),
            pltpu.VMEM((NS * 8, LANES), f32),
            pltpu.VMEM((CHUNKS * 8, LANES), f32),
            pltpu.VMEM((CELLS, FACES), bf16),
            pltpu.VMEM((NP, 1, LANES), f32),
            pltpu.VMEM((NP, 1, LANES), f32),
            pltpu.VMEM((NP, LANES), f32),
            pltpu.VMEM((1, 1, LANES), f32),
            pltpu.VMEM((NS, 1, LANES), f32),
            dma((GROUPS, 3)),
            dma((6,)),
            dma((NS,)),
            dma((NS,)),
            dma((NS,)),
            dma((NS,)),
            dma((NP,)),
            dma((NP,)),
            dma((NS,)),
            dma((NS,)),
        ],
        compiler_params=pltpu.CompilerParams(
            collective_id=0, has_side_effects=True, vmem_limit_bytes=40 * 1024 * 1024
        ),
        cost_estimate=pl.CostEstimate(
            flops=22_000_000, bytes_accessed=4_700_000, transcendentals=0
        ),
        name="sweep",
    )(*operands)
    return pl.pallas_call(
        store,
        out_shape=(
            jax.ShapeDtypeStruct((FIELDS, PLANES, CELLS), f32),
            jax.ShapeDtypeStruct((LOADS, SHELL), f32),
            jax.ShapeDtypeStruct((FIELDS,), f32),
        ),
        in_specs=[vmem] * 3,
        out_specs=(anywhere, vmem, vmem),
        scratch_shapes=[dma((CHUNKS,))],
        compiler_params=pltpu.CompilerParams(vmem_limit_bytes=16 * 1024 * 1024),
        name="store",
    )(*results)


def solution(mesh):
    in_specs = (
        P(None, "span", "plane"),
        P(None, None, "span", "plane"),
        P(None, None, "span", "plane"),
        P(("span", "plane")),
        P(("span", "plane"), None),
        P(("span", "plane")),
        P(("span", "plane")),
        P(("span", "plane")),
        P(None, None, ("span", "plane")),
        P(("span", "plane")),
    )
    out_specs = (P(None, "span", "plane"), P(None, ("span", "plane")), P())
    return jax.shard_map(
        on_device, mesh=mesh, in_specs=in_specs, out_specs=out_specs, check_vma=False
    )
```

```python
import math

import jax
import jax.numpy as jnp
from jax import lax
from jax.experimental import pallas as pl
from jax.experimental.pallas import tpu as pltpu
from jax.sharding import PartitionSpec as P

MESH = pl.DeviceIdType.MESH

FIELDS = 5
LOADS = 3
NS = 16
NP = 32
PLANES = 16
CELLS = 2048
LANES = 128
CHUNKS = CELLS // LANES
HALF = CHUNKS // 2
FACES = 256
SHELL = 128
CAP = 16
COMPS = FIELDS * (FIELDS + 1)
MAP_ROWS = 32
MAP_PITCH = 40
TERM_PITCH = 17
ADJ_PITCH = 24
GROUPS = 4
GROUP_CELLS = CELLS // GROUPS
GROUP_CHUNKS = CHUNKS // GROUPS
LOAD_AT = 0
SLOT_AT = 48


def chunk_of(dev):
    x, y = dev // 4, dev % 4
    return HALF * ((x + y) % 2) + 2 * x + y // 2


def device_of(half, j):
    x = j // 2
    return 4 * x + 2 * (j % 2) + (half + x) % 2


def split(value):
    high = value.astype(jnp.bfloat16)
    low = (value - high.astype(jnp.float32)).astype(jnp.bfloat16)
    return high, low


def kernel(
    forcing,
    inv_diag,
    upper,
    cell,
    owner,
    slot,
    count,
    aileron,
    fmap,
    arm,
    adj,
    shell_out,
    hinge_out,
    f_v,
    d_v,
    u_v,
    cell_v,
    owner_v,
    slot_v,
    ail_v,
    fmap_v,
    arm_v,
    terms,
    prefix,
    weights,
    maps,
    maps_in,
    gains,
    gains_in,
    inc_out,
    inc_in,
    hot,
    msg,
    msg_in,
    rows_in,
    zmsg,
    zmsg_in,
    hmsg,
    hmsg_in,
    load_sem,
    small_sem,
    map_ssem,
    map_rsem,
    gain_ssem,
    gain_rsem,
    inc_ssem,
    inc_rsem,
    face_ssem,
    face_rsem,
    z_ssem,
    z_rsem,
    hinge_ssem,
    hinge_rsem,
):
    me = lax.axis_index("span")
    q = lax.axis_index("plane")
    barrier = pltpu.get_barrier_semaphore()

    def load_copies(g):
        cells = pl.ds(g * GROUP_CELLS, GROUP_CELLS)
        return (
            pltpu.make_async_copy(
                inv_diag.at[:, :, :, cells], d_v.at[:, :, :, cells], load_sem.at[g, 0]
            ),
            pltpu.make_async_copy(
                upper.at[:, :, :, cells], u_v.at[:, :, :, cells], load_sem.at[g, 1]
            ),
            pltpu.make_async_copy(
                forcing.at[:, :, cells], f_v.at[:, :, cells], load_sem.at[g, 2]
            ),
        )

    small = [
        pltpu.make_async_copy(src, dst, small_sem.at[n])
        for n, (src, dst) in enumerate(
            (
                (cell, cell_v),
                (owner, owner_v),
                (slot, slot_v),
                (aileron, ail_v),
                (fmap, fmap_v),
                (arm, arm_v),
            )
        )
    ]
    for copy in small:
        copy.start()
    for g in range(GROUPS):
        for copy in load_copies(g):
            copy.start()

    def greet_span(r, carry):
        pl.semaphore_signal(
            barrier, inc=1, device_id=((me + r) % NS, q), device_id_type=MESH
        )
        return carry

    def greet_plane(r, carry):
        pl.semaphore_signal(
            barrier, inc=1, device_id=(me, (q + r) % NP), device_id_type=MESH
        )
        return carry

    lax.fori_loop(1, NS, greet_span, 0)
    lax.fori_loop(1, NP, greet_plane, 0)
    inc_out[...] = jnp.zeros_like(inc_out)

    def by_face(left, right):
        return lax.dot_general(
            left, right, (((1,), (1,)), ((), ())), preferred_element_type=jnp.float32
        )

    for copy in small:
        copy.wait()
    face_cell = cell_v[...].reshape(1, FACES)
    face_plane = face_cell // CELLS
    face_at = face_cell % CELLS
    for c in range(CHUNKS):
        at = lax.broadcasted_iota(jnp.int32, (LANES, FACES), 0) + c * LANES
        hot[pl.ds(c * LANES, LANES), :] = jnp.where(at == face_at, 1.0, 0.0).astype(jnp.bfloat16)
    plane_hit = lax.broadcasted_iota(jnp.int32, (PLANES, FACES), 0) == face_plane
    face_id = lax.broadcasted_iota(jnp.int32, (1, FACES), 1)
    live = jnp.where(face_id < count[0], 1.0, 0.0)
    owner_hot = jnp.where(
        lax.broadcasted_iota(jnp.int32, (NP, FACES), 0) == owner_v[...], 1.0, 0.0
    )
    owner_hot16 = owner_hot.astype(jnp.bfloat16)
    earlier = jnp.where(
        lax.broadcasted_iota(jnp.int32, (FACES, FACES), 0)
        < lax.broadcasted_iota(jnp.int32, (FACES, FACES), 1),
        1.0,
        0.0,
    ).astype(jnp.bfloat16)
    before = jnp.dot(owner_hot16, earlier, preferred_element_type=jnp.float32)
    rank = jnp.sum(owner_hot * before, axis=0, keepdims=True).astype(jnp.int32)
    rank_hot = jnp.where(lax.broadcasted_iota(jnp.int32, (CAP, FACES), 0) == rank, 1.0, 0.0)
    slot_value = (slot_v[...].reshape(1, FACES) + 1).astype(jnp.float32) * live
    slot_rows = rank_hot * slot_value
    weight = ail_v[...].reshape(1, FACES).astype(jnp.float32) * live * arm_v[...].reshape(1, FACES)
    at_plane = jnp.where(plane_hit, weight, 0.0)
    for c in range(CHUNKS):
        spread = by_face(jnp.concatenate(split(at_plane), axis=0), hot[pl.ds(c * LANES, LANES), :])
        weights[pl.ds(c * TERM_PITCH, PLANES), :] = spread[:PLANES] + spread[PLANES:]

    def chunk_terms(c, carry):
        cells = pl.ds(pl.multiple_of(c * LANES, LANES), LANES)
        rows = pl.ds(c * TERM_PITCH, PLANES)
        up = [
            [u_v[j, m, :, cells].astype(jnp.float32) for m in range(FIELDS)]
            for j in range(FIELDS)
        ]
        rhs = [f_v[m, :, cells] for m in range(FIELDS)]
        for i in range(FIELDS):
            inv = [d_v[m, i, :, cells].astype(jnp.float32) for m in range(FIELDS)]
            for j in range(FIELDS):
                total = inv[0] * up[j][0]
                for m in range(1, FIELDS):
                    total = total + inv[m] * up[j][m]
                terms[i * FIELDS + j, rows, :] = -total
            total = inv[0] * rhs[0]
            for m in range(1, FIELDS):
                total = total + inv[m] * rhs[m]
            terms[FIELDS * FIELDS + i, rows, :] = total
        return carry

    def term(n, half, k):
        return terms[n, pl.ds(half * HALF * TERM_PITCH + k, HALF, stride=TERM_PITCH), :]

    def matvec(coupling, vec, start=None):
        out = []
        for i in range(FIELDS):
            total = coupling[i * FIELDS] * vec[0]
            for j in range(1, FIELDS):
                total = total + coupling[i * FIELDS + j] * vec[j]
            out.append(total if start is None else total + start[i])
        return out

    def prefix_rows(half, k):
        return pl.ds(pl.multiple_of((k * 2 + half) * HALF, HALF), HALF)

    def section_map(half):
        state = tuple(term(n, half, PLANES - 1) for n in range(COMPS))
        for n in range(COMPS):
            prefix[n, prefix_rows(half, PLANES - 1), :] = state[n]

        def compose(step, state):
            k = PLANES - 2 - step
            coupling = [term(n, half, k) for n in range(FIELDS * FIELDS)]
            source = [term(FIELDS * FIELDS + i, half, k) for i in range(FIELDS)]
            new = [None] * COMPS
            for col in range(FIELDS):
                column = matvec(coupling, [state[j * FIELDS + col] for j in range(FIELDS)])
                for i in range(FIELDS):
                    new[i * FIELDS + col] = column[i]
            new[FIELDS * FIELDS :] = matvec(coupling, state[FIELDS * FIELDS :], source)
            for n in range(COMPS):
                prefix[n, prefix_rows(half, k), :] = new[n]
            return tuple(new)

        state = lax.fori_loop(0, PLANES - 1, compose, state)
        for n in range(COMPS):
            maps[pl.ds(half * HALF * MAP_PITCH + n, HALF, stride=MAP_PITCH), :] = state[n]

    def out_rows(c):
        return pl.ds(pl.multiple_of(c * MAP_PITCH, 8), MAP_ROWS)

    def map_rows(c):
        return pl.ds(pl.multiple_of(c * MAP_ROWS, MAP_ROWS), MAP_ROWS)

    def map_copy(c, dest, source):
        return pltpu.make_async_remote_copy(
            src_ref=maps.at[out_rows(c), :],
            dst_ref=maps_in.at[map_rows(source), :],
            send_sem=map_ssem.at[dest],
            recv_sem=map_rsem.at[source],
            device_id=(dest, q),
            device_id_type=MESH,
        )

    def gain_copy(c, dest, source):
        return pltpu.make_async_remote_copy(
            src_ref=gains.at[out_rows(c), :],
            dst_ref=gains_in.at[map_rows(source), :],
            send_sem=gain_ssem.at[dest],
            recv_sem=gain_rsem.at[source],
            device_id=(dest, q),
            device_id_type=MESH,
        )

    for n in range(FIELDS * FIELDS, MAP_ROWS):
        gains[pl.ds(n, CHUNKS, stride=MAP_PITCH), :] = jnp.zeros((CHUNKS, LANES), jnp.float32)
    for n in range(COMPS, MAP_ROWS):
        maps[pl.ds(n, CHUNKS, stride=MAP_PITCH), :] = jnp.zeros((CHUNKS, LANES), jnp.float32)

    my_chunk = chunk_of(me)
    my_j = my_chunk % HALF
    for half in range(2):
        for g in range(half * GROUPS // 2, (half + 1) * GROUPS // 2):
            for copy in load_copies(g):
                copy.wait()
            lax.fori_loop(g * GROUP_CHUNKS, (g + 1) * GROUP_CHUNKS, chunk_terms, 0)
        section_map(half)
        if half == 0:
            pl.semaphore_wait(barrier, NS - 1 + NP - 1)

        def send_map(t, carry):
            j = (my_j + t) % HALF
            dest = device_of(half, j)

            @pl.when(dest != me)
            def _():
                map_copy(half * HALF + j, dest, me).start()

            return carry

        lax.fori_loop(0, HALF, send_map, 0)

    constant = [jnp.zeros((HALF, LANES), jnp.float32) for _ in range(FIELDS)]
    for half in range(2):

        def add_plane(k, total):
            weight_k = weights[pl.ds(half * HALF * TERM_PITCH + k, HALF, stride=TERM_PITCH), :]
            return tuple(
                total[n] + weight_k * prefix[n, prefix_rows(half, k), :] for n in range(COMPS)
            )

        zero = jnp.zeros((HALF, LANES), jnp.float32)
        total = lax.fori_loop(0, PLANES, add_plane, (zero,) * COMPS)
        for n in range(FIELDS * FIELDS):
            gains[pl.ds(half * HALF * MAP_PITCH + n, HALF, stride=MAP_PITCH), :] = total[n]
        constant = [constant[i] + total[FIELDS * FIELDS + i] for i in range(FIELDS)]

    def send_gain(r, carry):
        dest = (me + r) % NS
        gain_copy(chunk_of(dest), dest, me).start()
        return carry

    lax.fori_loop(1, NS, send_gain, 0)
    gains_in[map_rows(me), :] = gains[out_rows(my_chunk), :]

    maps_in[map_rows(me), :] = maps[out_rows(my_chunk), :]
    vec = [jnp.zeros((1, LANES), jnp.float32) for _ in range(FIELDS)]
    for section in range(NS - 1, 0, -1):

        @pl.when(me != section)
        def _():
            map_copy(0, section, section).wait_recv()

        def entry(n):
            return maps_in[pl.ds(section * MAP_ROWS + n, 1), :]

        matrix = [entry(n) for n in range(FIELDS * FIELDS)]
        vec = matvec(matrix, vec, [entry(FIELDS * FIELDS + i) for i in range(FIELDS)])
        for i in range(FIELDS):
            inc_out[pl.ds((section - 1) * 8 + i, 1), :] = vec[i]

    @pl.when(me != 0)
    def _():
        map_copy(0, 0, 0).wait_recv()

    def inc_copy(dest, c, source):
        return pltpu.make_async_remote_copy(
            src_ref=inc_out.at[pl.ds(pl.multiple_of(dest * 8, 8), 8), :],
            dst_ref=inc_in.at[pl.ds(pl.multiple_of(c * 8, 8), 8), :],
            send_sem=inc_ssem.at[dest],
            recv_sem=inc_rsem.at[source],
            device_id=(dest, q),
            device_id_type=MESH,
        )

    def send_inc(r, carry):
        inc_copy((me + r) % NS, my_chunk, me).start()
        return carry

    lax.fori_loop(1, NS, send_inc, 0)
    inc_in[pl.ds(pl.multiple_of(my_chunk * 8, 8), 8), :] = inc_out[
        pl.ds(pl.multiple_of(me * 8, 8), 8), :
    ]

    def wait_gain(r, carry):
        peer = (me + r) % NS
        gain_copy(0, peer, peer).wait_recv()
        return carry

    lax.fori_loop(1, NS, wait_gain, 0)
    partial = constant
    for section in range(NS - 1):
        entering = inc_out[pl.ds(section * 8, 8), :]
        partial = [
            partial[i]
            + gains_in[pl.ds(section * MAP_ROWS + i * FIELDS, 8), :] * entering
            for i in range(FIELDS)
        ]
    columns = jnp.concatenate(
        [jnp.sum(partial[i], axis=0, keepdims=True) for i in range(FIELDS)]
        + [jnp.zeros((8 - FIELDS, LANES), jnp.float32)],
        axis=0,
    )
    diagonal = lax.broadcasted_iota(jnp.int32, (8, LANES), 0) == lax.broadcasted_iota(
        jnp.int32, (8, LANES), 1
    )
    zmsg[0] = jnp.sum(
        jnp.where(diagonal, jnp.sum(columns, axis=1, keepdims=True), 0.0), axis=0, keepdims=True
    )

    def z_copy(dest, source):
        return pltpu.make_async_remote_copy(
            src_ref=zmsg.at[0],
            dst_ref=zmsg_in.at[source],
            send_sem=z_ssem.at[dest],
            recv_sem=z_rsem.at[source],
            device_id=(me, dest),
            device_id_type=MESH,
        )

    def send_z(r, carry):
        z_copy((q + r) % NP, q).start()
        return carry

    lax.fori_loop(1, NP, send_z, 0)
    zmsg_in[q] = zmsg[0]

    for half in range(2):
        for j in range(HALF):
            dev = device_of(half, j)

            @pl.when(me != dev)
            def _():
                inc_copy(dev, half * HALF + j, dev).wait_recv()

    start = tuple(
        tuple(inc_in[pl.ds(half * HALF * 8 + i, HALF, stride=8), :] for i in range(FIELDS))
        for half in range(2)
    )

    def sweep(step, states):
        k = PLANES - 1 - step
        new = []
        for half in range(2):
            coupling = [term(n, half, k) for n in range(FIELDS * FIELDS)]
            source = [term(FIELDS * FIELDS + i, half, k) for i in range(FIELDS)]
            state = matvec(coupling, states[half], source)
            for i in range(FIELDS):
                adj[i, pl.ds(half * HALF * ADJ_PITCH + k, HALF, stride=ADJ_PITCH), :] = state[i]
            new.append(tuple(state))
        return tuple(new)

    lax.fori_loop(0, PLANES, sweep, start)
    gathered = jnp.zeros((2 * FIELDS * PLANES, FACES), jnp.float32)
    for c in range(0, CHUNKS, 2):
        pair = jnp.concatenate(
            [
                adj[:, pl.ds(e * ADJ_PITCH, PLANES), :].reshape(FIELDS * PLANES, LANES)
                for e in (c, c + 1)
            ],
            axis=1,
        )
        gathered = gathered + jnp.dot(
            jnp.concatenate(split(pair), axis=0),
            hot[pl.ds(c * LANES, 2 * LANES), :],
            preferred_element_type=jnp.float32,
        )

    both = gathered[: FIELDS * PLANES] + gathered[FIELDS * PLANES :]
    rows = [
        jnp.sum(
            jnp.where(plane_hit, both[i * PLANES : (i + 1) * PLANES], 0.0), axis=0, keepdims=True
        )
        for i in range(FIELDS)
    ]
    load_rows = []
    for a in range(LOADS):
        total = fmap_v[0, pl.ds(a, 1), :] * rows[0]
        for i in range(1, FIELDS):
            total = total + fmap_v[i, pl.ds(a, 1), :] * rows[i]
        load_rows.append(rank_hot * (total * live))
    face_rows = jnp.concatenate(
        load_rows
        + [slot_rows, jnp.zeros((LANES - SLOT_AT - CAP, FACES), jnp.float32)],
        axis=0,
    )

    packed = jnp.zeros((NP, LANES), jnp.float32)
    for piece in split(face_rows):
        packed = packed + by_face(owner_hot16, piece)
    msg[:, 0, :] = packed

    def face_copy(dest, source):
        return pltpu.make_async_remote_copy(
            src_ref=msg.at[dest],
            dst_ref=msg_in.at[source],
            send_sem=face_ssem.at[dest],
            recv_sem=face_rsem.at[source],
            device_id=(me, dest),
            device_id_type=MESH,
        )

    def send_face(r, carry):
        face_copy((q + r) % NP, q).start()
        return carry

    lax.fori_loop(1, NP, send_face, 0)
    msg_in[q] = msg[q]

    def wait_z(r, carry):
        peer = (q + r) % NP
        z_copy(peer, peer).wait_recv()
        return carry

    lax.fori_loop(1, NP, wait_z, 0)
    hmsg[0] = jnp.sum(zmsg_in[...], axis=0)

    def hinge_copy(dest, source):
        return pltpu.make_async_remote_copy(
            src_ref=hmsg.at[0],
            dst_ref=hmsg_in.at[source],
            send_sem=hinge_ssem.at[dest],
            recv_sem=hinge_rsem.at[source],
            device_id=(dest, q),
            device_id_type=MESH,
        )

    def send_hinge(r, carry):
        hinge_copy((me + r) % NS, me).start()
        return carry

    lax.fori_loop(1, NS, send_hinge, 0)
    hmsg_in[me] = hmsg[0]

    def wait_face(r, carry):
        peer = (q + r) % NP
        face_copy(peer, peer).wait_recv()
        return carry

    lax.fori_loop(1, NP, wait_face, 0)
    for peer in range(NP):
        rows_in[pl.ds(peer, 1), :] = msg_in[peer]
    arrived = rows_in[...]

    lane = lax.broadcasted_iota(jnp.int32, (NP, LANES), 1) + 1
    loads = [jnp.zeros((NP, SHELL), jnp.float32) for _ in range(LOADS)]
    for pos in range(CAP):
        at = SLOT_AT + pos
        hit = arrived[:, at : at + 1].astype(jnp.int32) == lane
        for a in range(LOADS):
            at = LOAD_AT + a * CAP + pos
            loads[a] = loads[a] + jnp.where(hit, arrived[:, at : at + 1], 0.0)
    for a in range(LOADS):
        shell_out[pl.ds(a, 1), :] = jnp.sum(loads[a], axis=0, keepdims=True)

    def sent(r, carry):
        peer = (me + r) % NS
        map_copy(0, peer, peer).wait_send()
        gain_copy(0, peer, peer).wait_send()
        inc_copy(peer, 0, peer).wait_send()
        return carry

    lax.fori_loop(1, NS, sent, 0)

    def sent_face(r, carry):
        peer = (q + r) % NP
        face_copy(peer, peer).wait_send()
        z_copy(peer, peer).wait_send()
        return carry

    lax.fori_loop(1, NP, sent_face, 0)

    def wait_hinge(r, carry):
        peer = (me + r) % NS
        hinge_copy(peer, peer).wait_send()
        hinge_copy(peer, peer).wait_recv()
        return carry

    lax.fori_loop(1, NS, wait_hinge, 0)
    total = jnp.sum(hmsg_in[:, 0, :], axis=0, keepdims=True)
    hinge_out[...] = total * (1.0 / math.sqrt(NS * NP * FACES))


def store(adj, shell, hinge, adj_out, shell_out, hinge_out, sem):
    copies = [
        pltpu.make_async_copy(
            adj.at[:, pl.ds(c * ADJ_PITCH, PLANES), :],
            adj_out.at[:, :, pl.ds(c * LANES, LANES)],
            sem.at[c],
        )
        for c in range(CHUNKS)
    ]
    for copy in copies:
        copy.start()
    shell_out[...] = shell[...]
    hinge_out[...] = hinge[0, :FIELDS]
    for copy in copies:
        copy.wait()


def on_device(
    forcing,
    inv_diag,
    upper_jac,
    face_cell,
    face_owner,
    face_slot,
    face_count,
    aileron,
    face_map,
    hinge_arm,
):
    anywhere = pl.BlockSpec(memory_space=pltpu.HBM)
    vmem = pl.BlockSpec(memory_space=pltpu.VMEM)
    f32, bf16, i32 = jnp.float32, jnp.bfloat16, jnp.int32
    dma = pltpu.SemaphoreType.DMA
    operands = (
        forcing,
        inv_diag,
        upper_jac,
        face_cell,
        face_owner.T,
        face_slot,
        face_count,
        aileron,
        jnp.swapaxes(face_map, 0, 1),
        hinge_arm,
    )
    operands = [
        x if x is face_count else pltpu.with_memory_space_constraint(x, pltpu.HBM)
        for x in operands
    ]
    results = pl.pallas_call(
        kernel,
        out_shape=(
            pltpu.VMEM((FIELDS, CHUNKS * ADJ_PITCH, LANES), f32),
            pltpu.VMEM((LOADS, SHELL), f32),
            pltpu.VMEM((1, LANES), f32),
        ),
        in_specs=[anywhere] * 6
        + [pl.BlockSpec(memory_space=pltpu.SMEM)]
        + [anywhere] * 3,
        out_specs=(vmem, vmem, vmem),
        scratch_shapes=[
            pltpu.VMEM((FIELDS, PLANES, CELLS), f32),
            pltpu.VMEM((FIELDS, FIELDS, PLANES, CELLS), bf16),
            pltpu.VMEM((FIELDS, FIELDS, PLANES, CELLS), bf16),
            pltpu.VMEM((FACES,), i32),
            pltpu.VMEM((1, FACES), i32),
            pltpu.VMEM((FACES,), i32),
            pltpu.VMEM((FACES,), i32),
            pltpu.VMEM((FIELDS, LOADS, FACES), f32),
            pltpu.VMEM((FACES,), f32),
            pltpu.VMEM((COMPS, CHUNKS * TERM_PITCH, LANES), f32),
            pltpu.VMEM((COMPS, 2 * PLANES * HALF, LANES), f32),
            pltpu.VMEM((CHUNKS * TERM_PITCH, LANES), f32),
            pltpu.VMEM((CHUNKS * MAP_PITCH, LANES), f32),
            pltpu.VMEM((NS * MAP_ROWS, LANES), f32),
            pltpu.VMEM((CHUNKS * MAP_PITCH, LANES), f32),
            pltpu.VMEM((NS * MAP_ROWS, LANES), f32),
            pltpu.VMEM((NS * 8, LANES), f32),
            pltpu.VMEM((CHUNKS * 8, LANES), f32),
            pltpu.VMEM((CELLS, FACES), bf16),
            pltpu.VMEM((NP, 1, LANES), f32),
            pltpu.VMEM((NP, 1, LANES), f32),
            pltpu.VMEM((NP, LANES), f32),
            pltpu.VMEM((1, 1, LANES), f32),
            pltpu.VMEM((NP, 1, LANES), f32),
            pltpu.VMEM((1, 1, LANES), f32),
            pltpu.VMEM((NS, 1, LANES), f32),
            dma((GROUPS, 3)),
            dma((6,)),
            dma((NS,)),
            dma((NS,)),
            dma((NS,)),
            dma((NS,)),
            dma((NS,)),
            dma((NS,)),
            dma((NP,)),
            dma((NP,)),
            dma((NP,)),
            dma((NP,)),
            dma((NS,)),
            dma((NS,)),
        ],
        compiler_params=pltpu.CompilerParams(
            collective_id=0, has_side_effects=True, vmem_limit_bytes=40 * 1024 * 1024
        ),
        cost_estimate=pl.CostEstimate(
            flops=22_000_000, bytes_accessed=4_700_000, transcendentals=0
        ),
        name="sweep",
    )(*operands)
    return pl.pallas_call(
        store,
        out_shape=(
            jax.ShapeDtypeStruct((FIELDS, PLANES, CELLS), f32),
            jax.ShapeDtypeStruct((LOADS, SHELL), f32),
            jax.ShapeDtypeStruct((FIELDS,), f32),
        ),
        in_specs=[vmem] * 3,
        out_specs=(anywhere, vmem, vmem),
        scratch_shapes=[dma((CHUNKS,))],
        compiler_params=pltpu.CompilerParams(vmem_limit_bytes=16 * 1024 * 1024),
        name="store",
    )(*results)


def solution(mesh):
    in_specs = (
        P(None, "span", "plane"),
        P(None, None, "span", "plane"),
        P(None, None, "span", "plane"),
        P(("span", "plane")),
        P(("span", "plane"), None),
        P(("span", "plane")),
        P(("span", "plane")),
        P(("span", "plane")),
        P(None, None, ("span", "plane")),
        P(("span", "plane")),
    )
    out_specs = (P(None, "span", "plane"), P(None, ("span", "plane")), P())
    return jax.shard_map(
        on_device, mesh=mesh, in_specs=in_specs, out_specs=out_specs, check_vma=False
    )
```

```python
import math

import jax
import jax.numpy as jnp
from jax import lax
from jax.experimental import pallas as pl
from jax.experimental.pallas import tpu as pltpu
from jax.sharding import PartitionSpec as P

MESH = pl.DeviceIdType.MESH

FIELDS = 5
LOADS = 3
NS = 16
NP = 32
PLANES = 16
CELLS = 2048
LANES = 128
CHUNKS = CELLS // LANES
HALF = CHUNKS // 2
FACES = 256
SHELL = 128
CAP = 16
COMPS = FIELDS * (FIELDS + 1)
MAP_ROWS = 32
MAP_PITCH = 40
TERM_PITCH = 17
ADJ_PITCH = 24
GROUPS = 4
GROUP_CELLS = CELLS // GROUPS
GROUP_CHUNKS = CHUNKS // GROUPS
HINGE_AT = 0
LOAD_AT = 16
SLOT_AT = 64


def chunk_of(dev):
    x, y = dev // 4, dev % 4
    return HALF * ((x + y) % 2) + 2 * x + y // 2


def device_of(half, j):
    x = j // 2
    return 4 * x + 2 * (j % 2) + (half + x) % 2


def split(value):
    high = value.astype(jnp.bfloat16)
    low = (value - high.astype(jnp.float32)).astype(jnp.bfloat16)
    return high, low


def kernel(
    forcing,
    inv_diag,
    upper,
    cell,
    owner,
    slot,
    count,
    aileron,
    fmap,
    arm,
    adj,
    shell_out,
    hinge_out,
    f_v,
    d_v,
    u_v,
    cell_v,
    owner_v,
    slot_v,
    ail_v,
    fmap_v,
    arm_v,
    terms,
    maps,
    maps_in,
    inc_out,
    inc_in,
    hot,
    msg,
    msg_in,
    rows_in,
    hmsg,
    hmsg_in,
    ready,
    load_sem,
    small_sem,
    map_ssem,
    map_rsem,
    inc_ssem,
    inc_rsem,
    face_ssem,
    face_rsem,
    hinge_ssem,
    hinge_rsem,
):
    me = lax.axis_index("span")
    q = lax.axis_index("plane")
    barrier = pltpu.get_barrier_semaphore()

    def load_copies(g):
        cells = pl.ds(g * GROUP_CELLS, GROUP_CELLS)
        return (
            pltpu.make_async_copy(
                inv_diag.at[:, :, :, cells], d_v.at[:, :, :, cells], load_sem.at[g, 0]
            ),
            pltpu.make_async_copy(
                upper.at[:, :, :, cells], u_v.at[:, :, :, cells], load_sem.at[g, 1]
            ),
            pltpu.make_async_copy(
                forcing.at[:, :, cells], f_v.at[:, :, cells], load_sem.at[g, 2]
            ),
        )

    for g in range(GROUPS):
        for copy in load_copies(g):
            copy.start()
    small = [
        pltpu.make_async_copy(src, dst, small_sem.at[n])
        for n, (src, dst) in enumerate(
            (
                (cell, cell_v),
                (owner, owner_v),
                (slot, slot_v),
                (aileron, ail_v),
                (fmap, fmap_v),
                (arm, arm_v),
            )
        )
    ]
    for copy in small:
        copy.start()

    def greet_span(r, carry):
        pl.semaphore_signal(
            barrier, inc=1, device_id=((me + r) % NS, q), device_id_type=MESH
        )
        return carry

    depth, core = q // 2, q % 2

    def along(distance, other=0):
        return (me, ((depth + distance) % (NP // 2)) * 2 + (core + other) % 2)

    near = [along(0, 1)] + [along(d, other) for d in (1, -1) for other in (0, 1)]
    for peer in near:
        pl.semaphore_signal(barrier, inc=1, device_id=peer, device_id_type=MESH)
    lax.fori_loop(1, NS, greet_span, 0)

    def tell(step):
        for d in (1 << step, -(1 << step)):
            pl.semaphore_signal(
                ready.at[step], inc=1, device_id=along(d), device_id_type=MESH
            )

    def hear(step):
        pl.semaphore_wait(ready.at[step], 2)

    inc_out[...] = jnp.zeros_like(inc_out)

    def everything(ref, count, send_sem, recv_sem, peer):
        whole = ref.at[pl.ds(0, count)]
        return pltpu.make_async_remote_copy(
            src_ref=whole,
            dst_ref=whole,
            send_sem=send_sem,
            recv_sem=recv_sem,
            device_id=peer,
            device_id_type=MESH,
        )

    def chunk_terms(c, carry):
        cells = pl.ds(pl.multiple_of(c * LANES, LANES), LANES)
        rows = pl.ds(c * TERM_PITCH, PLANES)
        up = [
            [u_v[j, m, :, cells].astype(jnp.float32) for m in range(FIELDS)]
            for j in range(FIELDS)
        ]
        rhs = [f_v[m, :, cells] for m in range(FIELDS)]
        for i in range(FIELDS):
            inv = [d_v[m, i, :, cells].astype(jnp.float32) for m in range(FIELDS)]
            for j in range(FIELDS):
                total = inv[0] * up[j][0]
                for m in range(1, FIELDS):
                    total = total + inv[m] * up[j][m]
                terms[i * FIELDS + j, rows, :] = -total
            total = inv[0] * rhs[0]
            for m in range(1, FIELDS):
                total = total + inv[m] * rhs[m]
            terms[FIELDS * FIELDS + i, rows, :] = total
        return carry

    def term(n, half, k):
        return terms[n, pl.ds(half * HALF * TERM_PITCH + k, HALF, stride=TERM_PITCH), :]

    def matvec(coupling, vec, start=None):
        out = []
        for i in range(FIELDS):
            total = coupling[i * FIELDS] * vec[0]
            for j in range(1, FIELDS):
                total = total + coupling[i * FIELDS + j] * vec[j]
            out.append(total if start is None else total + start[i])
        return out

    def section_map(half):
        state = tuple(term(n, half, PLANES - 1) for n in range(COMPS))

        def compose(step, state):
            k = PLANES - 2 - step
            coupling = [term(n, half, k) for n in range(FIELDS * FIELDS)]
            source = [term(FIELDS * FIELDS + i, half, k) for i in range(FIELDS)]
            new = [None] * COMPS
            for col in range(FIELDS):
                column = matvec(coupling, [state[j * FIELDS + col] for j in range(FIELDS)])
                for i in range(FIELDS):
                    new[i * FIELDS + col] = column[i]
            new[FIELDS * FIELDS :] = matvec(coupling, state[FIELDS * FIELDS :], source)
            return tuple(new)

        state = lax.fori_loop(0, PLANES - 1, compose, state)
        for n in range(COMPS):
            maps[pl.ds(half * HALF * MAP_PITCH + n, HALF, stride=MAP_PITCH), :] = state[n]

    def out_rows(c):
        return pl.ds(pl.multiple_of(c * MAP_PITCH, 8), MAP_ROWS)

    def map_rows(c):
        return pl.ds(pl.multiple_of(c * MAP_ROWS, MAP_ROWS), MAP_ROWS)

    def map_copy(c, dest, source):
        return pltpu.make_async_remote_copy(
            src_ref=maps.at[out_rows(c), :],
            dst_ref=maps_in.at[map_rows(source), :],
            send_sem=map_ssem,
            recv_sem=map_rsem,
            device_id=(dest, q),
            device_id_type=MESH,
        )

    for n in range(COMPS, MAP_ROWS):
        maps[pl.ds(n, CHUNKS, stride=MAP_PITCH), :] = jnp.zeros((CHUNKS, LANES), jnp.float32)

    my_chunk = chunk_of(me)
    my_j = my_chunk % HALF
    for half in range(2):
        for g in range(half * GROUPS // 2, (half + 1) * GROUPS // 2):
            for copy in load_copies(g):
                copy.wait()
            lax.fori_loop(g * GROUP_CHUNKS, (g + 1) * GROUP_CHUNKS, chunk_terms, 0)
        section_map(half)
        if half == 0:
            pl.semaphore_wait(barrier, NS - 1 + len(near))
            tell(0)

        def send_map(t, carry):
            j = (my_j + t) % HALF
            dest = device_of(half, j)

            @pl.when(dest != me)
            def _():
                map_copy(half * HALF + j, dest, me).start()

            return carry

        lax.fori_loop(0, HALF, send_map, 0)

    hear(0)
    tell(1)

    for copy in small:
        copy.wait()
    face_cell = cell_v[...].reshape(1, FACES)
    face_plane = face_cell // CELLS
    face_at = face_cell % CELLS
    for c in range(CHUNKS):
        at = lax.broadcasted_iota(jnp.int32, (LANES, FACES), 0) + c * LANES
        hot[pl.ds(c * LANES, LANES), :] = jnp.where(at == face_at, 1.0, 0.0).astype(jnp.bfloat16)
    plane_hit = lax.broadcasted_iota(jnp.int32, (PLANES, FACES), 0) == face_plane
    face_id = lax.broadcasted_iota(jnp.int32, (1, FACES), 1)
    live = jnp.where(face_id < count[0], 1.0, 0.0)
    owner_hot = jnp.where(
        lax.broadcasted_iota(jnp.int32, (NP, FACES), 0) == owner_v[...], 1.0, 0.0
    )
    owner_hot16 = owner_hot.astype(jnp.bfloat16)
    earlier = jnp.where(
        lax.broadcasted_iota(jnp.int32, (FACES, FACES), 0)
        < lax.broadcasted_iota(jnp.int32, (FACES, FACES), 1),
        1.0,
        0.0,
    ).astype(jnp.bfloat16)
    before = jnp.dot(owner_hot16, earlier, preferred_element_type=jnp.float32)
    rank = jnp.sum(owner_hot * before, axis=0, keepdims=True).astype(jnp.int32)
    rank_hot = jnp.where(lax.broadcasted_iota(jnp.int32, (CAP, FACES), 0) == rank, 1.0, 0.0)
    slot_value = (slot_v[...].reshape(1, FACES) + 1).astype(jnp.float32) * live
    slot_rows = rank_hot * slot_value
    weight = ail_v[...].reshape(1, FACES).astype(jnp.float32) * live * arm_v[...].reshape(1, FACES)

    hear(1)
    tell(2)

    all_maps = everything(maps_in, (NS - 1) * MAP_ROWS, map_ssem, map_rsem, near[0])
    all_maps.wait_recv()
    maps_in[map_rows(me), :] = maps[out_rows(my_chunk), :]
    vec = [jnp.zeros((1, LANES), jnp.float32) for _ in range(FIELDS)]
    for section in range(NS - 1, 0, -1):

        def entry(n):
            return maps_in[pl.ds(section * MAP_ROWS + n, 1), :]

        matrix = [entry(n) for n in range(FIELDS * FIELDS)]
        vec = matvec(matrix, vec, [entry(FIELDS * FIELDS + i) for i in range(FIELDS)])
        for i in range(FIELDS):
            inc_out[pl.ds((section - 1) * 8 + i, 1), :] = vec[i]

    def inc_copy(dest, c, source):
        return pltpu.make_async_remote_copy(
            src_ref=inc_out.at[pl.ds(pl.multiple_of(dest * 8, 8), 8), :],
            dst_ref=inc_in.at[pl.ds(pl.multiple_of(c * 8, 8), 8), :],
            send_sem=inc_ssem,
            recv_sem=inc_rsem,
            device_id=(dest, q),
            device_id_type=MESH,
        )

    def send_inc(r, carry):
        inc_copy((me + r) % NS, my_chunk, me).start()
        return carry

    lax.fori_loop(1, NS, send_inc, 0)
    all_inc = everything(inc_in, (NS - 1) * 8, inc_ssem, inc_rsem, near[0])
    all_inc.wait_recv()
    inc_in[pl.ds(pl.multiple_of(my_chunk * 8, 8), 8), :] = inc_out[
        pl.ds(pl.multiple_of(me * 8, 8), 8), :
    ]

    start = tuple(
        tuple(inc_in[pl.ds(half * HALF * 8 + i, HALF, stride=8), :] for i in range(FIELDS))
        for half in range(2)
    )

    def sweep(step, states):
        k = PLANES - 1 - step
        new = []
        for half in range(2):
            coupling = [term(n, half, k) for n in range(FIELDS * FIELDS)]
            source = [term(FIELDS * FIELDS + i, half, k) for i in range(FIELDS)]
            state = matvec(coupling, states[half], source)
            for i in range(FIELDS):
                adj[i, pl.ds(half * HALF * ADJ_PITCH + k, HALF, stride=ADJ_PITCH), :] = state[i]
            new.append(tuple(state))
        return tuple(new)

    lax.fori_loop(0, PLANES, sweep, start)
    gathered = jnp.zeros((2 * FIELDS * PLANES, FACES), jnp.float32)
    for c in range(0, CHUNKS, 2):
        pair = jnp.concatenate(
            [
                adj[:, pl.ds(e * ADJ_PITCH, PLANES), :].reshape(FIELDS * PLANES, LANES)
                for e in (c, c + 1)
            ],
            axis=1,
        )
        gathered = gathered + jnp.dot(
            jnp.concatenate(split(pair), axis=0),
            hot[pl.ds(c * LANES, 2 * LANES), :],
            preferred_element_type=jnp.float32,
        )

    both = gathered[: FIELDS * PLANES] + gathered[FIELDS * PLANES :]
    rows = [
        jnp.sum(
            jnp.where(plane_hit, both[i * PLANES : (i + 1) * PLANES], 0.0), axis=0, keepdims=True
        )
        for i in range(FIELDS)
    ]
    load_rows = []
    for a in range(LOADS):
        total = fmap_v[0, pl.ds(a, 1), :] * rows[0]
        for i in range(1, FIELDS):
            total = total + fmap_v[i, pl.ds(a, 1), :] * rows[i]
        load_rows.append(rank_hot * (total * live))
    hinge_rows = jnp.concatenate(
        [rows[i] * weight for i in range(FIELDS)]
        + [jnp.zeros((LANES - FIELDS, FACES), jnp.float32)],
        axis=0,
    )
    face_rows = jnp.concatenate(
        [jnp.zeros((LOAD_AT, FACES), jnp.float32)]
        + load_rows
        + [slot_rows, jnp.zeros((LANES - SLOT_AT - CAP, FACES), jnp.float32)],
        axis=0,
    )

    def by_face(left, right):
        return lax.dot_general(
            left, right, (((1,), (1,)), ((), ())), preferred_element_type=jnp.float32
        )

    every = jnp.ones((NP, FACES), jnp.bfloat16)
    packed = jnp.zeros((NP, LANES), jnp.float32)
    for piece in split(face_rows):
        packed = packed + by_face(owner_hot16, piece)
    for piece in split(hinge_rows):
        packed = packed + by_face(every, piece)
    msg[:, 0, :] = packed

    def face_copy(dest, source):
        return pltpu.make_async_remote_copy(
            src_ref=msg.at[dest],
            dst_ref=msg_in.at[source],
            send_sem=face_ssem,
            recv_sem=face_rsem,
            device_id=(me, dest),
            device_id_type=MESH,
        )

    hear(2)

    def send_face(r, carry):
        face_copy((q + r) % NP, q).start()
        return carry

    lax.fori_loop(1, NP, send_face, 0)
    all_faces = everything(msg_in, NP - 1, face_ssem, face_rsem, near[0])
    all_faces.wait_recv()
    msg_in[q] = msg[q]
    for peer in range(NP):
        rows_in[pl.ds(peer, 1), :] = msg_in[peer]
    arrived = rows_in[...]

    hmsg[0] = jnp.sum(arrived, axis=0, keepdims=True)

    def hinge_copy(dest, source):
        return pltpu.make_async_remote_copy(
            src_ref=hmsg.at[0],
            dst_ref=hmsg_in.at[source],
            send_sem=hinge_ssem,
            recv_sem=hinge_rsem,
            device_id=(dest, q),
            device_id_type=MESH,
        )

    def send_hinge(r, carry):
        hinge_copy((me + r) % NS, me).start()
        return carry

    lax.fori_loop(1, NS, send_hinge, 0)

    lane = lax.broadcasted_iota(jnp.int32, (NP, LANES), 1) + 1
    loads = [jnp.zeros((NP, SHELL), jnp.float32) for _ in range(LOADS)]
    for pos in range(CAP):
        at = SLOT_AT + pos
        hit = arrived[:, at : at + 1].astype(jnp.int32) == lane
        for a in range(LOADS):
            at = LOAD_AT + a * CAP + pos
            loads[a] = loads[a] + jnp.where(hit, arrived[:, at : at + 1], 0.0)
    for a in range(LOADS):
        shell_out[pl.ds(a, 1), :] = jnp.sum(loads[a], axis=0, keepdims=True)

    all_maps.wait_send()
    all_inc.wait_send()
    all_faces.wait_send()
    all_hinge = everything(hmsg_in, NS - 1, hinge_ssem, hinge_rsem, near[0])
    all_hinge.wait_send()
    all_hinge.wait_recv()
    hmsg_in[me] = hmsg[0]
    total = jnp.sum(hmsg_in[:, 0, :], axis=0) * (1.0 / math.sqrt(NS * NP * FACES))
    hinge_out[...] = total[:FIELDS]


def store(adj, shell, hinge, adj_out, shell_out, hinge_out, adj_sem, shell_sem, hinge_sem):
    for c in range(CHUNKS):
        pltpu.make_async_copy(
            adj.at[:, pl.ds(c * ADJ_PITCH, PLANES), :],
            adj_out.at[:, :, pl.ds(c * LANES, LANES)],
            adj_sem,
        ).start()
    rest = (
        pltpu.make_async_copy(shell, shell_out, shell_sem),
        pltpu.make_async_copy(hinge, hinge_out, hinge_sem),
    )
    for copy in rest:
        copy.start()
    pltpu.make_async_copy(adj_out, adj_out, adj_sem).wait()
    for copy in rest:
        copy.wait()


def on_device(
    forcing,
    inv_diag,
    upper_jac,
    face_cell,
    face_owner,
    face_slot,
    face_count,
    aileron,
    face_map,
    hinge_arm,
):
    anywhere = pl.BlockSpec(memory_space=pltpu.HBM)
    vmem = pl.BlockSpec(memory_space=pltpu.VMEM)
    f32, bf16, i32 = jnp.float32, jnp.bfloat16, jnp.int32
    dma = pltpu.SemaphoreType.DMA
    operands = (
        forcing,
        inv_diag,
        upper_jac,
        face_cell,
        face_owner.T,
        face_slot,
        face_count,
        aileron,
        jnp.swapaxes(face_map, 0, 1),
        hinge_arm,
    )
    operands = [
        x if x is face_count else pltpu.with_memory_space_constraint(x, pltpu.HBM)
        for x in operands
    ]
    results = pl.pallas_call(
        kernel,
        out_shape=(
            pltpu.VMEM((FIELDS, CHUNKS * ADJ_PITCH, LANES), f32),
            pltpu.VMEM((LOADS, SHELL), f32),
            pltpu.VMEM((FIELDS,), f32),
        ),
        in_specs=[anywhere] * 6
        + [pl.BlockSpec(memory_space=pltpu.SMEM)]
        + [anywhere] * 3,
        out_specs=(vmem, vmem, vmem),
        scratch_shapes=[
            pltpu.VMEM((FIELDS, PLANES, CELLS), f32),
            pltpu.VMEM((FIELDS, FIELDS, PLANES, CELLS), bf16),
            pltpu.VMEM((FIELDS, FIELDS, PLANES, CELLS), bf16),
            pltpu.VMEM((FACES,), i32),
            pltpu.VMEM((1, FACES), i32),
            pltpu.VMEM((FACES,), i32),
            pltpu.VMEM((FACES,), i32),
            pltpu.VMEM((FIELDS, LOADS, FACES), f32),
            pltpu.VMEM((FACES,), f32),
            pltpu.VMEM((COMPS, CHUNKS * TERM_PITCH, LANES), f32),
            pltpu.VMEM((CHUNKS * MAP_PITCH, LANES), f32),
            pltpu.VMEM((NS * MAP_ROWS, LANES), f32),
            pltpu.VMEM((NS * 8, LANES), f32),
            pltpu.VMEM((CHUNKS * 8, LANES), f32),
            pltpu.VMEM((CELLS, FACES), bf16),
            pltpu.VMEM((NP, 1, LANES), f32),
            pltpu.VMEM((NP, 1, LANES), f32),
            pltpu.VMEM((NP, LANES), f32),
            pltpu.VMEM((1, 1, LANES), f32),
            pltpu.VMEM((NS, 1, LANES), f32),
            pltpu.SemaphoreType.REGULAR((3,)),
            dma((GROUPS, 3)),
            dma((6,)),
        ]
        + [dma] * 8,
        compiler_params=pltpu.CompilerParams(
            collective_id=0, has_side_effects=True, vmem_limit_bytes=40 * 1024 * 1024
        ),
        cost_estimate=pl.CostEstimate(
            flops=22_000_000, bytes_accessed=4_700_000, transcendentals=0
        ),
        name="sweep",
    )(*operands)
    return pl.pallas_call(
        store,
        out_shape=(
            jax.ShapeDtypeStruct((FIELDS, PLANES, CELLS), f32),
            jax.ShapeDtypeStruct((LOADS, SHELL), f32),
            jax.ShapeDtypeStruct((FIELDS,), f32),
        ),
        in_specs=[vmem] * 3,
        out_specs=[anywhere] * 3,
        scratch_shapes=[dma] * 3,
        compiler_params=pltpu.CompilerParams(vmem_limit_bytes=16 * 1024 * 1024),
        name="store",
    )(*results)


def solution(mesh):
    in_specs = (
        P(None, "span", "plane"),
        P(None, None, "span", "plane"),
        P(None, None, "span", "plane"),
        P(("span", "plane")),
        P(("span", "plane"), None),
        P(("span", "plane")),
        P(("span", "plane")),
        P(("span", "plane")),
        P(None, None, ("span", "plane")),
        P(("span", "plane")),
    )
    out_specs = (P(None, "span", "plane"), P(None, ("span", "plane")), P())
    return jax.shard_map(
        on_device, mesh=mesh, in_specs=in_specs, out_specs=out_specs, check_vma=False
    )
```

```python
import math

import jax
import jax.numpy as jnp
from jax import lax
from jax.experimental import pallas as pl
from jax.experimental.pallas import tpu as pltpu
from jax.sharding import PartitionSpec as P

MESH = pl.DeviceIdType.MESH

FIELDS = 5
LOADS = 3
NS = 16
NP = 32
PLANES = 16
CELLS = 2048
LANES = 128
CHUNKS = CELLS // LANES
HALF = CHUNKS // 2
OWN = 10
SENDS = ((0, 1, 2, 3, 4, 5, 6, 7), (12, 13, 14, 15, 8, 9, 11))
FACES = 256
SHELL = 128
CAP = 16
COMPS = FIELDS * (FIELDS + 1)
MAP_ROWS = 32
MAP_PITCH = 40
TERM_PITCH = 17
ADJ_PITCH = 24
GROUPS = 4
GROUP_CELLS = CELLS // GROUPS
GROUP_CHUNKS = CHUNKS // GROUPS
LOAD_AT = 0
SLOT_AT = 48


def owner_of(dev, pos):
    return 4 * ((dev // 4 + pos // 4 + 2) % 4) + (dev + pos + 2) % 4


def mirror(pos):
    return 4 * ((4 - pos // 4) % 4) + (4 - pos % 4) % 4


def split(value):
    high = value.astype(jnp.bfloat16)
    low = (value - high.astype(jnp.float32)).astype(jnp.bfloat16)
    return high, low


def kernel(
    forcing,
    inv_diag,
    upper,
    cell,
    owner,
    slot,
    count,
    aileron,
    fmap,
    arm,
    adj,
    shell_out,
    hinge_out,
    f_v,
    d_v,
    u_v,
    cell_v,
    owner_v,
    slot_v,
    ail_v,
    fmap_v,
    arm_v,
    terms,
    prefix,
    weights,
    gains,
    maps,
    maps_in,
    inc_out,
    inc_in,
    hot,
    msg,
    msg_in,
    rows_in,
    zmsg,
    zmsg_in,
    hmsg,
    hmsg_in,
    ready,
    load_sem,
    small_sem,
    map_ssem,
    map_rsem,
    inc_ssem,
    inc_rsem,
    face_ssem,
    face_rsem,
    z_ssem,
    z_rsem,
    hinge_ssem,
    hinge_rsem,
):
    me = lax.axis_index("span")
    q = lax.axis_index("plane")
    barrier = pltpu.get_barrier_semaphore()

    def load_copies(g):
        block = (me // 4 + g + 2) % 4
        cells = pl.ds(pl.multiple_of(block * GROUP_CELLS, GROUP_CELLS), GROUP_CELLS)
        here = pl.ds(g * GROUP_CELLS, GROUP_CELLS)
        return (
            pltpu.make_async_copy(
                inv_diag.at[:, :, :, cells], d_v.at[:, :, :, here], load_sem.at[g, 0]
            ),
            pltpu.make_async_copy(
                upper.at[:, :, :, cells], u_v.at[:, :, :, here], load_sem.at[g, 1]
            ),
            pltpu.make_async_copy(
                forcing.at[:, :, cells], f_v.at[:, :, here], load_sem.at[g, 2]
            ),
        )

    for g in range(GROUPS):
        for copy in load_copies(g):
            copy.start()
    small = [
        pltpu.make_async_copy(src, dst, small_sem.at[n])
        for n, (src, dst) in enumerate(
            (
                (cell, cell_v),
                (owner, owner_v),
                (slot, slot_v),
                (aileron, ail_v),
                (fmap, fmap_v),
                (arm, arm_v),
            )
        )
    ]
    for copy in small:
        copy.start()

    def greet_span(pos, carry):
        pl.semaphore_signal(
            barrier, inc=1, device_id=(owner_of(me, pos), q), device_id_type=MESH
        )
        return carry

    depth, core = q // 2, q % 2

    def along(distance, other=0):
        return (me, ((depth + distance) % (NP // 2)) * 2 + (core + other) % 2)

    near = [along(0, 1)] + [along(d, other) for d in (1, -1) for other in (0, 1)]
    lax.fori_loop(0, OWN, greet_span, 0)
    lax.fori_loop(OWN + 1, NS, greet_span, 0)
    for peer in near:
        pl.semaphore_signal(barrier, inc=1, device_id=peer, device_id_type=MESH)

    def tell(step):
        for d in (1 << step, -(1 << step)):
            pl.semaphore_signal(
                ready.at[step], inc=1, device_id=along(d), device_id_type=MESH
            )

    def hear(step):
        pl.semaphore_wait(ready.at[step], 2)

    inc_out[...] = jnp.zeros_like(inc_out)

    def everything(ref, count, send_sem, recv_sem, peer):
        whole = ref.at[pl.ds(0, count)]
        return pltpu.make_async_remote_copy(
            src_ref=whole,
            dst_ref=whole,
            send_sem=send_sem,
            recv_sem=recv_sem,
            device_id=peer,
            device_id_type=MESH,
        )

    def chunk_terms(c, carry):
        cells = pl.ds(
            pl.multiple_of(c // 4 * GROUP_CELLS + (me + c + 2) % 4 * LANES, LANES), LANES
        )
        rows = pl.ds(c * TERM_PITCH, PLANES)
        up = [
            [u_v[j, m, :, cells].astype(jnp.float32) for m in range(FIELDS)]
            for j in range(FIELDS)
        ]
        rhs = [f_v[m, :, cells] for m in range(FIELDS)]
        for i in range(FIELDS):
            inv = [d_v[m, i, :, cells].astype(jnp.float32) for m in range(FIELDS)]
            for j in range(FIELDS):
                total = inv[0] * up[j][0]
                for m in range(1, FIELDS):
                    total = total + inv[m] * up[j][m]
                terms[i * FIELDS + j, rows, :] = -total
            total = inv[0] * rhs[0]
            for m in range(1, FIELDS):
                total = total + inv[m] * rhs[m]
            terms[FIELDS * FIELDS + i, rows, :] = total
        return carry

    def term(n, half, k):
        return terms[n, pl.ds(half * HALF * TERM_PITCH + k, HALF, stride=TERM_PITCH), :]

    def matvec(coupling, vec, start=None):
        out = []
        for i in range(FIELDS):
            total = coupling[i * FIELDS] * vec[0]
            for j in range(1, FIELDS):
                total = total + coupling[i * FIELDS + j] * vec[j]
            out.append(total if start is None else total + start[i])
        return out

    def prefix_rows(half, k):
        return pl.ds(pl.multiple_of((k * 2 + half) * HALF, HALF), HALF)

    def section_map(half):
        state = tuple(term(n, half, PLANES - 1) for n in range(COMPS))
        for n in range(COMPS):
            prefix[n, prefix_rows(half, PLANES - 1), :] = state[n]

        def compose(step, state):
            k = PLANES - 2 - step
            coupling = [term(n, half, k) for n in range(FIELDS * FIELDS)]
            source = [term(FIELDS * FIELDS + i, half, k) for i in range(FIELDS)]
            new = [None] * COMPS
            for col in range(FIELDS):
                column = matvec(coupling, [state[j * FIELDS + col] for j in range(FIELDS)])
                for i in range(FIELDS):
                    new[i * FIELDS + col] = column[i]
            new[FIELDS * FIELDS :] = matvec(coupling, state[FIELDS * FIELDS :], source)
            for n in range(COMPS):
                prefix[n, prefix_rows(half, k), :] = new[n]
            return tuple(new)

        state = lax.fori_loop(0, PLANES - 1, compose, state)
        for n in range(COMPS):
            maps[pl.ds(half * HALF * MAP_PITCH + n, HALF, stride=MAP_PITCH), :] = state[n]

    def out_rows(c):
        return pl.ds(pl.multiple_of(c * MAP_PITCH, 8), MAP_ROWS)

    def map_rows(c):
        return pl.ds(pl.multiple_of(c * MAP_ROWS, MAP_ROWS), MAP_ROWS)

    def map_copy(c, dest, source):
        return pltpu.make_async_remote_copy(
            src_ref=maps.at[out_rows(c), :],
            dst_ref=maps_in.at[map_rows(source), :],
            send_sem=map_ssem,
            recv_sem=map_rsem,
            device_id=(dest, q),
            device_id_type=MESH,
        )

    for n in range(COMPS, MAP_ROWS):
        maps[pl.ds(n, CHUNKS, stride=MAP_PITCH), :] = jnp.zeros((CHUNKS, LANES), jnp.float32)

    for half in range(2):
        for g in range(half * GROUPS // 2, (half + 1) * GROUPS // 2):
            for copy in load_copies(g):
                copy.wait()
            lax.fori_loop(g * GROUP_CHUNKS, (g + 1) * GROUP_CHUNKS, chunk_terms, 0)
        section_map(half)
        if half == 0:
            pl.semaphore_wait(barrier, NS - 1 + len(near))
            tell(0)

        for pos in SENDS[half]:
            map_copy(pos, owner_of(me, pos), me).start()

    hear(0)
    tell(1)

    for copy in small:
        copy.wait()
    face_cell = cell_v[...].reshape(1, FACES)
    face_plane = face_cell // CELLS
    face_at = face_cell % CELLS
    for c in range(CHUNKS):
        at = lax.broadcasted_iota(jnp.int32, (LANES, FACES), 0)
        here = face_at - owner_of(me, c) * LANES
        hot[pl.ds(c * LANES, LANES), :] = jnp.where(at == here, 1.0, 0.0).astype(jnp.bfloat16)
    plane_hit = lax.broadcasted_iota(jnp.int32, (PLANES, FACES), 0) == face_plane
    face_id = lax.broadcasted_iota(jnp.int32, (1, FACES), 1)
    live = jnp.where(face_id < count[0], 1.0, 0.0)
    owner_hot = jnp.where(
        lax.broadcasted_iota(jnp.int32, (NP, FACES), 0) == owner_v[...], 1.0, 0.0
    )
    owner_hot16 = owner_hot.astype(jnp.bfloat16)
    earlier = jnp.where(
        lax.broadcasted_iota(jnp.int32, (FACES, FACES), 0)
        < lax.broadcasted_iota(jnp.int32, (FACES, FACES), 1),
        1.0,
        0.0,
    ).astype(jnp.bfloat16)
    before = jnp.dot(owner_hot16, earlier, preferred_element_type=jnp.float32)
    rank = jnp.sum(owner_hot * before, axis=0, keepdims=True).astype(jnp.int32)
    rank_hot = jnp.where(lax.broadcasted_iota(jnp.int32, (CAP, FACES), 0) == rank, 1.0, 0.0)
    slot_value = (slot_v[...].reshape(1, FACES) + 1).astype(jnp.float32) * live
    slot_rows = rank_hot * slot_value
    weight = ail_v[...].reshape(1, FACES).astype(jnp.float32) * live * arm_v[...].reshape(1, FACES)

    hear(1)
    tell(2)

    def by_face(left, right):
        return lax.dot_general(
            left, right, (((1,), (1,)), ((), ())), preferred_element_type=jnp.float32
        )

    at_plane = jnp.concatenate(split(jnp.where(plane_hit, weight, 0.0)), axis=0)
    for c in range(CHUNKS):
        spread = by_face(at_plane, hot[pl.ds(c * LANES, LANES), :])
        weights[pl.ds(c * TERM_PITCH, PLANES), :] = spread[:PLANES] + spread[PLANES:]
    for half in range(2):

        def add_plane(k, total):
            weight_k = weights[pl.ds(half * HALF * TERM_PITCH + k, HALF, stride=TERM_PITCH), :]
            return tuple(
                total[n] + weight_k * prefix[n, prefix_rows(half, k), :] for n in range(COMPS)
            )

        zero = jnp.zeros((HALF, LANES), jnp.float32)
        total = lax.fori_loop(0, PLANES, add_plane, (zero,) * COMPS)
        for n in range(COMPS):
            gains[n, pl.ds(half * HALF, HALF), :] = total[n]

    all_maps = everything(maps_in, (NS - 1) * MAP_ROWS, map_ssem, map_rsem, near[0])
    all_maps.wait_recv()
    maps_in[map_rows(me), :] = maps[out_rows(OWN), :]
    vec = [jnp.zeros((1, LANES), jnp.float32) for _ in range(FIELDS)]
    for section in range(NS - 1, 0, -1):

        def entry(n):
            return maps_in[pl.ds(section * MAP_ROWS + n, 1), :]

        matrix = [entry(n) for n in range(FIELDS * FIELDS)]
        vec = matvec(matrix, vec, [entry(FIELDS * FIELDS + i) for i in range(FIELDS)])
        for i in range(FIELDS):
            inc_out[pl.ds((section - 1) * 8 + i, 1), :] = vec[i]

    def send_inc(pos, carry):
        dest = owner_of(me, pos)
        pltpu.make_async_remote_copy(
            src_ref=inc_out.at[pl.ds(pl.multiple_of(dest * 8, 8), 8), :],
            dst_ref=inc_in.at[pl.ds(pl.multiple_of(mirror(pos) * 8, 8), 8), :],
            send_sem=inc_ssem,
            recv_sem=inc_rsem,
            device_id=(dest, q),
            device_id_type=MESH,
        ).start()
        return carry

    lax.fori_loop(0, OWN, send_inc, 0)
    lax.fori_loop(OWN + 1, NS, send_inc, 0)
    all_inc = everything(inc_in, (NS - 1) * 8, inc_ssem, inc_rsem, near[0])
    all_inc.wait_recv()
    inc_in[pl.ds(OWN * 8, 8), :] = inc_out[
        pl.ds(pl.multiple_of(me * 8, 8), 8), :
    ]

    start = tuple(
        tuple(inc_in[pl.ds(half * HALF * 8 + i, HALF, stride=8), :] for i in range(FIELDS))
        for half in range(2)
    )

    partial = [
        sum(gains[FIELDS * FIELDS + i, pl.ds(half * HALF, HALF), :] for half in range(2))
        for i in range(FIELDS)
    ]
    for half in range(2):
        for i in range(FIELDS):
            for j in range(FIELDS):
                gain = gains[i * FIELDS + j, pl.ds(half * HALF, HALF), :]
                partial[i] = partial[i] + gain * start[half][j]
    columns = jnp.concatenate(
        [jnp.sum(partial[i], axis=0, keepdims=True) for i in range(FIELDS)]
        + [jnp.zeros((8 - FIELDS, LANES), jnp.float32)],
        axis=0,
    )
    diagonal = lax.broadcasted_iota(jnp.int32, (8, LANES), 0) == lax.broadcasted_iota(
        jnp.int32, (8, LANES), 1
    )
    hmsg[0] = jnp.sum(
        jnp.where(diagonal, jnp.sum(columns, axis=1, keepdims=True), 0.0), axis=0, keepdims=True
    )

    def hinge_copy(dest, source):
        return pltpu.make_async_remote_copy(
            src_ref=hmsg.at[0],
            dst_ref=hmsg_in.at[source],
            send_sem=hinge_ssem,
            recv_sem=hinge_rsem,
            device_id=(dest, q),
            device_id_type=MESH,
        )

    def send_hinge(pos, carry):
        hinge_copy(owner_of(me, pos), me).start()
        return carry

    lax.fori_loop(0, OWN, send_hinge, 0)
    lax.fori_loop(OWN + 1, NS, send_hinge, 0)

    def sweep(step, states):
        k = PLANES - 1 - step
        new = []
        for half in range(2):
            coupling = [term(n, half, k) for n in range(FIELDS * FIELDS)]
            source = [term(FIELDS * FIELDS + i, half, k) for i in range(FIELDS)]
            state = matvec(coupling, states[half], source)
            for i in range(FIELDS):
                adj[i, pl.ds(half * HALF * ADJ_PITCH + k, HALF, stride=ADJ_PITCH), :] = state[i]
            new.append(tuple(state))
        return tuple(new)

    lax.fori_loop(0, PLANES, sweep, start)
    gathered = jnp.zeros((2 * FIELDS * PLANES, FACES), jnp.float32)
    for c in range(0, CHUNKS, 2):
        pair = jnp.concatenate(
            [
                adj[:, pl.ds(e * ADJ_PITCH, PLANES), :].reshape(FIELDS * PLANES, LANES)
                for e in (c, c + 1)
            ],
            axis=1,
        )
        gathered = gathered + jnp.dot(
            jnp.concatenate(split(pair), axis=0),
            hot[pl.ds(c * LANES, 2 * LANES), :],
            preferred_element_type=jnp.float32,
        )

    both = gathered[: FIELDS * PLANES] + gathered[FIELDS * PLANES :]
    rows = [
        jnp.sum(
            jnp.where(plane_hit, both[i * PLANES : (i + 1) * PLANES], 0.0), axis=0, keepdims=True
        )
        for i in range(FIELDS)
    ]
    load_rows = []
    for a in range(LOADS):
        total = fmap_v[0, pl.ds(a, 1), :] * rows[0]
        for i in range(1, FIELDS):
            total = total + fmap_v[i, pl.ds(a, 1), :] * rows[i]
        load_rows.append(rank_hot * (total * live))
    face_rows = jnp.concatenate(
        load_rows
        + [slot_rows, jnp.zeros((LANES - SLOT_AT - CAP, FACES), jnp.float32)],
        axis=0,
    )

    packed = jnp.zeros((NP, LANES), jnp.float32)
    for piece in split(face_rows):
        packed = packed + by_face(owner_hot16, piece)
    msg[:, 0, :] = packed

    def face_copy(dest, source):
        return pltpu.make_async_remote_copy(
            src_ref=msg.at[dest],
            dst_ref=msg_in.at[source],
            send_sem=face_ssem,
            recv_sem=face_rsem,
            device_id=(me, dest),
            device_id_type=MESH,
        )

    hear(2)

    def far_first(t):
        return (q + NP // 2 + (t + 1) // 2 * (1 - 2 * (t % 2))) % NP

    def send_face(t, carry):
        face_copy(far_first(t), q).start()
        return carry

    lax.fori_loop(0, NP - 1, send_face, 0)
    all_hinge = everything(hmsg_in, NS - 1, hinge_ssem, hinge_rsem, near[0])
    all_hinge.wait_recv()
    hmsg_in[me] = hmsg[0]
    zmsg[0] = jnp.sum(hmsg_in[...], axis=0)

    def send_z(t, carry):
        pltpu.make_async_remote_copy(
            src_ref=zmsg.at[0],
            dst_ref=zmsg_in.at[q],
            send_sem=z_ssem,
            recv_sem=z_rsem,
            device_id=(me, far_first(t)),
            device_id_type=MESH,
        ).start()
        return carry

    lax.fori_loop(0, NP - 1, send_z, 0)
    all_faces = everything(msg_in, NP - 1, face_ssem, face_rsem, near[0])
    all_faces.wait_recv()
    msg_in[q] = msg[q]
    for peer in range(NP):
        rows_in[pl.ds(peer, 1), :] = msg_in[peer]
    arrived = rows_in[...]

    lane = lax.broadcasted_iota(jnp.int32, (NP, LANES), 1) + 1
    loads = [jnp.zeros((NP, SHELL), jnp.float32) for _ in range(LOADS)]
    for pos in range(CAP):
        at = SLOT_AT + pos
        hit = arrived[:, at : at + 1].astype(jnp.int32) == lane
        for a in range(LOADS):
            at = LOAD_AT + a * CAP + pos
            loads[a] = loads[a] + jnp.where(hit, arrived[:, at : at + 1], 0.0)
    for a in range(LOADS):
        shell_out[pl.ds(a, 1), :] = jnp.sum(loads[a], axis=0, keepdims=True)

    all_maps.wait_send()
    all_inc.wait_send()
    all_faces.wait_send()
    all_hinge.wait_send()
    all_z = everything(zmsg_in, NP - 1, z_ssem, z_rsem, near[0])
    all_z.wait_send()
    all_z.wait_recv()
    zmsg_in[q] = zmsg[0]
    total = jnp.sum(zmsg_in[:, 0, :], axis=0) * (1.0 / math.sqrt(NS * NP * FACES))
    hinge_out[...] = total[:FIELDS]


def store(adj, shell, hinge, adj_out, shell_out, hinge_out, adj_sem, shell_sem, hinge_sem):
    me = lax.axis_index("span")
    for c in range(CHUNKS):
        cells = pl.ds(pl.multiple_of(owner_of(me, c) * LANES, LANES), LANES)
        pltpu.make_async_copy(
            adj.at[:, pl.ds(c * ADJ_PITCH, PLANES), :],
            adj_out.at[:, :, cells],
            adj_sem,
        ).start()
    rest = (
        pltpu.make_async_copy(shell, shell_out, shell_sem),
        pltpu.make_async_copy(hinge, hinge_out, hinge_sem),
    )
    for copy in rest:
        copy.start()
    pltpu.make_async_copy(adj_out, adj_out, adj_sem).wait()
    for copy in rest:
        copy.wait()


def on_device(
    forcing,
    inv_diag,
    upper_jac,
    face_cell,
    face_owner,
    face_slot,
    face_count,
    aileron,
    face_map,
    hinge_arm,
):
    anywhere = pl.BlockSpec(memory_space=pltpu.HBM)
    vmem = pl.BlockSpec(memory_space=pltpu.VMEM)
    f32, bf16, i32 = jnp.float32, jnp.bfloat16, jnp.int32
    dma = pltpu.SemaphoreType.DMA
    operands = (
        forcing,
        inv_diag,
        upper_jac,
        face_cell,
        face_owner.T,
        face_slot,
        face_count,
        aileron,
        jnp.swapaxes(face_map, 0, 1),
        hinge_arm,
    )
    operands = [
        x if x is face_count else pltpu.with_memory_space_constraint(x, pltpu.HBM)
        for x in operands
    ]
    results = pl.pallas_call(
        kernel,
        out_shape=(
            pltpu.VMEM((FIELDS, CHUNKS * ADJ_PITCH, LANES), f32),
            pltpu.VMEM((LOADS, SHELL), f32),
            pltpu.VMEM((FIELDS,), f32),
        ),
        in_specs=[anywhere] * 6
        + [pl.BlockSpec(memory_space=pltpu.SMEM)]
        + [anywhere] * 3,
        out_specs=(vmem, vmem, vmem),
        scratch_shapes=[
            pltpu.VMEM((FIELDS, PLANES, CELLS), f32),
            pltpu.VMEM((FIELDS, FIELDS, PLANES, CELLS), bf16),
            pltpu.VMEM((FIELDS, FIELDS, PLANES, CELLS), bf16),
            pltpu.VMEM((FACES,), i32),
            pltpu.VMEM((1, FACES), i32),
            pltpu.VMEM((FACES,), i32),
            pltpu.VMEM((FACES,), i32),
            pltpu.VMEM((FIELDS, LOADS, FACES), f32),
            pltpu.VMEM((FACES,), f32),
            pltpu.VMEM((COMPS, CHUNKS * TERM_PITCH, LANES), f32),
            pltpu.VMEM((COMPS, 2 * PLANES * HALF, LANES), f32),
            pltpu.VMEM((CHUNKS * TERM_PITCH, LANES), f32),
            pltpu.VMEM((COMPS, 2 * HALF, LANES), f32),
            pltpu.VMEM((CHUNKS * MAP_PITCH, LANES), f32),
            pltpu.VMEM((NS * MAP_ROWS, LANES), f32),
            pltpu.VMEM((NS * 8, LANES), f32),
            pltpu.VMEM((CHUNKS * 8, LANES), f32),
            pltpu.VMEM((CELLS, FACES), bf16),
            pltpu.VMEM((NP, 1, LANES), f32),
            pltpu.VMEM((NP, 1, LANES), f32),
            pltpu.VMEM((NP, LANES), f32),
            pltpu.VMEM((1, 1, LANES), f32),
            pltpu.VMEM((NP, 1, LANES), f32),
            pltpu.VMEM((1, 1, LANES), f32),
            pltpu.VMEM((NS, 1, LANES), f32),
            pltpu.SemaphoreType.REGULAR((3,)),
            dma((GROUPS, 3)),
            dma((6,)),
        ]
        + [dma] * 10,
        compiler_params=pltpu.CompilerParams(
            collective_id=0, has_side_effects=True, vmem_limit_bytes=40 * 1024 * 1024
        ),
        cost_estimate=pl.CostEstimate(
            flops=22_000_000, bytes_accessed=4_700_000, transcendentals=0
        ),
        name="sweep",
    )(*operands)
    return pl.pallas_call(
        store,
        out_shape=(
            jax.ShapeDtypeStruct((FIELDS, PLANES, CELLS), f32),
            jax.ShapeDtypeStruct((LOADS, SHELL), f32),
            jax.ShapeDtypeStruct((FIELDS,), f32),
        ),
        in_specs=[vmem] * 3,
        out_specs=[anywhere] * 3,
        scratch_shapes=[dma] * 3,
        compiler_params=pltpu.CompilerParams(vmem_limit_bytes=16 * 1024 * 1024),
        name="store",
    )(*results)


def solution(mesh):
    in_specs = (
        P(None, "span", "plane"),
        P(None, None, "span", "plane"),
        P(None, None, "span", "plane"),
        P(("span", "plane")),
        P(("span", "plane"), None),
        P(("span", "plane")),
        P(("span", "plane")),
        P(("span", "plane")),
        P(None, None, ("span", "plane")),
        P(("span", "plane")),
    )
    out_specs = (P(None, "span", "plane"), P(None, ("span", "plane")), P())
    return jax.shard_map(
        on_device, mesh=mesh, in_specs=in_specs, out_specs=out_specs, check_vma=False
    )
```

```python
import math

import jax
import jax.numpy as jnp
from jax import lax
from jax.experimental import pallas as pl
from jax.experimental.pallas import tpu as pltpu
from jax.sharding import PartitionSpec as P

MESH = pl.DeviceIdType.MESH

FIELDS = 5
LOADS = 3
NS = 16
NP = 32
PLANES = 16
CELLS = 2048
LANES = 128
CHUNKS = CELLS // LANES
HALF = CHUNKS // 2
OWN = 10
SENDS = ((0, 1, 2, 3, 4, 5, 6, 7), (12, 13, 14, 15, 8, 9, 11))
FACES = 256
SHELL = 128
CAP = 16
COMPS = FIELDS * (FIELDS + 1)
MAP_ROWS = 32
MAP_PITCH = 40
TERM_PITCH = 17
ADJ_PITCH = 24
GROUPS = 4
GROUP_CELLS = CELLS // GROUPS
GROUP_CHUNKS = CHUNKS // GROUPS
LOAD_AT = 0
SLOT_AT = 48


def owner_of(dev, pos):
    return 4 * ((dev // 4 + pos // 4 + 2) % 4) + (dev + pos + 2) % 4


def mirror(pos):
    return 4 * ((4 - pos // 4) % 4) + (4 - pos % 4) % 4


def split(value):
    high = value.astype(jnp.bfloat16)
    low = (value - high.astype(jnp.float32)).astype(jnp.bfloat16)
    return high, low


def kernel(
    forcing,
    inv_diag,
    upper,
    cell,
    owner,
    slot,
    count,
    aileron,
    fmap,
    arm,
    adj,
    shell_out,
    hinge_out,
    f_v,
    d_v,
    u_v,
    cell_v,
    owner_v,
    slot_v,
    ail_v,
    fmap_v,
    arm_v,
    terms,
    prefix,
    weights,
    gains,
    gains_in,
    maps,
    maps_in,
    inc_out,
    inc_in,
    hot,
    msg,
    msg_in,
    rows_in,
    zmsg,
    zmsg_in,
    hmsg,
    hmsg_in,
    ready,
    load_sem,
    small_sem,
    map_ssem,
    map_rsem,
    gain_ssem,
    gain_rsem,
    inc_ssem,
    inc_rsem,
    face_ssem,
    face_rsem,
    z_ssem,
    z_rsem,
    hinge_ssem,
    hinge_rsem,
):
    me = lax.axis_index("span")
    q = lax.axis_index("plane")
    barrier = pltpu.get_barrier_semaphore()

    def load_copies(g):
        block = (me // 4 + g + 2) % 4
        cells = pl.ds(pl.multiple_of(block * GROUP_CELLS, GROUP_CELLS), GROUP_CELLS)
        here = pl.ds(g * GROUP_CELLS, GROUP_CELLS)
        return (
            pltpu.make_async_copy(
                inv_diag.at[:, :, :, cells], d_v.at[:, :, :, here], load_sem.at[g, 0]
            ),
            pltpu.make_async_copy(
                upper.at[:, :, :, cells], u_v.at[:, :, :, here], load_sem.at[g, 1]
            ),
            pltpu.make_async_copy(
                forcing.at[:, :, cells], f_v.at[:, :, here], load_sem.at[g, 2]
            ),
        )

    for g in range(GROUPS):
        for copy in load_copies(g):
            copy.start()
    small = [
        pltpu.make_async_copy(src, dst, small_sem.at[n])
        for n, (src, dst) in enumerate(
            (
                (cell, cell_v),
                (owner, owner_v),
                (slot, slot_v),
                (aileron, ail_v),
                (fmap, fmap_v),
                (arm, arm_v),
            )
        )
    ]
    for copy in small:
        copy.start()

    def greet_span(pos, carry):
        pl.semaphore_signal(
            barrier, inc=1, device_id=(owner_of(me, pos), q), device_id_type=MESH
        )
        return carry

    depth, core = q // 2, q % 2

    def along(distance, other=0):
        return (me, ((depth + distance) % (NP // 2)) * 2 + (core + other) % 2)

    near = [along(0, 1)] + [along(d, other) for d in (1, -1) for other in (0, 1)]
    lax.fori_loop(0, OWN, greet_span, 0)
    lax.fori_loop(OWN + 1, NS, greet_span, 0)
    for peer in near:
        pl.semaphore_signal(barrier, inc=1, device_id=peer, device_id_type=MESH)

    def tell(step):
        for d in (1 << step, -(1 << step)):
            pl.semaphore_signal(
                ready.at[step], inc=1, device_id=along(d), device_id_type=MESH
            )

    def hear(step):
        pl.semaphore_wait(ready.at[step], 2)

    inc_out[...] = jnp.zeros_like(inc_out)

    def everything(ref, count, send_sem, recv_sem, peer):
        whole = ref.at[pl.ds(0, count)]
        return pltpu.make_async_remote_copy(
            src_ref=whole,
            dst_ref=whole,
            send_sem=send_sem,
            recv_sem=recv_sem,
            device_id=peer,
            device_id_type=MESH,
        )

    def chunk_terms(c, carry):
        cells = pl.ds(
            pl.multiple_of(c // 4 * GROUP_CELLS + (me + c + 2) % 4 * LANES, LANES), LANES
        )
        rows = pl.ds(c * TERM_PITCH, PLANES)
        up = [
            [u_v[j, m, :, cells].astype(jnp.float32) for m in range(FIELDS)]
            for j in range(FIELDS)
        ]
        rhs = [f_v[m, :, cells] for m in range(FIELDS)]
        for i in range(FIELDS):
            inv = [d_v[m, i, :, cells].astype(jnp.float32) for m in range(FIELDS)]
            for j in range(FIELDS):
                total = inv[0] * up[j][0]
                for m in range(1, FIELDS):
                    total = total + inv[m] * up[j][m]
                terms[i * FIELDS + j, rows, :] = -total
            total = inv[0] * rhs[0]
            for m in range(1, FIELDS):
                total = total + inv[m] * rhs[m]
            terms[FIELDS * FIELDS + i, rows, :] = total
        return carry

    def term(n, half, k):
        return terms[n, pl.ds(half * HALF * TERM_PITCH + k, HALF, stride=TERM_PITCH), :]

    def matvec(coupling, vec, start=None):
        out = []
        for i in range(FIELDS):
            total = coupling[i * FIELDS] * vec[0]
            for j in range(1, FIELDS):
                total = total + coupling[i * FIELDS + j] * vec[j]
            out.append(total if start is None else total + start[i])
        return out

    def prefix_rows(half, k):
        return pl.ds(pl.multiple_of((k * 2 + half) * HALF, HALF), HALF)

    def section_map(half):
        state = tuple(term(n, half, PLANES - 1) for n in range(COMPS))
        for n in range(COMPS):
            prefix[n, prefix_rows(half, PLANES - 1), :] = state[n]

        def compose(step, state):
            k = PLANES - 2 - step
            coupling = [term(n, half, k) for n in range(FIELDS * FIELDS)]
            source = [term(FIELDS * FIELDS + i, half, k) for i in range(FIELDS)]
            new = [None] * COMPS
            for col in range(FIELDS):
                column = matvec(coupling, [state[j * FIELDS + col] for j in range(FIELDS)])
                for i in range(FIELDS):
                    new[i * FIELDS + col] = column[i]
            new[FIELDS * FIELDS :] = matvec(coupling, state[FIELDS * FIELDS :], source)
            for n in range(COMPS):
                prefix[n, prefix_rows(half, k), :] = new[n]
            return tuple(new)

        state = lax.fori_loop(0, PLANES - 1, compose, state)
        for n in range(COMPS):
            maps[pl.ds(half * HALF * MAP_PITCH + n, HALF, stride=MAP_PITCH), :] = state[n]

    def out_rows(c):
        return pl.ds(pl.multiple_of(c * MAP_PITCH, 8), MAP_ROWS)

    def map_rows(c):
        return pl.ds(pl.multiple_of(c * MAP_ROWS, MAP_ROWS), MAP_ROWS)

    def map_copy(c, dest, source):
        return pltpu.make_async_remote_copy(
            src_ref=maps.at[out_rows(c), :],
            dst_ref=maps_in.at[map_rows(source), :],
            send_sem=map_ssem,
            recv_sem=map_rsem,
            device_id=(dest, q),
            device_id_type=MESH,
        )

    for n in range(COMPS, MAP_ROWS):
        maps[pl.ds(n, CHUNKS, stride=MAP_PITCH), :] = jnp.zeros((CHUNKS, LANES), jnp.float32)

    for half in range(2):
        for g in range(half * GROUPS // 2, (half + 1) * GROUPS // 2):
            for copy in load_copies(g):
                copy.wait()
            lax.fori_loop(g * GROUP_CHUNKS, (g + 1) * GROUP_CHUNKS, chunk_terms, 0, unroll=2)
        section_map(half)
        if half == 0:
            pl.semaphore_wait(barrier, NS - 1 + len(near))
            tell(0)

        for pos in SENDS[half]:
            map_copy(pos, owner_of(me, pos), me).start()

    hear(0)
    tell(1)

    for copy in small:
        copy.wait()
    face_cell = cell_v[...].reshape(1, FACES)
    face_plane = face_cell // CELLS
    face_at = face_cell % CELLS
    for c in range(CHUNKS):
        at = lax.broadcasted_iota(jnp.int32, (LANES, FACES), 0)
        here = face_at - owner_of(me, c) * LANES
        hot[pl.ds(c * LANES, LANES), :] = jnp.where(at == here, 1.0, 0.0).astype(jnp.bfloat16)
    plane_hit = lax.broadcasted_iota(jnp.int32, (PLANES, FACES), 0) == face_plane
    face_id = lax.broadcasted_iota(jnp.int32, (1, FACES), 1)
    live = jnp.where(face_id < count[0], 1.0, 0.0)
    owner_hot = jnp.where(
        lax.broadcasted_iota(jnp.int32, (NP, FACES), 0) == owner_v[...], 1.0, 0.0
    )
    owner_hot16 = owner_hot.astype(jnp.bfloat16)
    earlier = jnp.where(
        lax.broadcasted_iota(jnp.int32, (FACES, FACES), 0)
        < lax.broadcasted_iota(jnp.int32, (FACES, FACES), 1),
        1.0,
        0.0,
    ).astype(jnp.bfloat16)
    before = jnp.dot(owner_hot16, earlier, preferred_element_type=jnp.float32)
    rank = jnp.sum(owner_hot * before, axis=0, keepdims=True).astype(jnp.int32)
    rank_hot = jnp.where(lax.broadcasted_iota(jnp.int32, (CAP, FACES), 0) == rank, 1.0, 0.0)
    slot_value = (slot_v[...].reshape(1, FACES) + 1).astype(jnp.float32) * live
    slot_rows = rank_hot * slot_value
    weight = ail_v[...].reshape(1, FACES).astype(jnp.float32) * live * arm_v[...].reshape(1, FACES)

    hear(1)
    tell(2)

    def by_face(left, right):
        return lax.dot_general(
            left, right, (((1,), (1,)), ((), ())), preferred_element_type=jnp.float32
        )

    at_plane = jnp.concatenate(split(jnp.where(plane_hit, weight, 0.0)), axis=0)
    for c in range(CHUNKS):
        spread = by_face(at_plane, hot[pl.ds(c * LANES, LANES), :])
        weights[pl.ds(c * TERM_PITCH, PLANES), :] = spread[:PLANES] + spread[PLANES:]
    constant = [jnp.zeros((HALF, LANES), jnp.float32) for _ in range(FIELDS)]
    for n in range(FIELDS * FIELDS, MAP_ROWS):
        gains[pl.ds(n, CHUNKS, stride=MAP_PITCH), :] = jnp.zeros((CHUNKS, LANES), jnp.float32)
    for half in range(2):

        def add_plane(k, total):
            weight_k = weights[pl.ds(half * HALF * TERM_PITCH + k, HALF, stride=TERM_PITCH), :]
            return tuple(
                total[n] + weight_k * prefix[n, prefix_rows(half, k), :] for n in range(COMPS)
            )

        zero = jnp.zeros((HALF, LANES), jnp.float32)
        total = lax.fori_loop(0, PLANES, add_plane, (zero,) * COMPS)
        for n in range(FIELDS * FIELDS):
            gains[pl.ds(half * HALF * MAP_PITCH + n, HALF, stride=MAP_PITCH), :] = total[n]
        constant = [constant[i] + total[FIELDS * FIELDS + i] for i in range(FIELDS)]
        for pos in SENDS[half]:
            dest = owner_of(me, pos)
            pltpu.make_async_remote_copy(
                src_ref=gains.at[out_rows(pos), :],
                dst_ref=gains_in.at[map_rows(me), :],
                send_sem=gain_ssem,
                recv_sem=gain_rsem,
                device_id=(dest, q),
                device_id_type=MESH,
            ).start()

    all_maps = everything(maps_in, (NS - 1) * MAP_ROWS, map_ssem, map_rsem, near[0])
    all_maps.wait_recv()
    maps_in[map_rows(me), :] = maps[out_rows(OWN), :]
    vec = [jnp.zeros((1, LANES), jnp.float32) for _ in range(FIELDS)]
    for section in range(NS - 1, 0, -1):

        def entry(n):
            return maps_in[pl.ds(section * MAP_ROWS + n, 1), :]

        matrix = [entry(n) for n in range(FIELDS * FIELDS)]
        vec = matvec(matrix, vec, [entry(FIELDS * FIELDS + i) for i in range(FIELDS)])
        for i in range(FIELDS):
            inc_out[pl.ds((section - 1) * 8 + i, 1), :] = vec[i]

    def send_inc(pos, carry):
        dest = owner_of(me, pos)
        pltpu.make_async_remote_copy(
            src_ref=inc_out.at[pl.ds(pl.multiple_of(dest * 8, 8), 8), :],
            dst_ref=inc_in.at[pl.ds(pl.multiple_of(mirror(pos) * 8, 8), 8), :],
            send_sem=inc_ssem,
            recv_sem=inc_rsem,
            device_id=(dest, q),
            device_id_type=MESH,
        ).start()
        return carry

    lax.fori_loop(0, OWN, send_inc, 0)
    lax.fori_loop(OWN + 1, NS, send_inc, 0)
    all_gains = everything(gains_in, (NS - 1) * MAP_ROWS, gain_ssem, gain_rsem, near[0])
    all_gains.wait_recv()
    gains_in[map_rows(me), :] = gains[out_rows(OWN), :]
    partial = constant
    for section in range(NS - 1):
        entering = inc_out[pl.ds(section * 8, 8), :]
        partial = [
            partial[i] + gains_in[pl.ds(section * MAP_ROWS + i * FIELDS, 8), :] * entering
            for i in range(FIELDS)
        ]
    columns = jnp.concatenate(
        [jnp.sum(partial[i], axis=0, keepdims=True) for i in range(FIELDS)]
        + [jnp.zeros((8 - FIELDS, LANES), jnp.float32)],
        axis=0,
    )
    diagonal = lax.broadcasted_iota(jnp.int32, (8, LANES), 0) == lax.broadcasted_iota(
        jnp.int32, (8, LANES), 1
    )
    hmsg[0] = jnp.sum(
        jnp.where(diagonal, jnp.sum(columns, axis=1, keepdims=True), 0.0), axis=0, keepdims=True
    )

    def hinge_copy(dest, source):
        return pltpu.make_async_remote_copy(
            src_ref=hmsg.at[0],
            dst_ref=hmsg_in.at[source],
            send_sem=hinge_ssem,
            recv_sem=hinge_rsem,
            device_id=(dest, q),
            device_id_type=MESH,
        )

    def send_hinge(pos, carry):
        hinge_copy(owner_of(me, pos), me).start()
        return carry

    lax.fori_loop(0, OWN, send_hinge, 0)
    lax.fori_loop(OWN + 1, NS, send_hinge, 0)

    all_inc = everything(inc_in, (NS - 1) * 8, inc_ssem, inc_rsem, near[0])
    all_inc.wait_recv()
    inc_in[pl.ds(OWN * 8, 8), :] = inc_out[
        pl.ds(pl.multiple_of(me * 8, 8), 8), :
    ]

    start = tuple(
        tuple(inc_in[pl.ds(half * HALF * 8 + i, HALF, stride=8), :] for i in range(FIELDS))
        for half in range(2)
    )

    def sweep(step, states):
        k = PLANES - 1 - step
        new = []
        for half in range(2):
            coupling = [term(n, half, k) for n in range(FIELDS * FIELDS)]
            source = [term(FIELDS * FIELDS + i, half, k) for i in range(FIELDS)]
            state = matvec(coupling, states[half], source)
            for i in range(FIELDS):
                adj[i, pl.ds(half * HALF * ADJ_PITCH + k, HALF, stride=ADJ_PITCH), :] = state[i]
            new.append(tuple(state))
        return tuple(new)

    lax.fori_loop(0, PLANES, sweep, start)
    gathered = jnp.zeros((2 * FIELDS * PLANES, FACES), jnp.float32)
    for c in range(0, CHUNKS, 2):
        pair = jnp.concatenate(
            [
                adj[:, pl.ds(e * ADJ_PITCH, PLANES), :].reshape(FIELDS * PLANES, LANES)
                for e in (c, c + 1)
            ],
            axis=1,
        )
        gathered = gathered + jnp.dot(
            jnp.concatenate(split(pair), axis=0),
            hot[pl.ds(c * LANES, 2 * LANES), :],
            preferred_element_type=jnp.float32,
        )

    both = gathered[: FIELDS * PLANES] + gathered[FIELDS * PLANES :]
    rows = [
        jnp.sum(
            jnp.where(plane_hit, both[i * PLANES : (i + 1) * PLANES], 0.0), axis=0, keepdims=True
        )
        for i in range(FIELDS)
    ]
    load_rows = []
    for a in range(LOADS):
        total = fmap_v[0, pl.ds(a, 1), :] * rows[0]
        for i in range(1, FIELDS):
            total = total + fmap_v[i, pl.ds(a, 1), :] * rows[i]
        load_rows.append(rank_hot * (total * live))
    face_rows = jnp.concatenate(
        load_rows
        + [slot_rows, jnp.zeros((LANES - SLOT_AT - CAP, FACES), jnp.float32)],
        axis=0,
    )

    packed = jnp.zeros((NP, LANES), jnp.float32)
    for piece in split(face_rows):
        packed = packed + by_face(owner_hot16, piece)
    msg[:, 0, :] = packed

    def face_copy(dest, source):
        return pltpu.make_async_remote_copy(
            src_ref=msg.at[dest],
            dst_ref=msg_in.at[source],
            send_sem=face_ssem,
            recv_sem=face_rsem,
            device_id=(me, dest),
            device_id_type=MESH,
        )

    hear(2)

    def far_first(t):
        return (q + NP // 2 + (t + 1) // 2 * (1 - 2 * (t % 2))) % NP

    def send_face(t, carry):
        face_copy(far_first(t), q).start()
        return carry

    lax.fori_loop(0, NP - 1, send_face, 0)
    all_hinge = everything(hmsg_in, NS - 1, hinge_ssem, hinge_rsem, near[0])
    all_hinge.wait_recv()
    hmsg_in[me] = hmsg[0]
    zmsg[0] = jnp.sum(hmsg_in[...], axis=0)

    def send_z(t, carry):
        pltpu.make_async_remote_copy(
            src_ref=zmsg.at[0],
            dst_ref=zmsg_in.at[q],
            send_sem=z_ssem,
            recv_sem=z_rsem,
            device_id=(me, far_first(t)),
            device_id_type=MESH,
        ).start()
        return carry

    lax.fori_loop(0, NP - 1, send_z, 0)
    all_faces = everything(msg_in, NP - 1, face_ssem, face_rsem, near[0])
    all_faces.wait_recv()
    msg_in[q] = msg[q]
    for peer in range(NP):
        rows_in[pl.ds(peer, 1), :] = msg_in[peer]
    arrived = rows_in[...]

    lane = lax.broadcasted_iota(jnp.int32, (NP, LANES), 1) + 1
    loads = [jnp.zeros((NP, SHELL), jnp.float32) for _ in range(LOADS)]
    for pos in range(CAP):
        at = SLOT_AT + pos
        hit = arrived[:, at : at + 1].astype(jnp.int32) == lane
        for a in range(LOADS):
            at = LOAD_AT + a * CAP + pos
            loads[a] = loads[a] + jnp.where(hit, arrived[:, at : at + 1], 0.0)
    for a in range(LOADS):
        shell_out[pl.ds(a, 1), :] = jnp.sum(loads[a], axis=0, keepdims=True)

    all_maps.wait_send()
    all_gains.wait_send()
    all_inc.wait_send()
    all_faces.wait_send()
    all_hinge.wait_send()
    all_z = everything(zmsg_in, NP - 1, z_ssem, z_rsem, near[0])
    all_z.wait_send()
    all_z.wait_recv()
    zmsg_in[q] = zmsg[0]
    total = jnp.sum(zmsg_in[:, 0, :], axis=0) * (1.0 / math.sqrt(NS * NP * FACES))
    hinge_out[...] = total[:FIELDS]


def store(adj, shell, hinge, adj_out, shell_out, hinge_out, adj_sem, shell_sem, hinge_sem):
    me = lax.axis_index("span")
    for c in range(CHUNKS):
        cells = pl.ds(pl.multiple_of(owner_of(me, c) * LANES, LANES), LANES)
        pltpu.make_async_copy(
            adj.at[:, pl.ds(c * ADJ_PITCH, PLANES), :],
            adj_out.at[:, :, cells],
            adj_sem,
        ).start()
    rest = (
        pltpu.make_async_copy(shell, shell_out, shell_sem),
        pltpu.make_async_copy(hinge, hinge_out, hinge_sem),
    )
    for copy in rest:
        copy.start()
    pltpu.make_async_copy(adj_out, adj_out, adj_sem).wait()
    for copy in rest:
        copy.wait()


def on_device(
    forcing,
    inv_diag,
    upper_jac,
    face_cell,
    face_owner,
    face_slot,
    face_count,
    aileron,
    face_map,
    hinge_arm,
):
    anywhere = pl.BlockSpec(memory_space=pltpu.HBM)
    vmem = pl.BlockSpec(memory_space=pltpu.VMEM)
    f32, bf16, i32 = jnp.float32, jnp.bfloat16, jnp.int32
    dma = pltpu.SemaphoreType.DMA
    operands = (
        forcing,
        inv_diag,
        upper_jac,
        face_cell,
        face_owner.T,
        face_slot,
        face_count,
        aileron,
        jnp.swapaxes(face_map, 0, 1),
        hinge_arm,
    )
    operands = [
        x if x is face_count else pltpu.with_memory_space_constraint(x, pltpu.HBM)
        for x in operands
    ]
    results = pl.pallas_call(
        kernel,
        out_shape=(
            pltpu.VMEM((FIELDS, CHUNKS * ADJ_PITCH, LANES), f32),
            pltpu.VMEM((LOADS, SHELL), f32),
            pltpu.VMEM((FIELDS,), f32),
        ),
        in_specs=[anywhere] * 6
        + [pl.BlockSpec(memory_space=pltpu.SMEM)]
        + [anywhere] * 3,
        out_specs=(vmem, vmem, vmem),
        scratch_shapes=[
            pltpu.VMEM((FIELDS, PLANES, CELLS), f32),
            pltpu.VMEM((FIELDS, FIELDS, PLANES, CELLS), bf16),
            pltpu.VMEM((FIELDS, FIELDS, PLANES, CELLS), bf16),
            pltpu.VMEM((FACES,), i32),
            pltpu.VMEM((1, FACES), i32),
            pltpu.VMEM((FACES,), i32),
            pltpu.VMEM((FACES,), i32),
            pltpu.VMEM((FIELDS, LOADS, FACES), f32),
            pltpu.VMEM((FACES,), f32),
            pltpu.VMEM((COMPS, CHUNKS * TERM_PITCH, LANES), f32),
            pltpu.VMEM((COMPS, 2 * PLANES * HALF, LANES), f32),
            pltpu.VMEM((CHUNKS * TERM_PITCH, LANES), f32),
            pltpu.VMEM((CHUNKS * MAP_PITCH, LANES), f32),
            pltpu.VMEM((NS * MAP_ROWS, LANES), f32),
            pltpu.VMEM((CHUNKS * MAP_PITCH, LANES), f32),
            pltpu.VMEM((NS * MAP_ROWS, LANES), f32),
            pltpu.VMEM((NS * 8, LANES), f32),
            pltpu.VMEM((CHUNKS * 8, LANES), f32),
            pltpu.VMEM((CELLS, FACES), bf16),
            pltpu.VMEM((NP, 1, LANES), f32),
            pltpu.VMEM((NP, 1, LANES), f32),
            pltpu.VMEM((NP, LANES), f32),
            pltpu.VMEM((1, 1, LANES), f32),
            pltpu.VMEM((NP, 1, LANES), f32),
            pltpu.VMEM((1, 1, LANES), f32),
            pltpu.VMEM((NS, 1, LANES), f32),
            pltpu.SemaphoreType.REGULAR((3,)),
            dma((GROUPS, 3)),
            dma((6,)),
        ]
        + [dma] * 12,
        compiler_params=pltpu.CompilerParams(
            collective_id=0, has_side_effects=True, vmem_limit_bytes=40 * 1024 * 1024
        ),
        cost_estimate=pl.CostEstimate(
            flops=22_000_000, bytes_accessed=4_700_000, transcendentals=0
        ),
        name="sweep",
    )(*operands)
    return pl.pallas_call(
        store,
        out_shape=(
            jax.ShapeDtypeStruct((FIELDS, PLANES, CELLS), f32),
            jax.ShapeDtypeStruct((LOADS, SHELL), f32),
            jax.ShapeDtypeStruct((FIELDS,), f32),
        ),
        in_specs=[vmem] * 3,
        out_specs=[anywhere] * 3,
        scratch_shapes=[dma] * 3,
        compiler_params=pltpu.CompilerParams(vmem_limit_bytes=16 * 1024 * 1024),
        name="store",
    )(*results)


def solution(mesh):
    in_specs = (
        P(None, "span", "plane"),
        P(None, None, "span", "plane"),
        P(None, None, "span", "plane"),
        P(("span", "plane")),
        P(("span", "plane"), None),
        P(("span", "plane")),
        P(("span", "plane")),
        P(("span", "plane")),
        P(None, None, ("span", "plane")),
        P(("span", "plane")),
    )
    out_specs = (P(None, "span", "plane"), P(None, ("span", "plane")), P())
    return jax.shard_map(
        on_device, mesh=mesh, in_specs=in_specs, out_specs=out_specs, check_vma=False
    )
```

```python
import math

import jax
import jax.numpy as jnp
from jax import lax
from jax.experimental import pallas as pl
from jax.experimental.pallas import tpu as pltpu
from jax.sharding import PartitionSpec as P

MESH = pl.DeviceIdType.MESH

FIELDS = 5
LOADS = 3
NS = 16
NP = 32
PLANES = 16
CELLS = 2048
LANES = 128
CHUNKS = CELLS // LANES
HALF = CHUNKS // 2
OWN = 10
SENDS = ((0, 1, 2, 3, 4, 5, 6, 7), (12, 13, 14, 15, 8, 9, 11))
FACES = 256
SHELL = 128
CAP = 16
COMPS = FIELDS * (FIELDS + 1)
MAP_ROWS = 32
MAP_PITCH = 40
TERM_PITCH = 17
ADJ_PITCH = 24
GROUPS = 4
GROUP_CELLS = CELLS // GROUPS
GROUP_CHUNKS = CHUNKS // GROUPS
LOAD_AT = 0
SLOT_AT = 48


def owner_of(dev, pos):
    return 4 * ((dev // 4 + pos // 4 + 2) % 4) + (dev + pos + 2) % 4


def mirror(pos):
    return 4 * ((4 - pos // 4) % 4) + (4 - pos % 4) % 4


def split(value):
    high = value.astype(jnp.bfloat16)
    low = (value - high.astype(jnp.float32)).astype(jnp.bfloat16)
    return high, low


def kernel(
    forcing,
    inv_diag,
    upper,
    cell,
    owner,
    slot,
    count,
    aileron,
    fmap,
    arm,
    adj,
    shell_out,
    hinge_out,
    f_v,
    d_v,
    u_v,
    cell_v,
    owner_v,
    slot_v,
    ail_v,
    fmap_v,
    arm_v,
    terms,
    prefix,
    weights,
    gains,
    gains_in,
    maps,
    maps_in,
    inc_out,
    inc_in,
    hot,
    msg,
    msg_in,
    rows_in,
    zmsg,
    zmsg_in,
    hmsg,
    hmsg_in,
    ready,
    load_sem,
    small_sem,
    map_ssem,
    map_rsem,
    gain_ssem,
    gain_rsem,
    inc_ssem,
    inc_rsem,
    face_ssem,
    face_rsem,
    z_ssem,
    z_rsem,
    hinge_ssem,
    hinge_rsem,
):
    me = lax.axis_index("span")
    q = lax.axis_index("plane")
    barrier = pltpu.get_barrier_semaphore()

    def load_copies(g):
        block = (me // 4 + g + 2) % 4
        cells = pl.ds(pl.multiple_of(block * GROUP_CELLS, GROUP_CELLS), GROUP_CELLS)
        here = pl.ds(g * GROUP_CELLS, GROUP_CELLS)
        return (
            pltpu.make_async_copy(
                inv_diag.at[:, :, :, cells], d_v.at[:, :, :, here], load_sem.at[g, 0]
            ),
            pltpu.make_async_copy(
                upper.at[:, :, :, cells], u_v.at[:, :, :, here], load_sem.at[g, 1]
            ),
            pltpu.make_async_copy(
                forcing.at[:, :, cells], f_v.at[:, :, here], load_sem.at[g, 2]
            ),
        )

    for g in range(GROUPS):
        for copy in load_copies(g):
            copy.start()
    small = [
        pltpu.make_async_copy(src, dst, small_sem.at[n])
        for n, (src, dst) in enumerate(
            (
                (cell, cell_v),
                (owner, owner_v),
                (slot, slot_v),
                (aileron, ail_v),
                (fmap, fmap_v),
                (arm, arm_v),
            )
        )
    ]
    for copy in small:
        copy.start()

    def greet_span(pos, carry):
        pl.semaphore_signal(
            barrier, inc=1, device_id=(owner_of(me, pos), q), device_id_type=MESH
        )
        return carry

    depth, core = q // 2, q % 2

    def along(distance, other=0):
        return (me, ((depth + distance) % (NP // 2)) * 2 + (core + other) % 2)

    near = [along(0, 1)] + [along(d, other) for d in (1, -1) for other in (0, 1)]
    lax.fori_loop(0, OWN, greet_span, 0)
    lax.fori_loop(OWN + 1, NS, greet_span, 0)
    for peer in near:
        pl.semaphore_signal(barrier, inc=1, device_id=peer, device_id_type=MESH)

    def tell(step):
        for d in (1 << step, -(1 << step)):
            pl.semaphore_signal(
                ready.at[step], inc=1, device_id=along(d), device_id_type=MESH
            )

    def hear(step):
        pl.semaphore_wait(ready.at[step], 2)

    inc_out[...] = jnp.zeros_like(inc_out)

    def everything(ref, count, send_sem, recv_sem, peer):
        whole = ref.at[pl.ds(0, count)]
        return pltpu.make_async_remote_copy(
            src_ref=whole,
            dst_ref=whole,
            send_sem=send_sem,
            recv_sem=recv_sem,
            device_id=peer,
            device_id_type=MESH,
        )

    def chunk_terms(c, carry):
        cells = pl.ds(
            pl.multiple_of(c // 4 * GROUP_CELLS + (me + c + 2) % 4 * LANES, LANES), LANES
        )
        rows = pl.ds(c * TERM_PITCH, PLANES)
        up = [
            [u_v[j, m, :, cells].astype(jnp.float32) for m in range(FIELDS)]
            for j in range(FIELDS)
        ]
        rhs = [f_v[m, :, cells] for m in range(FIELDS)]
        for i in range(FIELDS):
            inv = [d_v[m, i, :, cells].astype(jnp.float32) for m in range(FIELDS)]
            for j in range(FIELDS):
                total = inv[0] * up[j][0]
                for m in range(1, FIELDS):
                    total = total + inv[m] * up[j][m]
                terms[i * FIELDS + j, rows, :] = -total
            total = inv[0] * rhs[0]
            for m in range(1, FIELDS):
                total = total + inv[m] * rhs[m]
            terms[FIELDS * FIELDS + i, rows, :] = total
        return carry

    def term(n, half, k):
        return terms[n, pl.ds(half * HALF * TERM_PITCH + k, HALF, stride=TERM_PITCH), :]

    def matvec(coupling, vec, start=None):
        out = []
        for i in range(FIELDS):
            total = coupling[i * FIELDS] * vec[0]
            for j in range(1, FIELDS):
                total = total + coupling[i * FIELDS + j] * vec[j]
            out.append(total if start is None else total + start[i])
        return out

    def prefix_rows(half, k):
        return pl.ds(pl.multiple_of((k * 2 + half) * HALF, HALF), HALF)

    def section_map(half):
        state = tuple(term(n, half, PLANES - 1) for n in range(COMPS))
        for n in range(COMPS):
            prefix[n, prefix_rows(half, PLANES - 1), :] = state[n]

        def compose(step, state):
            k = PLANES - 2 - step
            coupling = [term(n, half, k) for n in range(FIELDS * FIELDS)]
            source = [term(FIELDS * FIELDS + i, half, k) for i in range(FIELDS)]
            new = [None] * COMPS
            for col in range(FIELDS):
                column = matvec(coupling, [state[j * FIELDS + col] for j in range(FIELDS)])
                for i in range(FIELDS):
                    new[i * FIELDS + col] = column[i]
            new[FIELDS * FIELDS :] = matvec(coupling, state[FIELDS * FIELDS :], source)
            for n in range(COMPS):
                prefix[n, prefix_rows(half, k), :] = new[n]
            return tuple(new)

        state = lax.fori_loop(0, PLANES - 1, compose, state)
        for n in range(COMPS):
            maps[pl.ds(half * HALF * MAP_PITCH + n, HALF, stride=MAP_PITCH), :] = state[n]

    def out_rows(c):
        return pl.ds(pl.multiple_of(c * MAP_PITCH, 8), MAP_ROWS)

    def map_rows(c):
        return pl.ds(pl.multiple_of(c * MAP_ROWS, MAP_ROWS), MAP_ROWS)

    def map_copy(c, dest, source):
        return pltpu.make_async_remote_copy(
            src_ref=maps.at[out_rows(c), :],
            dst_ref=maps_in.at[map_rows(source), :],
            send_sem=map_ssem,
            recv_sem=map_rsem,
            device_id=(dest, q),
            device_id_type=MESH,
        )

    for n in range(COMPS, MAP_ROWS):
        maps[pl.ds(n, CHUNKS, stride=MAP_PITCH), :] = jnp.zeros((CHUNKS, LANES), jnp.float32)

    for half in range(2):
        for g in range(half * GROUPS // 2, (half + 1) * GROUPS // 2):
            for copy in load_copies(g):
                copy.wait()
            lax.fori_loop(g * GROUP_CHUNKS, (g + 1) * GROUP_CHUNKS, chunk_terms, 0, unroll=2)
        section_map(half)
        if half == 0:
            pl.semaphore_wait(barrier, NS - 1 + len(near))
            tell(0)

        for pos in SENDS[half]:
            map_copy(pos, owner_of(me, pos), me).start()

    hear(0)
    tell(1)

    for copy in small:
        copy.wait()
    face_cell = cell_v[...].reshape(1, FACES)
    face_plane = face_cell // CELLS
    face_at = face_cell % CELLS
    for c in range(CHUNKS):
        at = lax.broadcasted_iota(jnp.int32, (LANES, FACES), 0)
        here = face_at - owner_of(me, c) * LANES
        hot[pl.ds(c * LANES, LANES), :] = jnp.where(at == here, 1.0, 0.0).astype(jnp.bfloat16)
    plane_hit = lax.broadcasted_iota(jnp.int32, (PLANES, FACES), 0) == face_plane
    face_id = lax.broadcasted_iota(jnp.int32, (1, FACES), 1)
    live = jnp.where(face_id < count[0], 1.0, 0.0)
    owner_hot = jnp.where(
        lax.broadcasted_iota(jnp.int32, (NP, FACES), 0) == owner_v[...], 1.0, 0.0
    )
    owner_hot16 = owner_hot.astype(jnp.bfloat16)
    earlier = jnp.where(
        lax.broadcasted_iota(jnp.int32, (FACES, FACES), 0)
        < lax.broadcasted_iota(jnp.int32, (FACES, FACES), 1),
        1.0,
        0.0,
    ).astype(jnp.bfloat16)
    before = jnp.dot(owner_hot16, earlier, preferred_element_type=jnp.float32)
    rank = jnp.sum(owner_hot * before, axis=0, keepdims=True).astype(jnp.int32)
    rank_hot = jnp.where(lax.broadcasted_iota(jnp.int32, (CAP, FACES), 0) == rank, 1.0, 0.0)
    slot_value = (slot_v[...].reshape(1, FACES) + 1).astype(jnp.float32) * live
    slot_rows = rank_hot * slot_value
    weight = ail_v[...].reshape(1, FACES).astype(jnp.float32) * live * arm_v[...].reshape(1, FACES)

    hear(1)
    tell(2)

    def by_face(left, right):
        return lax.dot_general(
            left, right, (((1,), (1,)), ((), ())), preferred_element_type=jnp.float32
        )

    at_plane = jnp.concatenate(split(jnp.where(plane_hit, weight, 0.0)), axis=0)
    for c in range(CHUNKS):
        spread = by_face(at_plane, hot[pl.ds(c * LANES, LANES), :])
        weights[pl.ds(c * TERM_PITCH, PLANES), :] = spread[:PLANES] + spread[PLANES:]
    constant = [jnp.zeros((HALF, LANES), jnp.float32) for _ in range(FIELDS)]
    for n in range(FIELDS * FIELDS, MAP_ROWS):
        gains[pl.ds(n, CHUNKS, stride=MAP_PITCH), :] = jnp.zeros((CHUNKS, LANES), jnp.float32)
    for half in range(2):

        def add_plane(k, total):
            weight_k = weights[pl.ds(half * HALF * TERM_PITCH + k, HALF, stride=TERM_PITCH), :]
            return tuple(
                total[n] + weight_k * prefix[n, prefix_rows(half, k), :] for n in range(COMPS)
            )

        zero = jnp.zeros((HALF, LANES), jnp.float32)
        total = lax.fori_loop(0, PLANES, add_plane, (zero,) * COMPS, unroll=4)
        for n in range(FIELDS * FIELDS):
            gains[pl.ds(half * HALF * MAP_PITCH + n, HALF, stride=MAP_PITCH), :] = total[n]
        constant = [constant[i] + total[FIELDS * FIELDS + i] for i in range(FIELDS)]

        @pl.when(me != NS - 1)
        def _():
            for pos in SENDS[half]:
                dest = owner_of(me, pos)
                pltpu.make_async_remote_copy(
                    src_ref=gains.at[out_rows(pos), :],
                    dst_ref=gains_in.at[map_rows(me), :],
                    send_sem=gain_ssem,
                    recv_sem=gain_rsem,
                    device_id=(dest, q),
                    device_id_type=MESH,
                ).start()

    all_maps = everything(maps_in, (NS - 1) * MAP_ROWS, map_ssem, map_rsem, near[0])
    all_maps.wait_recv()
    maps_in[map_rows(me), :] = maps[out_rows(OWN), :]
    vec = [jnp.zeros((1, LANES), jnp.float32) for _ in range(FIELDS)]
    for section in range(NS - 1, 0, -1):

        def entry(n):
            return maps_in[pl.ds(section * MAP_ROWS + n, 1), :]

        matrix = [entry(n) for n in range(FIELDS * FIELDS)]
        vec = matvec(matrix, vec, [entry(FIELDS * FIELDS + i) for i in range(FIELDS)])
        for i in range(FIELDS):
            inc_out[pl.ds((section - 1) * 8 + i, 1), :] = vec[i]

    def send_inc(pos, carry):
        dest = owner_of(me, pos)
        pltpu.make_async_remote_copy(
            src_ref=inc_out.at[pl.ds(pl.multiple_of(dest * 8, 8), 8), :],
            dst_ref=inc_in.at[pl.ds(pl.multiple_of(mirror(pos) * 8, 8), 8), :],
            send_sem=inc_ssem,
            recv_sem=inc_rsem,
            device_id=(dest, q),
            device_id_type=MESH,
        ).start()
        return carry

    lax.fori_loop(0, OWN, send_inc, 0)
    lax.fori_loop(OWN + 1, NS, send_inc, 0)
    all_gains = everything(gains_in, (NS - 1) * MAP_ROWS, gain_ssem, gain_rsem, near[0])

    @pl.when(me == NS - 1)
    def _():
        all_gains.wait_recv()

    @pl.when(me != NS - 1)
    def _():
        everything(gains_in, (NS - 2) * MAP_ROWS, gain_ssem, gain_rsem, near[0]).wait_recv()

    gains_in[map_rows(me), :] = gains[out_rows(OWN), :]
    partial = constant
    for section in range(NS - 1):
        entering = inc_out[pl.ds(section * 8, 8), :]
        partial = [
            partial[i] + gains_in[pl.ds(section * MAP_ROWS + i * FIELDS, 8), :] * entering
            for i in range(FIELDS)
        ]
    columns = jnp.concatenate(
        [jnp.sum(partial[i], axis=0, keepdims=True) for i in range(FIELDS)]
        + [jnp.zeros((8 - FIELDS, LANES), jnp.float32)],
        axis=0,
    )
    diagonal = lax.broadcasted_iota(jnp.int32, (8, LANES), 0) == lax.broadcasted_iota(
        jnp.int32, (8, LANES), 1
    )
    hmsg[0] = jnp.sum(
        jnp.where(diagonal, jnp.sum(columns, axis=1, keepdims=True), 0.0), axis=0, keepdims=True
    )

    def hinge_copy(dest, source):
        return pltpu.make_async_remote_copy(
            src_ref=hmsg.at[0],
            dst_ref=hmsg_in.at[source],
            send_sem=hinge_ssem,
            recv_sem=hinge_rsem,
            device_id=(dest, q),
            device_id_type=MESH,
        )

    def send_hinge(pos, carry):
        hinge_copy(owner_of(me, pos), me).start()
        return carry

    lax.fori_loop(0, OWN, send_hinge, 0)
    lax.fori_loop(OWN + 1, NS, send_hinge, 0)

    all_inc = everything(inc_in, (NS - 1) * 8, inc_ssem, inc_rsem, near[0])
    all_inc.wait_recv()
    inc_in[pl.ds(OWN * 8, 8), :] = inc_out[
        pl.ds(pl.multiple_of(me * 8, 8), 8), :
    ]

    start = tuple(
        tuple(inc_in[pl.ds(half * HALF * 8 + i, HALF, stride=8), :] for i in range(FIELDS))
        for half in range(2)
    )

    def sweep(step, states):
        k = PLANES - 1 - step
        new = []
        for half in range(2):
            coupling = [term(n, half, k) for n in range(FIELDS * FIELDS)]
            source = [term(FIELDS * FIELDS + i, half, k) for i in range(FIELDS)]
            state = matvec(coupling, states[half], source)
            for i in range(FIELDS):
                adj[i, pl.ds(half * HALF * ADJ_PITCH + k, HALF, stride=ADJ_PITCH), :] = state[i]
            new.append(tuple(state))
        return tuple(new)

    lax.fori_loop(0, PLANES, sweep, start)
    gathered = jnp.zeros((2 * FIELDS * PLANES, FACES), jnp.float32)
    for c in range(0, CHUNKS, 2):
        pair = jnp.concatenate(
            [
                adj[:, pl.ds(e * ADJ_PITCH, PLANES), :].reshape(FIELDS * PLANES, LANES)
                for e in (c, c + 1)
            ],
            axis=1,
        )
        gathered = gathered + jnp.dot(
            jnp.concatenate(split(pair), axis=0),
            hot[pl.ds(c * LANES, 2 * LANES), :],
            preferred_element_type=jnp.float32,
        )

    both = gathered[: FIELDS * PLANES] + gathered[FIELDS * PLANES :]
    rows = [
        jnp.sum(
            jnp.where(plane_hit, both[i * PLANES : (i + 1) * PLANES], 0.0), axis=0, keepdims=True
        )
        for i in range(FIELDS)
    ]
    load_rows = []
    for a in range(LOADS):
        total = fmap_v[0, pl.ds(a, 1), :] * rows[0]
        for i in range(1, FIELDS):
            total = total + fmap_v[i, pl.ds(a, 1), :] * rows[i]
        load_rows.append(rank_hot * (total * live))
    face_rows = jnp.concatenate(
        load_rows
        + [slot_rows, jnp.zeros((LANES - SLOT_AT - CAP, FACES), jnp.float32)],
        axis=0,
    )

    packed = jnp.zeros((NP, LANES), jnp.float32)
    for piece in split(face_rows):
        packed = packed + by_face(owner_hot16, piece)
    msg[:, 0, :] = packed

    def face_copy(dest, source):
        return pltpu.make_async_remote_copy(
            src_ref=msg.at[dest],
            dst_ref=msg_in.at[source],
            send_sem=face_ssem,
            recv_sem=face_rsem,
            device_id=(me, dest),
            device_id_type=MESH,
        )

    hear(2)

    def far_first(t):
        return (q + NP // 2 + (t + 1) // 2 * (1 - 2 * (t % 2))) % NP

    def send_face(t, carry):
        face_copy(far_first(t), q).start()
        return carry

    lax.fori_loop(0, NP - 1, send_face, 0)
    all_hinge = everything(hmsg_in, NS - 1, hinge_ssem, hinge_rsem, near[0])
    all_hinge.wait_recv()
    hmsg_in[me] = hmsg[0]
    zmsg[0] = jnp.sum(hmsg_in[...], axis=0)

    def send_z(t, carry):
        pltpu.make_async_remote_copy(
            src_ref=zmsg.at[0],
            dst_ref=zmsg_in.at[q],
            send_sem=z_ssem,
            recv_sem=z_rsem,
            device_id=(me, far_first(t)),
            device_id_type=MESH,
        ).start()
        return carry

    lax.fori_loop(0, NP - 1, send_z, 0)
    all_faces = everything(msg_in, NP - 1, face_ssem, face_rsem, near[0])
    all_faces.wait_recv()
    msg_in[q] = msg[q]
    for peer in range(NP):
        rows_in[pl.ds(peer, 1), :] = msg_in[peer]
    arrived = rows_in[...]

    lane = lax.broadcasted_iota(jnp.int32, (NP, LANES), 1) + 1
    loads = [jnp.zeros((NP, SHELL), jnp.float32) for _ in range(LOADS)]
    for pos in range(CAP):
        at = SLOT_AT + pos
        hit = arrived[:, at : at + 1].astype(jnp.int32) == lane
        for a in range(LOADS):
            at = LOAD_AT + a * CAP + pos
            loads[a] = loads[a] + jnp.where(hit, arrived[:, at : at + 1], 0.0)
    for a in range(LOADS):
        shell_out[pl.ds(a, 1), :] = jnp.sum(loads[a], axis=0, keepdims=True)

    all_maps.wait_send()

    @pl.when(me != NS - 1)
    def _():
        all_gains.wait_send()

    all_inc.wait_send()
    all_faces.wait_send()
    all_hinge.wait_send()
    all_z = everything(zmsg_in, NP - 1, z_ssem, z_rsem, near[0])
    all_z.wait_send()
    all_z.wait_recv()
    zmsg_in[q] = zmsg[0]
    total = jnp.sum(zmsg_in[:, 0, :], axis=0) * (1.0 / math.sqrt(NS * NP * FACES))
    hinge_out[...] = total[:FIELDS]


def store(adj, shell, hinge, adj_out, shell_out, hinge_out, adj_sem, shell_sem, hinge_sem):
    me = lax.axis_index("span")
    for c in range(CHUNKS):
        cells = pl.ds(pl.multiple_of(owner_of(me, c) * LANES, LANES), LANES)
        pltpu.make_async_copy(
            adj.at[:, pl.ds(c * ADJ_PITCH, PLANES), :],
            adj_out.at[:, :, cells],
            adj_sem,
        ).start()
    rest = (
        pltpu.make_async_copy(shell, shell_out, shell_sem),
        pltpu.make_async_copy(hinge, hinge_out, hinge_sem),
    )
    for copy in rest:
        copy.start()
    pltpu.make_async_copy(adj_out, adj_out, adj_sem).wait()
    for copy in rest:
        copy.wait()


def on_device(
    forcing,
    inv_diag,
    upper_jac,
    face_cell,
    face_owner,
    face_slot,
    face_count,
    aileron,
    face_map,
    hinge_arm,
):
    anywhere = pl.BlockSpec(memory_space=pltpu.HBM)
    vmem = pl.BlockSpec(memory_space=pltpu.VMEM)
    f32, bf16, i32 = jnp.float32, jnp.bfloat16, jnp.int32
    dma = pltpu.SemaphoreType.DMA
    operands = (
        forcing,
        inv_diag,
        upper_jac,
        face_cell,
        face_owner.T,
        face_slot,
        face_count,
        aileron,
        jnp.swapaxes(face_map, 0, 1),
        hinge_arm,
    )
    operands = [
        x if x is face_count else pltpu.with_memory_space_constraint(x, pltpu.HBM)
        for x in operands
    ]
    results = pl.pallas_call(
        kernel,
        out_shape=(
            pltpu.VMEM((FIELDS, CHUNKS * ADJ_PITCH, LANES), f32),
            pltpu.VMEM((LOADS, SHELL), f32),
            pltpu.VMEM((FIELDS,), f32),
        ),
        in_specs=[anywhere] * 6
        + [pl.BlockSpec(memory_space=pltpu.SMEM)]
        + [anywhere] * 3,
        out_specs=(vmem, vmem, vmem),
        scratch_shapes=[
            pltpu.VMEM((FIELDS, PLANES, CELLS), f32),
            pltpu.VMEM((FIELDS, FIELDS, PLANES, CELLS), bf16),
            pltpu.VMEM((FIELDS, FIELDS, PLANES, CELLS), bf16),
            pltpu.VMEM((FACES,), i32),
            pltpu.VMEM((1, FACES), i32),
            pltpu.VMEM((FACES,), i32),
            pltpu.VMEM((FACES,), i32),
            pltpu.VMEM((FIELDS, LOADS, FACES), f32),
            pltpu.VMEM((FACES,), f32),
            pltpu.VMEM((COMPS, CHUNKS * TERM_PITCH, LANES), f32),
            pltpu.VMEM((COMPS, 2 * PLANES * HALF, LANES), f32),
            pltpu.VMEM((CHUNKS * TERM_PITCH, LANES), f32),
            pltpu.VMEM((CHUNKS * MAP_PITCH, LANES), f32),
            pltpu.VMEM((NS * MAP_ROWS, LANES), f32),
            pltpu.VMEM((CHUNKS * MAP_PITCH, LANES), f32),
            pltpu.VMEM((NS * MAP_ROWS, LANES), f32),
            pltpu.VMEM((NS * 8, LANES), f32),
            pltpu.VMEM((CHUNKS * 8, LANES), f32),
            pltpu.VMEM((CELLS, FACES), bf16),
            pltpu.VMEM((NP, 1, LANES), f32),
            pltpu.VMEM((NP, 1, LANES), f32),
            pltpu.VMEM((NP, LANES), f32),
            pltpu.VMEM((1, 1, LANES), f32),
            pltpu.VMEM((NP, 1, LANES), f32),
            pltpu.VMEM((1, 1, LANES), f32),
            pltpu.VMEM((NS, 1, LANES), f32),
            pltpu.SemaphoreType.REGULAR((3,)),
            dma((GROUPS, 3)),
            dma((6,)),
        ]
        + [dma] * 12,
        compiler_params=pltpu.CompilerParams(
            collective_id=0, has_side_effects=True, vmem_limit_bytes=40 * 1024 * 1024
        ),
        cost_estimate=pl.CostEstimate(
            flops=22_000_000, bytes_accessed=4_700_000, transcendentals=0
        ),
        name="sweep",
    )(*operands)
    return pl.pallas_call(
        store,
        out_shape=(
            jax.ShapeDtypeStruct((FIELDS, PLANES, CELLS), f32),
            jax.ShapeDtypeStruct((LOADS, SHELL), f32),
            jax.ShapeDtypeStruct((FIELDS,), f32),
        ),
        in_specs=[vmem] * 3,
        out_specs=[anywhere] * 3,
        scratch_shapes=[dma] * 3,
        compiler_params=pltpu.CompilerParams(vmem_limit_bytes=16 * 1024 * 1024),
        name="store",
    )(*results)


def solution(mesh):
    in_specs = (
        P(None, "span", "plane"),
        P(None, None, "span", "plane"),
        P(None, None, "span", "plane"),
        P(("span", "plane")),
        P(("span", "plane"), None),
        P(("span", "plane")),
        P(("span", "plane")),
        P(("span", "plane")),
        P(None, None, ("span", "plane")),
        P(("span", "plane")),
    )
    out_specs = (P(None, "span", "plane"), P(None, ("span", "plane")), P())
    return jax.shard_map(
        on_device, mesh=mesh, in_specs=in_specs, out_specs=out_specs, check_vma=False
    )
```
